32 devices in a mesh: dp: 8 (over y, x, core), tensor: 4 (over z).
Axes of the slice: x: 2, y: 2, z: 4, core: 2. Of those that a mesh axis runs over, the one named last changes fastest.
Arguments:
- tokens: bfloat16 [2, 8, 2048, 768], P(None, 'dp', 'tensor'), may hold values from -6 to 6
- segments: int32 [2, 8, 2048], P(None, 'dp'), may hold values from 0 to 127, never falling along the last dimension, each value on 1 to 1024 neighbouring positions
- w_query: bfloat16 [768, 768], P(('dp', 'tensor')), may hold values from -0.21875 to 0.21875
- w_key: bfloat16 [768, 768], P(('dp', 'tensor')), may hold values from -0.21875 to 0.21875
- w_value: bfloat16 [768, 768], P(('dp', 'tensor')), may hold values from -0.21875 to 0.21875
- w_out: bfloat16 [768, 768], P(('dp', 'tensor')), may hold values from -0.875 to 0.875
- norm_attn: bfloat16 [768], P(('dp', 'tensor')), may hold values from 0.5 to 1.5
- norm_ffn: bfloat16 [768], P(('dp', 'tensor')), may hold values from 0.5 to 1.5
- pre_mix: bfloat16 [12, 12], replicated, may hold values from -1.75 to 1.75
- post_mix: bfloat16 [12, 12], replicated, may hold values from -1.75 to 1.75
- w_up: bfloat16 [768, 3072], P('dp', 'tensor'), may hold values from -0.21875 to 0.21875
- w_down: bfloat16 [768, 3072], P('dp', 'tensor'), may hold values from -0.15625 to 0.15625
- out_grad: bfloat16 [2, 8, 2048, 768], P(None, 'dp', 'tensor'), may hold values from -6 to 6
Outputs:
- out: bfloat16 [2, 8, 2048, 768], P(None, 'dp', 'tensor')
- d_tokens: float32 [2, 8, 2048, 768], P(None, 'dp', 'tensor')
- d_w_query: float32 [768, 768], P(('dp', 'tensor'))
- d_w_key: float32 [768, 768], P(('dp', 'tensor'))
- d_w_value: float32 [768, 768], P(('dp', 'tensor'))
- d_w_out: float32 [768, 768], P(('dp', 'tensor'))
- d_norm_attn: float32 [768], P(('dp', 'tensor'))
- d_norm_ffn: float32 [768], P(('dp', 'tensor'))
- d_pre_mix: float32 [12, 12], replicated
- d_post_mix: float32 [12, 12], replicated
- d_w_up: float32 [768, 3072], P('dp', 'tensor')
- d_w_down: float32 [768, 3072], P('dp', 'tensor')
The draws below stay inside these ranges and needn't reach their ends.
Inputs may be any that keep to these rules, and one draw needn't show every extreme that they name: `segments`: within each sequence the numbers never fall; a run of equal numbers is one document, and some document is 1024 tokens long.
All inputs are finite; a program needn't handle non-finite values.
Results may differ from the reference program's by a relative error of at most 0.018.
Values may be sent and summed in bfloat16 or wider, within the bound.
A program may use at most 512 MiB of HBM per device.

```python
import math
import jax
import jax.numpy as jnp
import numpy as np
from jax import lax

D = 768
HEADS = 12
FF = 3072
SEQ = 2048
MICRO = 2
SEQS = 8
SEGS = 128


def level_of(rng, dims, pieces, least, top_value):
    factor_of, own = 1.0, jax.random.fold_in(rng, 6)
    for dim, parts in pieces:
        heights = jnp.exp(jax.random.uniform(jax.random.fold_in(own, dim), (parts,), jnp.float32, least / len(pieces), top_value / len(pieces)))
        factor_of = factor_of * jnp.repeat(heights, dims[dim] // parts).reshape([-1 if axis == dim else 1 for axis in range(len(dims))])
    return factor_of


def split_up(number_of, total, most, skew):
    portions = [(1 << 20) // math.isqrt(grade ** skew) + 1 for grade in range(2, number_of + 1)]
    rest, holding = total - most - (number_of - 1), [1] * (number_of - 1)
    while rest > 0:
        candidates = [i for i in range(number_of - 1) if holding[i] < most]
        pool, left = sum([portions[i] for i in candidates]), rest
        for i in candidates:
            more = min(most - holding[i], max(1, left * portions[i] // pool), rest)
            holding[i] = holding[i] + more
            rest = rest - more
    return np.array([most] + holding)


def uneven_parts(key, number_of, total, bound, skew):
    if number_of == 2:
        one = jax.random.randint(key, (), max(1, total - bound), min(bound, total - 1) + 1)
        return jnp.stack([one, total - one])
    tallies = jnp.asarray(split_up(number_of, total, bound, skew), jnp.int32)
    pairs = (number_of - 1) // 2
    donor, sink = tallies[1:1 + 2 * pairs:2], tallies[2:2 + 2 * pairs:2]
    room = jnp.minimum(donor - 1, bound - sink)
    shifted = jax.random.randint(jax.random.fold_in(key, 1), (pairs,), 0, 1 << 20) % (room + 1)
    tallies = tallies.at[1:1 + 2 * pairs:2].set(donor - shifted).at[2:2 + 2 * pairs:2].set(sink + shifted)
    return tallies[jax.random.permutation(jax.random.fold_in(key, 2), number_of)]


def centred(rng, dims, width, limit, pieces=(), kind=jnp.bfloat16):
    values = jax.random.normal(rng, dims, jnp.float32) * width
    if len(pieces) > 0:
        values = level_of(rng, dims, pieces, -0.22, 0.18) * values
    return jnp.clip(values, min=-limit, max=limit).astype(kind)


def setup_inputs(seed: int = 0) -> dict:
    streams_of = jax.random.split(jax.random.key(seed), 14)
    return {
        "tokens": centred(streams_of[0], (MICRO, SEQS, SEQ, D), 1.0, 6.0, ((1, 8), (2, 4))),
        "segments": jax.vmap(lambda own: jnp.searchsorted(jnp.cumsum(uneven_parts(own, SEGS, SEQ, SEQ // 2, 2)), jnp.arange(SEQ), side="right"))(jax.random.split(streams_of[1], MICRO * SEQS)).reshape((MICRO, SEQS, SEQ)).astype(jnp.int32),
        "w_query": centred(streams_of[2], (D, D), D ** -0.5, 0.21875, ((0, 32),)),
        "w_key": centred(streams_of[3], (D, D), D ** -0.5, 0.21875, ((0, 32),)),
        "w_value": centred(streams_of[4], (D, D), D ** -0.5, 0.21875, ((0, 32),)),
        "w_out": centred(streams_of[5], (D, D), (D // 16) ** -0.5, 0.875, ((0, 32),)),
        "norm_attn": jnp.clip(1.0 + 0.1 * jax.random.normal(streams_of[6], (D,), jnp.float32), 0.5, 1.5).astype(jnp.bfloat16),
        "norm_ffn": jnp.clip(1.0 + 0.1 * jax.random.normal(streams_of[7], (D,), jnp.float32), 0.5, 1.5).astype(jnp.bfloat16),
        "pre_mix": centred(streams_of[8], (HEADS, HEADS), HEADS ** -0.5, 1.75),
        "post_mix": centred(streams_of[9], (HEADS, HEADS), HEADS ** -0.5, 1.75),
        "w_up": centred(streams_of[10], (D, FF), D ** -0.5, 0.21875, ((0, 8), (1, 4))),
        "w_down": centred(streams_of[11], (D, FF), (FF // 2) ** -0.5, 0.15625, ((0, 8), (1, 4))),
        "out_grad": centred(streams_of[12], (MICRO, SEQS, SEQ, D), 1.0, 6.0, ((1, 8), (2, 4))),
    }


@jax.custom_vjp
def low(v):
    return lax.optimization_barrier(v.astype(jnp.bfloat16)).astype(jnp.float32)

@jax.custom_vjp
def low_back(v):
    return v

def low_keep(v):
    return (low(v), None)

def low_pass(kept, grad):
    return (grad,)

def back_keep(v):
    return (v, None)

def back_low(kept, grad):
    return (low(grad),)
low.defvjp(low_keep, low_pass)
low_back.defvjp(back_keep, back_low)

def rounded(value):
    return low_back(low(value))

def product(left, right):
    return jnp.dot(left, right, precision=lax.Precision.HIGHEST)

def normalize(values, gain):
    scale = lax.rsqrt(lax.optimization_barrier(jnp.mean(values * values, axis=-1, keepdims=True)) + 1e-06)
    return values * scale * gain

def layer(inputs, seg_row, w_query, w_key, w_value, w_out, norm_attn, norm_ffn, pre_mix, post_mix, w_up, w_down):
    highest = lax.Precision.HIGHEST
    length = inputs.shape[0]
    heads = pre_mix.shape[0]
    head_width = inputs.shape[1] // heads
    h_attn = low(normalize(inputs, norm_attn))
    query = rounded(product(h_attn, w_query)).reshape(length, heads, head_width)
    keyed = rounded(product(h_attn, w_key)).reshape(length, heads, head_width)
    valued = rounded(product(h_attn, w_value)).reshape(length, heads, head_width)
    block_rows = min(512, length)
    places = jnp.arange(length, dtype=jnp.int32)

    def attend(start):
        query_block = lax.dynamic_slice_in_dim(query, start, block_rows, 0)
        row_place = start + jnp.arange(block_rows, dtype=jnp.int32)
        row_seg = lax.dynamic_slice_in_dim(seg_row, start, block_rows, 0)
        logits = rounded(jnp.einsum('qgd,kgd->gqk', query_block, keyed, precision=highest) * head_width ** (-0.5))
        mixed = low_back(jnp.einsum('gh,gqk->hqk', pre_mix, logits, precision=highest))
        allowed = (row_seg[:, None] == seg_row[None, :]) & (places[None, :] <= row_place[:, None])
        mixed = jnp.where(allowed[None], mixed, -1e+30)
        top = lax.optimization_barrier(jnp.max(mixed, axis=-1, keepdims=True))
        expd = jnp.exp(mixed - top)
        weights = low(expd / lax.optimization_barrier(jnp.sum(expd, axis=-1, keepdims=True)))
        post = rounded(jnp.einsum('gh,gqk->hqk', post_mix, weights, precision=highest))
        result = jnp.einsum('hqk,khd->qhd', post, valued, precision=highest)
        return result.reshape(block_rows, heads * head_width)
    starts = jnp.arange(length // block_rows, dtype=jnp.int32) * block_rows
    attended = rounded(lax.map(jax.checkpoint(attend), starts).reshape(length, heads * head_width))
    after_attn = inputs + low_back(product(attended, w_out))
    h_ffn = low(normalize(after_attn, norm_ffn))
    hidden = rounded(jax.nn.gelu(product(h_ffn, w_up), approximate=False))
    return after_attn + product(hidden, w_down.T)

def reference(tokens, segments, w_query, w_key, w_value, w_out, norm_attn, norm_ffn, pre_mix, post_mix, w_up, w_down, out_grad):
    params = (w_query.astype(jnp.float32), w_key.astype(jnp.float32), w_value.astype(jnp.float32), w_out.astype(jnp.float32), norm_attn.astype(jnp.float32), norm_ffn.astype(jnp.float32), pre_mix.astype(jnp.float32), post_mix.astype(jnp.float32), w_up.astype(jnp.float32), w_down.astype(jnp.float32))
    seq_count = MICRO * SEQS
    flat_inputs = tokens.reshape(seq_count, SEQ, D).astype(jnp.float32)
    flat_segments = segments.reshape(seq_count, SEQ)
    flat_grads = out_grad.reshape(seq_count, SEQ, D).astype(jnp.float32)

    def one_sequence(carry, packed):
        inputs, seg_row, cotangent = packed

        def forward(values, *weights):
            return layer(values, seg_row, *weights)
        result, pull = jax.vjp(forward, inputs, *params)
        grads = pull(cotangent)
        carry = tuple((total + grad for total, grad in zip(carry, grads[1:])))
        return (carry, (result.astype(jnp.bfloat16), grads[0]))
    zeros = tuple((jnp.zeros(param.shape, jnp.float32) for param in params))
    sums, (results, input_grads) = lax.scan(one_sequence, zeros, (flat_inputs, flat_segments, flat_grads))
    return (results.reshape(tokens.shape), input_grads.reshape(tokens.shape), sums[0], sums[1], sums[2], sums[3], sums[4], sums[5], sums[6], sums[7], sums[8], sums[9])
```

```python
import functools

import jax
import jax.numpy as jnp
from jax import lax
from jax.experimental import pallas as pl
from jax.experimental.pallas import tpu as pltpu
from jax.sharding import PartitionSpec as P

F32 = jnp.float32
BF16 = jnp.bfloat16
BLOCK = 128
TILE = 2 * BLOCK
AXES = ("dp", "tensor")


def matmul(left, right):
    return jnp.dot(left, right, preferred_element_type=F32)


def right_t(left, right):
    return lax.dot_general(left, right, (((1,), (1,)), ((), ())), preferred_element_type=F32)


def left_t(left, right):
    return lax.dot_general(left, right, (((0,), (0,)), ((), ())), preferred_element_type=F32)


def rms_scale(values):
    return lax.rsqrt(jnp.mean(values * values, axis=-1, keepdims=True) + 1e-06)


def rms_back(grad_norm, normed, scale, gain):
    scaled = grad_norm * gain
    return scale * (scaled - normed * jnp.mean(scaled * normed, axis=-1, keepdims=True))


def gelu_exact(values):
    return jax.nn.gelu(values, approximate=False)


def gelu_back(upper, grad):
    unused, pull = jax.vjp(gelu_exact, upper)
    return pull(grad)[0]


def send(x, to):
    nd, nt = lax.axis_size("dp"), lax.axis_size("tensor")
    pairs = []
    for d in range(nd):
        for t in range(nt):
            d2, t2 = to(d, t)
            pairs.append((d * nt + t, d2 * nt + t2))
    return lax.ppermute(x, AXES, pairs)


def by_shift(shift):
    nt = lax.axis_size("tensor")
    return lambda d, t: (d, (t + shift) % nt)


def by_bit(bit):
    return lambda d, t: (d ^ bit, t)


def gather(piece, bits):
    nt = lax.axis_size("tensor")
    have = {0: jnp.stack([piece] + [send(piece, by_shift(s)) for s in range(1, nt)])}
    for bit in bits:
        have.update({mask | bit: send(block, by_bit(bit)) for mask, block in have.items()})
    return [have[mask] for mask in range(len(have))]


def place_kernel(slot_of, *refs):
    pieces, out, sem = refs[:-2], refs[-2], refs[-1]
    copies = []
    for mask, piece in enumerate(pieces):
        for shift in range(piece.shape[0]):
            copies.append(
                pltpu.make_async_copy(piece.at[shift], out.at[slot_of(mask, shift)], sem)
            )
    for copy in copies:
        copy.start()
    for copy in copies:
        copy.wait()


def placed(pieces, tensor_first):
    nd, nt = len(pieces), pieces[0].shape[0]

    def slot_of(mask, shift):
        d = lax.axis_index("dp") ^ mask
        t = lax.rem(lax.axis_index("tensor") + (nt - shift), nt)
        return t * nd + d if tensor_first else d * nt + t

    return pl.pallas_call(
        functools.partial(place_kernel, slot_of),
        out_shape=jax.ShapeDtypeStruct((nd * nt,) + pieces[0].shape[1:], pieces[0].dtype),
        in_specs=[pl.BlockSpec(memory_space=pl.ANY)] * nd,
        out_specs=pl.BlockSpec(memory_space=pl.ANY),
        scratch_shapes=[pltpu.SemaphoreType.DMA],
        name="place",
    )(*pieces)


def pick(x, index, axis):
    return lax.dynamic_index_in_dim(x, index, axis, keepdims=False)


def sum_to_owner(x, bits):
    nt, nd = x.shape[:2]
    d, t = lax.axis_index("dp"), lax.axis_index("tensor")
    rest = x.shape[2:]
    names = [1 << k for k in range(nd.bit_length() - 1)][::-1]
    x = x.reshape((nt,) + (2,) * len(names) + rest)
    for bit in bits:
        axis = 1 + names.index(bit)
        names.remove(bit)
        mine = (d // bit) % 2
        got = send(pick(x, 1 - mine, axis), by_bit(bit))
        x = pick(x, mine, axis).astype(F32) + got.astype(F32)
        if names or nt > 1:
            x = x.astype(BF16)
    total = pick(x, t, 0).astype(F32)
    for shift in range(1, nt):
        total = total + send(pick(x, lax.rem(t + shift, nt), 0), by_shift(shift)).astype(F32)
    return total


def seat(turn):
    nt = lax.axis_size("tensor")
    t, core = lax.axis_index("tensor"), lax.axis_index("dp") % 2
    block = lax.rem(turn + t, nt)
    source = lax.rem(2 * (t // 2) + core + nt - turn, nt)
    return block, source


def turn_to(turn):
    nt = lax.axis_size("tensor")

    def to(d, t):
        block = (turn + t) % nt
        return d - d % 2 + block % 2, 2 * (block // 2) + d % 2

    return to


def turn_back(turn):
    nt = lax.axis_size("tensor")

    def to(d, t):
        return d - d % 2 + t % 2, (2 * (t // 2) + d % 2 + nt - turn) % nt

    return to


def to_sequences(x):
    micro, _, rows, width = x.shape
    nt = lax.axis_size("tensor")
    x = x.reshape(micro, rows // TILE, 2, BLOCK, width).transpose(0, 2, 1, 3, 4)
    x = x.reshape(nt, rows // 2, width)
    return [send(pick(x, seat(turn)[0], 0), turn_to(turn)) for turn in range(nt)]


def from_sequences(pieces, micro):
    nt = len(pieces)
    half, width = pieces[0].shape
    back = [send(piece, turn_back(turn)) for turn, piece in enumerate(pieces)]
    back = jnp.stack(back + back[:-1])
    t = lax.axis_index("tensor")
    x = lax.dynamic_slice_in_dim(back, lax.rem(nt - t, nt), nt, 0)
    x = x.reshape(micro, 2, half // BLOCK, BLOCK, width).transpose(0, 2, 1, 3, 4)
    return x.reshape(micro, 1, 2 * half, width)


def load_rows(core, own, other, scratch, sem):
    blocks = own.shape[0]
    copies = []
    for k in range(blocks):
        copies.append(pltpu.make_async_copy(own.at[k], scratch.at[1 + 2 * k + core], sem))
        copies.append(pltpu.make_async_copy(other.at[k], scratch.at[2 + 2 * k - core], sem))
    return copies


def row_mask(row_seg, col_seg, row_place, col_start):
    rows, cols = row_seg.shape[0], col_seg.shape[1]
    place = col_start + lax.broadcasted_iota(jnp.int32, (rows, cols), 1)
    allowed = (row_seg == col_seg) & (place <= row_place)
    return jnp.where(allowed, 0.0, -1e30).astype(F32)


def spread(row, heads, query):
    return [(query * row[h : h + 1, :]).astype(BF16) for h in range(heads)]


def forward_kernel(
    heads, groups, info, q_ref, ko, kx, vo, vx, seg_rows, seg_cols, pre_ref, post_ref,
    att_ref, u_ref, lse_ref, k_s, v_s, qp_s, s_s, m_s, l_s, u_s, sem,
):
    step = pl.program_id(0)
    core = info[0]
    blocks = ko.shape[0]

    @pl.when(step == 0)
    def _():
        copies = load_rows(core, ko, kx, k_s, sem) + load_rows(core, vo, vx, v_s, sem)
        for copy in copies:
            copy.start()
        k_s[0] = jnp.zeros(k_s.shape[1:], BF16)
        v_s[0] = jnp.zeros(v_s.shape[1:], BF16)
        for copy in copies:
            copy.wait()

    block = info[1 + step]
    tiles = info[1 + blocks + step]
    query = q_ref[...].astype(F32)
    for h, part in enumerate(spread(pre_ref, heads, query)):
        qp_s[h * BLOCK : (h + 1) * BLOCK, :] = part
    row_seg = seg_rows[0]
    row_place = block * BLOCK + lax.broadcasted_iota(jnp.int32, (BLOCK, 1), 0)
    m_s[...] = jnp.full(m_s.shape, -3e38, F32)
    l_s[...] = jnp.zeros(l_s.shape, F32)
    u_s[...] = jnp.zeros(u_s.shape, F32)
    size = heads // groups * BLOCK

    def scores(tile, carry):
        first = block + 2 - 2 * (tile + 1)
        keys = k_s[pl.ds(first, 2)].reshape(TILE, -1)
        col_seg = jnp.concatenate([seg_cols[first], seg_cols[first + 1]], axis=1)
        mask = row_mask(row_seg, col_seg, row_place, (first - 1) * BLOCK)
        for g in range(groups):
            rows = pl.ds(g * size, size)
            s = right_t(qp_s[rows, :], keys)
            s = (s.reshape(heads // groups, BLOCK, TILE) + mask[None]).reshape(size, TILE)
            s_s[tile, rows, :] = s
            m_s[rows, :] = jnp.maximum(m_s[rows, :], jnp.maximum(s[:, :BLOCK], s[:, BLOCK:]))
        return carry

    lax.fori_loop(0, tiles, scores, 0)
    m_s[...] = jnp.broadcast_to(jnp.max(m_s[...], axis=-1, keepdims=True), m_s.shape)

    def weigh(tile, carry):
        first = block + 2 - 2 * (tile + 1)
        values = v_s[pl.ds(first, 2)].reshape(TILE, -1)
        for g in range(groups):
            rows = pl.ds(g * size, size)
            top = m_s[rows, :]
            p = jnp.exp(s_s[tile, rows, :] - jnp.concatenate([top, top], axis=1))
            l_s[rows, :] += p[:, :BLOCK] + p[:, BLOCK:]
            u_s[rows, :] += matmul(p.astype(BF16), values)
        return carry

    lax.fori_loop(0, tiles, weigh, 0)
    att = jnp.zeros((BLOCK, att_ref.shape[1]), F32)
    for h in range(heads):
        rows = slice(h * BLOCK, (h + 1) * BLOCK)
        total = jnp.sum(l_s[rows, :], axis=-1, keepdims=True)
        lse_ref[0, rows, :] = m_s[rows, :] + jnp.log(total)
        u = u_s[rows, :] * (1.0 / total)
        u_ref[0, h] = u.astype(BF16)
        att = att + u * post_ref[h : h + 1, :]
    att_ref[...] = att.astype(BF16)


def whole(shape):
    return pl.BlockSpec(shape, lambda i, info: (0,) * len(shape))


ANY = pl.BlockSpec(memory_space=pl.ANY)


def attend(info, query, k_own, k_other, v_own, v_other, seg_rows, seg_cols, pre, post):
    heads, width = pre.shape
    blocks = k_own.shape[0]
    rows, stack = blocks * BLOCK, heads * BLOCK
    most = info.shape[0] and (1024 // BLOCK + 2) // 2
    groups = 4
    return pl.pallas_call(
        functools.partial(forward_kernel, heads, groups),
        grid_spec=pltpu.PrefetchScalarGridSpec(
            num_scalar_prefetch=1,
            grid=(blocks,),
            in_specs=[
                pl.BlockSpec((BLOCK, width), lambda i, info: (i, 0)),
                ANY, ANY, ANY, ANY,
                pl.BlockSpec((1, BLOCK, 1), lambda i, info: (i, 0, 0)),
                whole(seg_cols.shape), whole(pre.shape), whole(post.shape),
            ],
            out_specs=[
                pl.BlockSpec((BLOCK, width), lambda i, info: (i, 0)),
                pl.BlockSpec((1, heads, BLOCK, width), lambda i, info: (i, 0, 0, 0)),
                pl.BlockSpec((1, stack, BLOCK), lambda i, info: (i, 0, 0)),
            ],
            scratch_shapes=[
                pltpu.VMEM((2 * blocks + 1, BLOCK, width), BF16),
                pltpu.VMEM((2 * blocks + 1, BLOCK, width), BF16),
                pltpu.VMEM((stack, width), BF16),
                pltpu.VMEM((most, stack, TILE), F32),
                pltpu.VMEM((stack, BLOCK), F32),
                pltpu.VMEM((stack, BLOCK), F32),
                pltpu.VMEM((stack, width), F32),
                pltpu.SemaphoreType.DMA,
            ],
        ),
        out_shape=[
            jax.ShapeDtypeStruct((rows, width), BF16),
            jax.ShapeDtypeStruct((blocks, heads, BLOCK, width), BF16),
            jax.ShapeDtypeStruct((blocks, stack, BLOCK), F32),
        ],
        compiler_params=pltpu.CompilerParams(vmem_limit_bytes=60 << 20),
        name="attend",
    )(info, query, k_own, k_other, v_own, v_other, seg_rows, seg_cols, pre, post)


def backward_kernel(
    heads, groups, info, q_ref, g_ref, u_ref, lse_ref, ko, kx, vo, vx, seg_rows, seg_cols, pre_ref, post_ref,
    dq_ref, dk_ref, dv_ref, dpre_ref, dpost_ref,
    k_s, v_s, dk_s, dv_s, qp_s, gp_s, d_s, t_s, sem,
):
    step = pl.program_id(0)
    core = info[0]
    blocks = ko.shape[0]

    @pl.when(step == 0)
    def _():
        copies = load_rows(core, ko, kx, k_s, sem) + load_rows(core, vo, vx, v_s, sem)
        for copy in copies:
            copy.start()
        k_s[0] = jnp.zeros(k_s.shape[1:], BF16)
        v_s[0] = jnp.zeros(v_s.shape[1:], BF16)
        dk_s[...] = jnp.zeros(dk_s.shape, F32)
        dv_s[...] = jnp.zeros(dv_s.shape, F32)
        dpre_ref[...] = jnp.zeros(dpre_ref.shape, F32)
        dpost_ref[...] = jnp.zeros(dpost_ref.shape, F32)
        for copy in copies:
            copy.wait()

    block = info[1 + step]
    tiles = info[1 + blocks + step]
    query = q_ref[...].astype(F32)
    grad = g_ref[...].astype(F32)
    for h in range(heads):
        rows = slice(h * BLOCK, (h + 1) * BLOCK)
        qp_s[rows, :] = (query * pre_ref[h : h + 1, :]).astype(BF16)
        gain = post_ref[h : h + 1, :]
        gp_s[rows, :] = (grad * gain).astype(BF16)
        both = grad * u_ref[0, h].astype(F32)
        d_s[rows, :] = jnp.broadcast_to(jnp.sum(both * gain, axis=-1, keepdims=True), (BLOCK, BLOCK))
        dpost_ref[h] += jnp.sum(both.reshape(BLOCK // 8, 8, -1), axis=0)
    row_seg = seg_rows[0]
    row_place = block * BLOCK + lax.broadcasted_iota(jnp.int32, (BLOCK, 1), 0)
    t_s[...] = jnp.zeros(t_s.shape, F32)
    size = heads // groups * BLOCK

    def tile_step(tile, carry):
        first = block + 2 - 2 * (tile + 1)
        keys = k_s[pl.ds(first, 2)].reshape(TILE, -1)
        values = v_s[pl.ds(first, 2)].reshape(TILE, -1)
        col_seg = jnp.concatenate([seg_cols[first], seg_cols[first + 1]], axis=1)
        mask = row_mask(row_seg, col_seg, row_place, (first - 1) * BLOCK)
        dk = jnp.zeros((TILE, keys.shape[1]), F32)
        dv = jnp.zeros((TILE, keys.shape[1]), F32)
        for g in range(groups):
            rows = pl.ds(g * size, size)
            s = right_t(qp_s[rows, :], keys)
            s = (s.reshape(heads // groups, BLOCK, TILE) + mask[None]).reshape(size, TILE)
            top = lse_ref[0, rows, :]
            p = jnp.exp(s - jnp.concatenate([top, top], axis=1))
            dw = right_t(gp_s[rows, :], values)
            term = d_s[rows, :]
            ds = (p * (dw - jnp.concatenate([term, term], axis=1))).astype(BF16)
            t_s[rows, :] += matmul(ds, keys)
            dv = dv + left_t(p.astype(BF16), gp_s[rows, :])
            dk = dk + left_t(ds, qp_s[rows, :])
        dk_s[pl.ds(first, 2)] += dk.reshape(2, BLOCK, -1)
        dv_s[pl.ds(first, 2)] += dv.reshape(2, BLOCK, -1)
        return carry

    lax.fori_loop(0, tiles, tile_step, 0)
    dq = jnp.zeros(query.shape, F32)
    for h in range(heads):
        part = t_s[h * BLOCK : (h + 1) * BLOCK, :]
        dq = dq + part * pre_ref[h : h + 1, :]
        dpre_ref[h] += jnp.sum((query * part).reshape(BLOCK // 8, 8, -1), axis=0)
    dq_ref[...] = dq.astype(BF16)

    @pl.when(step == blocks - 1)
    def _():
        for k in range(blocks):
            for part in range(2):
                place = 1 + 2 * k + (core if part == 0 else 1 - core)
                dk_ref[part, k] = dk_s[place].astype(BF16)
                dv_ref[part, k] = dv_s[place].astype(BF16)


def attend_back(info, query, grad, u, lse, k_own, k_other, v_own, v_other, seg_rows, seg_cols, pre, post):
    heads, width = pre.shape
    blocks = k_own.shape[0]
    rows, stack = blocks * BLOCK, heads * BLOCK
    groups = 4
    return pl.pallas_call(
        functools.partial(backward_kernel, heads, groups),
        grid_spec=pltpu.PrefetchScalarGridSpec(
            num_scalar_prefetch=1,
            grid=(blocks,),
            in_specs=[
                pl.BlockSpec((BLOCK, width), lambda i, info: (i, 0)),
                pl.BlockSpec((BLOCK, width), lambda i, info: (i, 0)),
                pl.BlockSpec((1, heads, BLOCK, width), lambda i, info: (i, 0, 0, 0)),
                pl.BlockSpec((1, stack, BLOCK), lambda i, info: (i, 0, 0)),
                ANY, ANY, ANY, ANY,
                pl.BlockSpec((1, BLOCK, 1), lambda i, info: (i, 0, 0)),
                whole(seg_cols.shape), whole(pre.shape), whole(post.shape),
            ],
            out_specs=[
                pl.BlockSpec((BLOCK, width), lambda i, info: (i, 0)),
                whole((2, blocks, BLOCK, width)),
                whole((2, blocks, BLOCK, width)),
                whole((heads, 8, width)),
                whole((heads, 8, width)),
            ],
            scratch_shapes=[
                pltpu.VMEM((2 * blocks + 1, BLOCK, width), BF16),
                pltpu.VMEM((2 * blocks + 1, BLOCK, width), BF16),
                pltpu.VMEM((2 * blocks + 1, BLOCK, width), F32),
                pltpu.VMEM((2 * blocks + 1, BLOCK, width), F32),
                pltpu.VMEM((stack, width), BF16),
                pltpu.VMEM((stack, width), BF16),
                pltpu.VMEM((stack, BLOCK), F32),
                pltpu.VMEM((stack, width), F32),
                pltpu.SemaphoreType.DMA,
            ],
        ),
        out_shape=[
            jax.ShapeDtypeStruct((rows, width), BF16),
            jax.ShapeDtypeStruct((2, blocks, BLOCK, width), BF16),
            jax.ShapeDtypeStruct((2, blocks, BLOCK, width), BF16),
            jax.ShapeDtypeStruct((heads, 8, width), F32),
            jax.ShapeDtypeStruct((heads, 8, width), F32),
        ],
        compiler_params=pltpu.CompilerParams(vmem_limit_bytes=62 << 20),
        name="attend_back",
    )(info, query, grad, u, lse, k_own, k_other, v_own, v_other, seg_rows, seg_cols, pre, post)


def per_device(
    tokens, segments, w_query, w_key, w_value, w_out, norm_attn, norm_ffn, pre_mix, post_mix, w_up, w_down, out_grad,
):
    micro, _, rows, width = tokens.shape
    nd, nt = lax.axis_size("dp"), lax.axis_size("tensor")
    heads = pre_mix.shape[0]
    head_width = width // heads
    length = rows * nt
    count = length // 2
    blocks = count // BLOCK
    share = w_query.shape[0]
    bits = [1 << k for k in range(nd.bit_length() - 1)]
    d, t = lax.axis_index("dp"), lax.axis_index("tensor")
    core = d % 2

    gains = jnp.concatenate([norm_attn, norm_ffn, jnp.zeros((width - 2 * share,), BF16)])[None]
    gains = jnp.concatenate([gains, jnp.zeros((7, width), BF16)])
    bundle = jnp.concatenate([w_query, w_key, w_value, w_out, gains])
    order = bits[1:][::-1] + bits[:1]
    everything = placed(gather(bundle, order), False)
    all_query, all_key, all_value, all_out = (
        everything[:, k * share : (k + 1) * share].reshape(width, width) for k in range(4)
    )
    gain_attn = everything[:, 4 * share, :share].reshape(width).astype(F32)
    gain_ffn = everything[:, 4 * share, share : 2 * share].reshape(width).astype(F32)
    all_up = placed(gather(w_up, order), True).reshape(nt, width, -1)
    all_down = placed(gather(w_down, bits[1:] + bits[:1]), True).reshape(nt, width, -1)

    token_turns = to_sequences(tokens)
    grad_turns = to_sequences(out_grad)
    segs = segments.reshape(micro, length)
    segs = jnp.where(t % 2 == core, segs, send(segs, by_bit(1)))
    segs = pick(segs, t // 2, 0)
    sources = jnp.stack([seat(turn)[1] for turn in range(nt)])
    per_turn = blocks // nt
    block_ids = (2 * (sources[:, None] * per_turn + jnp.arange(per_turn)) + core).reshape(blocks)
    block_segs = segs.reshape(2 * blocks, BLOCK)
    starts = jnp.sum(segs[None, :] < block_segs[:, :1], axis=1) // BLOCK
    tiles = (jnp.arange(2 * blocks) + 2 - starts) // 2
    info = jnp.concatenate([core[None], block_ids, tiles[block_ids]]).astype(jnp.int32)
    seg_rows = block_segs[block_ids][:, :, None]
    seg_cols = jnp.concatenate([jnp.full((1, BLOCK), -1, jnp.int32), block_segs])[:, None, :]

    def by_lane(mix):
        return jnp.repeat(mix.astype(F32), head_width, axis=1)

    pre = by_lane(pre_mix.T) * head_width ** (-0.5)
    post = by_lane(post_mix)

    inputs = jnp.concatenate(token_turns).astype(F32)
    grad_out = jnp.concatenate(grad_turns)
    scale_attn = rms_scale(inputs)
    normed_attn = inputs * scale_attn
    h_attn = (normed_attn * gain_attn).astype(BF16)
    query = matmul(h_attn, all_query).astype(BF16)
    k_turn = matmul(h_attn, all_key).astype(BF16)
    v_turn = matmul(h_attn, all_value).astype(BF16)

    by_place = jnp.argsort(block_ids)
    in_turns = block_ids // 2

    def ordered(x):
        return x.reshape(blocks, BLOCK, width)[by_place]

    def turned(x):
        return x[in_turns].reshape(count, width)

    k_own, v_own = ordered(k_turn), ordered(v_turn)
    k_other, v_other = send(k_own, by_bit(1)), send(v_own, by_bit(1))
    attended, u, lse = attend(info, query, k_own, k_other, v_own, v_other, seg_rows, seg_cols, pre, post)

    after_attn = inputs + matmul(attended, all_out)
    scale_ffn = rms_scale(after_attn)
    normed_ffn = after_attn * scale_ffn
    h_ffn = (normed_ffn * gain_ffn).astype(BF16)
    upper = [matmul(h_ffn, all_up[k]) for k in range(nt)]
    hidden = [gelu_exact(up).astype(BF16) for up in upper]
    output = after_attn + sum(right_t(hidden[k], all_down[k]) for k in range(nt))
    d_hidden = [gelu_back(upper[k], matmul(grad_out, all_down[k])).astype(BF16) for k in range(nt)]
    grad_h_ffn = sum(right_t(d_hidden[k], all_up[k]) for k in range(nt))
    grad_up = jnp.stack([left_t(h_ffn, d_hidden[k]).astype(BF16) for k in range(nt)])
    grad_down = jnp.stack([left_t(grad_out, hidden[k]).astype(BF16) for k in range(nt)])
    grad_gain_ffn = jnp.sum(grad_h_ffn * normed_ffn, axis=0)
    grad_after = grad_out.astype(F32) + rms_back(grad_h_ffn, normed_ffn, scale_ffn, gain_ffn)
    grad_branch = grad_after.astype(BF16)
    grad_w_out = left_t(attended, grad_branch)
    grad_attended = right_t(grad_branch, all_out).astype(BF16)

    out_turns = jnp.split(output.astype(BF16), nt)
    out = from_sequences(out_turns, micro)
    part_up = sum_to_owner(grad_up.reshape(nt, nd, -1, grad_up.shape[2]), bits)
    part_down = sum_to_owner(grad_down.reshape(nt, nd, -1, grad_down.shape[2]), bits[:1] + bits[1:][::-1])

    grad_query, grad_key, grad_value, d_pre, d_post = attend_back(
        info, query, grad_attended, u, lse, k_own, k_other, v_own, v_other, seg_rows, seg_cols, pre, post
    )
    grad_key = turned((grad_key[0].astype(F32) + send(grad_key[1], by_bit(1)).astype(F32)).astype(BF16))
    grad_value = turned((grad_value[0].astype(F32) + send(grad_value[1], by_bit(1)).astype(F32)).astype(BF16))

    grad_h_attn = (
        right_t(grad_query, all_query) + right_t(grad_key, all_key) + right_t(grad_value, all_value)
    )
    grad_gain_attn = jnp.sum(grad_h_attn * normed_attn, axis=0)
    grad_tokens = grad_after + rms_back(grad_h_attn, normed_attn, scale_attn, gain_attn)
    d_tokens = from_sequences(jnp.split(grad_tokens.astype(BF16), nt), micro).astype(F32)

    grads = [left_t(h_attn, grad_query), left_t(h_attn, grad_key), left_t(h_attn, grad_value), grad_w_out]
    grads = jnp.stack([g.astype(BF16).reshape(nd, nt, share, width) for g in grads], axis=2)
    owned = sum_to_owner(grads.transpose(1, 0, 2, 3, 4), bits)

    d_pre = d_pre.reshape(heads, 8, heads, head_width).sum((1, 3)).T * head_width ** (-0.5)
    d_post = d_post.reshape(heads, 8, heads, head_width).sum((1, 3))
    small = jnp.concatenate([grad_gain_attn, grad_gain_ffn, d_pre.reshape(-1), d_post.reshape(-1)])
    small = lax.psum(small, AXES)
    place = (d * nt + t) * share
    return (
        out,
        d_tokens,
        owned[0],
        owned[1],
        owned[2],
        owned[3],
        lax.dynamic_slice_in_dim(small, place, share),
        lax.dynamic_slice_in_dim(small, width + place, share),
        small[2 * width : 2 * width + heads * heads].reshape(heads, heads),
        small[2 * width + heads * heads :].reshape(heads, heads),
        part_up,
        part_down,
    )


def solution(mesh):
    both = P(("dp", "tensor"), None)
    gain = P(("dp", "tensor"))
    data = P(None, "dp", "tensor", None)
    ffn = P("dp", "tensor")
    return jax.shard_map(
        per_device,
        mesh=mesh,
        in_specs=(data, P(None, "dp", None), both, both, both, both, gain, gain, P(), P(), ffn, ffn, data),
        out_specs=(data, data, both, both, both, both, gain, gain, P(), P(), ffn, ffn),
        check_vma=False,
    )
```

```python
import functools

import jax
import jax.numpy as jnp
from jax import lax
from jax.experimental import pallas as pl
from jax.experimental.pallas import tpu as pltpu
from jax.sharding import PartitionSpec as P

F32 = jnp.float32
BF16 = jnp.bfloat16
BLOCK = 128
TILE = 2 * BLOCK
AXES = ("dp", "tensor")


def matmul(left, right):
    return jnp.dot(left, right, preferred_element_type=F32)


def right_t(left, right):
    return lax.dot_general(left, right, (((1,), (1,)), ((), ())), preferred_element_type=F32)


def left_t(left, right):
    return lax.dot_general(left, right, (((0,), (0,)), ((), ())), preferred_element_type=F32)


def rms_scale(values):
    return lax.rsqrt(jnp.mean(values * values, axis=-1, keepdims=True) + 1e-06)


def rms_back(grad_norm, normed, scale, gain):
    scaled = grad_norm * gain
    return scale * (scaled - normed * jnp.mean(scaled * normed, axis=-1, keepdims=True))


def gelu_exact(values):
    return jax.nn.gelu(values, approximate=False)


def gelu_back(upper, grad):
    unused, pull = jax.vjp(gelu_exact, upper)
    return pull(grad)[0]


def send(x, to):
    nd, nt = lax.axis_size("dp"), lax.axis_size("tensor")
    pairs = []
    for d in range(nd):
        for t in range(nt):
            d2, t2 = to(d, t)
            pairs.append((d * nt + t, d2 * nt + t2))
    return lax.ppermute(x, AXES, pairs)


def by_shift(shift):
    nt = lax.axis_size("tensor")
    return lambda d, t: (d, (t + shift) % nt)


def by_bit(bit):
    return lambda d, t: (d ^ bit, t)


def gather(piece, bits):
    nt = lax.axis_size("tensor")
    have = {0: jnp.stack([piece] + [send(piece, by_shift(s)) for s in range(1, nt)])}
    for bit in bits:
        have.update({mask | bit: send(block, by_bit(bit)) for mask, block in have.items()})
    return [have[mask] for mask in range(len(have))]


def place_kernel(slot_of, *refs):
    pieces, out, sem = refs[:-2], refs[-2], refs[-1]
    copies = []
    for mask, piece in enumerate(pieces):
        for shift in range(piece.shape[0]):
            copies.append(
                pltpu.make_async_copy(piece.at[shift], out.at[slot_of(mask, shift)], sem)
            )
    for copy in copies:
        copy.start()
    for copy in copies:
        copy.wait()


def placed(pieces, tensor_first):
    nd, nt = len(pieces), pieces[0].shape[0]

    def slot_of(mask, shift):
        d = lax.axis_index("dp") ^ mask
        t = lax.rem(lax.axis_index("tensor") + (nt - shift), nt)
        return t * nd + d if tensor_first else d * nt + t

    return pl.pallas_call(
        functools.partial(place_kernel, slot_of),
        out_shape=jax.ShapeDtypeStruct((nd * nt,) + pieces[0].shape[1:], pieces[0].dtype),
        in_specs=[pl.BlockSpec(memory_space=pl.ANY)] * nd,
        out_specs=pl.BlockSpec(memory_space=pl.ANY),
        scratch_shapes=[pltpu.SemaphoreType.DMA],
        name="place",
    )(*pieces)


def pick(x, index, axis):
    return lax.dynamic_index_in_dim(x, index, axis, keepdims=False)


def sum_to_owner(x, bits):
    nt, nd = x.shape[:2]
    d, t = lax.axis_index("dp"), lax.axis_index("tensor")
    rest = x.shape[2:]
    names = [1 << k for k in range(nd.bit_length() - 1)][::-1]
    x = x.reshape((nt,) + (2,) * len(names) + rest)
    for bit in bits:
        axis = 1 + names.index(bit)
        names.remove(bit)
        mine = (d // bit) % 2
        got = send(pick(x, 1 - mine, axis), by_bit(bit))
        x = pick(x, mine, axis).astype(F32) + got.astype(F32)
        if names or nt > 1:
            x = x.astype(BF16)
    total = pick(x, t, 0).astype(F32)
    for shift in range(1, nt):
        total = total + send(pick(x, lax.rem(t + shift, nt), 0), by_shift(shift)).astype(F32)
    return total


def seat(turn):
    nt = lax.axis_size("tensor")
    t, core = lax.axis_index("tensor"), lax.axis_index("dp") % 2
    block = lax.rem(turn + t, nt)
    source = lax.rem(2 * (t // 2) + core + nt - turn, nt)
    return block, source


def turn_to(turn):
    nt = lax.axis_size("tensor")

    def to(d, t):
        block = (turn + t) % nt
        return d - d % 2 + block % 2, 2 * (block // 2) + d % 2

    return to


def turn_back(turn):
    nt = lax.axis_size("tensor")

    def to(d, t):
        return d - d % 2 + t % 2, (2 * (t // 2) + d % 2 + nt - turn) % nt

    return to


def split_kernel(x_ref, *outs):
    for turn, out in enumerate(outs):
        block = seat(turn)[0]
        out[...] = x_ref[block // 2, :, block % 2].reshape(out.shape)


def join_kernel(*refs):
    out = refs[-1]
    for turn, piece in enumerate(refs[:-1]):
        block = seat(turn)[0]
        out[block // 2, :, block % 2] = piece[...].reshape(out.shape[1], BLOCK, out.shape[4])


def to_sequences(x):
    micro, _, rows, width = x.shape
    nt = lax.axis_size("tensor")
    pieces = pl.pallas_call(
        split_kernel, out_shape=[jax.ShapeDtypeStruct((rows // 2, width), x.dtype)] * nt, name="split"
    )(x.reshape(micro, rows // TILE, 2, BLOCK, width))
    return [send(piece, turn_to(turn)) for turn, piece in enumerate(pieces)]


def from_sequences(pieces, micro):
    half, width = pieces[0].shape
    back = [send(piece, turn_back(turn)) for turn, piece in enumerate(pieces)]
    out = pl.pallas_call(
        join_kernel,
        out_shape=jax.ShapeDtypeStruct((micro, half // BLOCK, 2, BLOCK, width), pieces[0].dtype),
        name="join",
    )(*back)
    return out.reshape(micro, 1, 2 * half, width)


def load_rows(rows, scratch, sem):
    return pltpu.make_async_copy(rows, scratch.at[pl.ds(1, rows.shape[0])], sem)


def reach(block, seg_low):
    first = seg_low[block, 0]
    before = 0
    for k in range(seg_low.shape[0]):
        before += (seg_low[k, BLOCK - 1] < first).astype(jnp.int32)
    return (block + 2 - before) // 2


def rows_of(block, seg_s):
    return jnp.broadcast_to(seg_s[block + 1], (BLOCK, BLOCK)).T


def row_mask(row_seg, first, block, seg_s):
    row = lax.broadcasted_iota(jnp.int32, (BLOCK, BLOCK), 0)
    col = lax.broadcasted_iota(jnp.int32, (BLOCK, BLOCK), 1)
    masks = []
    for k in range(2):
        ahead = (first + k - 1 - block) * BLOCK
        allowed = (row_seg == seg_s[first + k]) & (col + ahead <= row)
        masks.append(jnp.where(allowed, 0.0, -1e30).astype(F32))
    return jnp.concatenate(masks, axis=1)


def forward_kernel(
    heads, groups, q_ref, k_all, v_all, seg_low, seg_ref, pre_ref, post_ref,
    att_ref, u_ref, lse_ref, k_s, v_s, seg_s, qp_s, s_s, m_s, l_s, u_s, sems,
):
    step = pl.program_id(0)
    core = lax.axis_index("dp") % 2

    @pl.when(step == 0)
    def _():
        copies = [load_rows(k_all, k_s, sems.at[0]), load_rows(v_all, v_s, sems.at[1])]
        for copy in copies:
            copy.start()
        seg_s[0] = jnp.full((1, BLOCK), -1, jnp.int32)
        seg_s[1:] = seg_ref[...]
        k_s[0] = jnp.zeros(k_s.shape[1:], BF16)
        v_s[0] = jnp.zeros(v_s.shape[1:], BF16)
        for copy in copies:
            copy.wait()

    block = 2 * step + core
    tiles = reach(block, seg_low)
    query = q_ref[...].astype(F32)
    for h in range(heads):
        qp_s[h * BLOCK : (h + 1) * BLOCK, :] = (query * pre_ref[h : h + 1, :]).astype(BF16)
    row_seg = rows_of(block, seg_s)
    m_s[...] = jnp.full(m_s.shape, -3e38, F32)
    l_s[...] = jnp.zeros(l_s.shape, F32)
    u_s[...] = jnp.zeros(u_s.shape, F32)
    size = heads // groups * BLOCK

    def scores(tile, carry):
        first = block + 2 - 2 * (tile + 1)
        keys = k_s[pl.ds(first, 2)].reshape(TILE, -1)
        mask = row_mask(row_seg, first, block, seg_s)
        for g in range(groups):
            rows = pl.ds(g * size, size)
            s = right_t(qp_s[rows, :], keys)
            s = (s.reshape(heads // groups, BLOCK, TILE) + mask[None]).reshape(size, TILE)
            s_s[tile, rows, :] = s
            m_s[rows, :] = jnp.maximum(m_s[rows, :], jnp.maximum(s[:, :BLOCK], s[:, BLOCK:]))
        return carry

    lax.fori_loop(0, tiles, scores, 0)
    m_s[...] = jnp.broadcast_to(jnp.max(m_s[...], axis=-1, keepdims=True), m_s.shape)

    def weigh(tile, carry):
        first = block + 2 - 2 * (tile + 1)
        values = v_s[pl.ds(first, 2)].reshape(TILE, -1)
        for g in range(groups):
            rows = pl.ds(g * size, size)
            top = m_s[rows, :]
            p = jnp.exp(s_s[tile, rows, :] - jnp.concatenate([top, top], axis=1))
            l_s[rows, :] += p[:, :BLOCK] + p[:, BLOCK:]
            u_s[rows, :] += matmul(p.astype(BF16), values)
        return carry

    lax.fori_loop(0, tiles, weigh, 0)
    att = jnp.zeros((BLOCK, att_ref.shape[1]), F32)
    for h in range(heads):
        rows = slice(h * BLOCK, (h + 1) * BLOCK)
        total = jnp.sum(l_s[rows, :], axis=-1, keepdims=True)
        lse_ref[0, rows, :] = m_s[rows, :] + jnp.log(total)
        u = u_s[rows, :] * (1.0 / total)
        u_ref[0, h] = u.astype(BF16)
        att = att + u * post_ref[h : h + 1, :]
    att_ref[...] = att.astype(BF16)


def whole(shape):
    return pl.BlockSpec(shape, lambda i: (0,) * len(shape), pipeline_mode=pl.Buffered(1))


def cost(flops, moved):
    return pl.CostEstimate(flops=int(flops), bytes_accessed=int(moved), transcendentals=0)


ANY = pl.BlockSpec(memory_space=pl.ANY)
SCALARS = pl.BlockSpec(memory_space=pltpu.SMEM)


def attend(query, k_all, v_all, segs, pre, post):
    heads, width = pre.shape
    rows, stack = query.shape[0], heads * BLOCK
    blocks = rows // BLOCK
    most = (1024 // BLOCK + 2) // 2
    groups = 4
    by_block = pl.BlockSpec((BLOCK, width), lambda i: (i, 0))
    return pl.pallas_call(
        functools.partial(forward_kernel, heads, groups),
        grid=(blocks,),
        in_specs=[
            by_block, ANY, ANY, SCALARS, whole((2 * blocks, 1, BLOCK)), whole(pre.shape), whole(post.shape),
        ],
        out_specs=[
            by_block,
            pl.BlockSpec((1, heads, BLOCK, width), lambda i: (i, 0, 0, 0)),
            pl.BlockSpec((1, stack, BLOCK), lambda i: (i, 0, 0)),
        ],
        scratch_shapes=[
            pltpu.VMEM((2 * blocks + 1, BLOCK, width), BF16),
            pltpu.VMEM((2 * blocks + 1, BLOCK, width), BF16),
            pltpu.VMEM((2 * blocks + 1, 1, BLOCK), jnp.int32),
            pltpu.VMEM((stack, width), BF16),
            pltpu.VMEM((most, stack, TILE), F32),
            pltpu.VMEM((stack, BLOCK), F32),
            pltpu.VMEM((stack, BLOCK), F32),
            pltpu.VMEM((stack, width), F32),
            pltpu.SemaphoreType.DMA((2,)),
        ],
        out_shape=[
            jax.ShapeDtypeStruct((rows, width), BF16),
            jax.ShapeDtypeStruct((blocks, heads, BLOCK, width), BF16),
            jax.ShapeDtypeStruct((blocks, stack, BLOCK), F32),
        ],
        compiler_params=pltpu.CompilerParams(vmem_limit_bytes=60 << 20),
        cost_estimate=cost(4 * rows * 1024 * stack // BLOCK * width, 4 * rows * stack // BLOCK * width),
        name="attend",
    )(query, k_all, v_all, segs, segs[:, None, :], pre, post)


def backward_kernel(
    heads, groups, q_ref, g_ref, u_ref, lse_ref, k_all, v_all, seg_low, seg_ref, pre_ref, post_ref,
    dq_ref, dk_ref, dv_ref, dpre_ref, dpost_ref,
    k_s, v_s, seg_s, dk_s, dv_s, qp_s, gp_s, d_s, t_s, sems,
):
    step = pl.program_id(0)
    core = lax.axis_index("dp") % 2

    @pl.when(step == 0)
    def _():
        copies = [load_rows(k_all, k_s, sems.at[0]), load_rows(v_all, v_s, sems.at[1])]
        for copy in copies:
            copy.start()
        seg_s[0] = jnp.full((1, BLOCK), -1, jnp.int32)
        seg_s[1:] = seg_ref[...]
        k_s[0] = jnp.zeros(k_s.shape[1:], BF16)
        v_s[0] = jnp.zeros(v_s.shape[1:], BF16)
        dk_s[...] = jnp.zeros(dk_s.shape, F32)
        dv_s[...] = jnp.zeros(dv_s.shape, F32)
        dpre_ref[...] = jnp.zeros(dpre_ref.shape, F32)
        dpost_ref[...] = jnp.zeros(dpost_ref.shape, F32)
        for copy in copies:
            copy.wait()

    block = 2 * step + core
    tiles = reach(block, seg_low)
    query = q_ref[...].astype(F32)
    grad = g_ref[...].astype(F32)
    for h in range(heads):
        rows = slice(h * BLOCK, (h + 1) * BLOCK)
        qp_s[rows, :] = (query * pre_ref[h : h + 1, :]).astype(BF16)
        gain = post_ref[h : h + 1, :]
        gp_s[rows, :] = (grad * gain).astype(BF16)
        both = grad * u_ref[0, h].astype(F32)
        d_s[rows, :] = jnp.broadcast_to(jnp.sum(both * gain, axis=-1, keepdims=True), (BLOCK, BLOCK))
        dpost_ref[h] += jnp.sum(both.reshape(BLOCK // 8, 8, -1), axis=0)
    row_seg = rows_of(block, seg_s)
    t_s[...] = jnp.zeros(t_s.shape, F32)
    size = heads // groups * BLOCK

    def tile_step(tile, carry):
        first = block + 2 - 2 * (tile + 1)
        keys = k_s[pl.ds(first, 2)].reshape(TILE, -1)
        values = v_s[pl.ds(first, 2)].reshape(TILE, -1)
        mask = row_mask(row_seg, first, block, seg_s)
        dk = jnp.zeros((TILE, keys.shape[1]), F32)
        dv = jnp.zeros((TILE, keys.shape[1]), F32)
        for g in range(groups):
            rows = pl.ds(g * size, size)
            s = right_t(qp_s[rows, :], keys)
            s = (s.reshape(heads // groups, BLOCK, TILE) + mask[None]).reshape(size, TILE)
            top = lse_ref[0, rows, :]
            p = jnp.exp(s - jnp.concatenate([top, top], axis=1))
            dw = right_t(gp_s[rows, :], values)
            term = d_s[rows, :]
            ds = (p * (dw - jnp.concatenate([term, term], axis=1))).astype(BF16)
            t_s[rows, :] += matmul(ds, keys)
            dv = dv + left_t(p.astype(BF16), gp_s[rows, :])
            dk = dk + left_t(ds, qp_s[rows, :])
        dk_s[pl.ds(first, 2)] += dk.reshape(2, BLOCK, -1)
        dv_s[pl.ds(first, 2)] += dv.reshape(2, BLOCK, -1)
        return carry

    lax.fori_loop(0, tiles, tile_step, 0)
    dq = jnp.zeros(query.shape, F32)
    for h in range(heads):
        part = t_s[h * BLOCK : (h + 1) * BLOCK, :]
        dq = dq + part * pre_ref[h : h + 1, :]
        dpre_ref[h] += jnp.sum((query * part).reshape(BLOCK // 8, 8, -1), axis=0)
    dq_ref[...] = dq.astype(BF16)

    @pl.when(step == pl.num_programs(0) - 1)
    def _():
        for k in range(dk_ref.shape[0]):
            dk_ref[k] = dk_s[k + 1].astype(BF16)
            dv_ref[k] = dv_s[k + 1].astype(BF16)


def attend_back(query, grad, u, lse, k_all, v_all, segs, pre, post):
    heads, width = pre.shape
    rows, stack = query.shape[0], heads * BLOCK
    blocks = rows // BLOCK
    groups = 4
    by_block = pl.BlockSpec((BLOCK, width), lambda i: (i, 0))
    return pl.pallas_call(
        functools.partial(backward_kernel, heads, groups),
        grid=(blocks,),
        in_specs=[
            by_block,
            by_block,
            pl.BlockSpec((1, heads, BLOCK, width), lambda i: (i, 0, 0, 0)),
            pl.BlockSpec((1, stack, BLOCK), lambda i: (i, 0, 0)),
            ANY, ANY, SCALARS, whole((2 * blocks, 1, BLOCK)), whole(pre.shape), whole(post.shape),
        ],
        out_specs=[
            by_block,
            whole((2 * blocks, BLOCK, width)),
            whole((2 * blocks, BLOCK, width)),
            whole((heads, 8, width)),
            whole((heads, 8, width)),
        ],
        scratch_shapes=[
            pltpu.VMEM((2 * blocks + 1, BLOCK, width), BF16),
            pltpu.VMEM((2 * blocks + 1, BLOCK, width), BF16),
            pltpu.VMEM((2 * blocks + 1, 1, BLOCK), jnp.int32),
            pltpu.VMEM((2 * blocks + 1, BLOCK, width), F32),
            pltpu.VMEM((2 * blocks + 1, BLOCK, width), F32),
            pltpu.VMEM((stack, width), BF16),
            pltpu.VMEM((stack, width), BF16),
            pltpu.VMEM((stack, BLOCK), F32),
            pltpu.VMEM((stack, width), F32),
            pltpu.SemaphoreType.DMA((2,)),
        ],
        out_shape=[
            jax.ShapeDtypeStruct((rows, width), BF16),
            jax.ShapeDtypeStruct((2 * blocks, BLOCK, width), BF16),
            jax.ShapeDtypeStruct((2 * blocks, BLOCK, width), BF16),
            jax.ShapeDtypeStruct((heads, 8, width), F32),
            jax.ShapeDtypeStruct((heads, 8, width), F32),
        ],
        compiler_params=pltpu.CompilerParams(vmem_limit_bytes=62 << 20),
        cost_estimate=cost(10 * rows * 1024 * stack // BLOCK * width, 4 * rows * stack // BLOCK * width),
        name="attend_back",
    )(query, grad, u, lse, k_all, v_all, segs, segs[:, None, :], pre, post)


MESH = pl.DeviceIdType.MESH


def flip(index, bit):
    return index + bit - 2 * bit * ((index // bit) % 2)


def greet(nd, nt, d, t):
    barrier = pltpu.get_barrier_semaphore()
    core = d % 2
    partners = [(d, lax.rem(t + s, nt)) for s in range(1, nt)]
    partners += [(flip(d, 1), lax.rem(t + s, nt)) for s in range(nt)]
    bit = 2
    while bit < nd:
        partners.append((flip(d, bit), t))
        bit *= 2
    for partner in partners:
        pl.semaphore_signal(barrier, inc=1, device_id=partner, device_id_type=MESH)
    pl.semaphore_wait(barrier, len(partners))


def remote(src, dst, send_sem, recv_sem, to):
    return pltpu.make_async_remote_copy(
        src_ref=src, dst_ref=dst, send_sem=send_sem, recv_sem=recv_sem, device_id=to, device_id_type=MESH
    )


def start_kernel(
    nd, nt, share, halves, *refs,
):
    if halves:
        tokens, segments, bundle, later = refs[:4]
        x_out, q_out, k_out, v_out, seg_out, w_out, gain_out, later_out = refs[4:12]
        wg_s, w_send, w_recv, w_self = refs[12:16]
    else:
        tokens, segments, w_out, gain_out, later = refs[:5]
        x_out, q_out, k_out, v_out, seg_out, later_out = refs[5:11]
    (l_send, l_recv, l_self, x_s, kv_s, x_send, x_recv, x_self, kv_send, kv_recv, kv_self, seg_send, seg_recv, seg_self) = refs[-14:]
    d, t = lax.axis_index("dp"), lax.axis_index("tensor")
    core = d % 2
    width = x_out.shape[1]
    micro = tokens.shape[0]
    per = tokens.shape[1]
    greet(nd, nt, d, t)

    if halves:
        own = pltpu.make_async_copy(bundle, wg_s.at[d, t], w_self)
        own.start()
        z_copies = []
        for s in range(1, nt):
            copy = remote(bundle, wg_s.at[d, t], w_send.at[0, 0, s], w_recv.at[0, 0, s], (d, lax.rem(t + s, nt)))
            copy.start()
            z_copies.append(copy)
        own.wait()
        for copy in z_copies:
            copy.wait()

    sends = []
    for m in range(micro):
        for c in range(2):
            to = (d - core + c, 2 * m + core)
            here = (to[0] == d) & (to[1] == t)
            src, dst = tokens.at[m, :, c], x_s.at[pl.ds(per * t, per)]
            far = remote(src, dst, x_send.at[2 * m + c], x_recv.at[t], to)
            near = pltpu.make_async_copy(src, dst, x_self)
            pl.when(jnp.logical_not(here))(far.start)
            pl.when(here)(near.start)
            sends.append((here, far, near))

    holder = t % 2 == core
    seg_here = pltpu.make_async_copy(segments.at[t // 2], seg_out, seg_self)
    seg_there = remote(segments.at[t // 2], seg_out, seg_send, seg_recv, (flip(d, 1), t))

    @pl.when(holder)
    def _():
        seg_here.start()
        seg_there.start()

    l_copies = [pltpu.make_async_copy(later, later_out.at[t], l_self)]
    for s in range(1, nt):
        l_copies.append(remote(later, later_out.at[t], l_send.at[s], l_recv.at[s], (d, lax.rem(t + s, nt))))
    for copy in l_copies:
        copy.start()

    if halves:
        bits = [1 << k for k in range(1, nd.bit_length() - 1)]
        routes = [bits + [1], bits[::-1] + [1]]
        have = [[0] for _ in halves]
        for stage in range(len(bits) + 1):
            copies = []
            for h, (lo, hi) in enumerate(halves):
                bit = routes[h][stage]
                for k, mask in enumerate(have[h]):
                    slab = d
                    for b in [1 << j for j in range(nd.bit_length() - 1)]:
                        if mask & b:
                            slab = flip(slab, b)
                    ref = wg_s.at[slab, :, pl.ds(lo, hi - lo)]
                    copies.append(
                        remote(ref, ref, w_send.at[1 + h, stage, k], w_recv.at[1 + h, stage, k], (flip(d, bit), t))
                    )
                have[h] = have[h] + [mask | bit for mask in have[h]]
            for copy in copies:
                copy.start()
            for copy in copies:
                copy.wait()

        gains = jnp.zeros((8, width), F32)
        for pair in range(nd * nt // 2):
            slabs = [wg_s[(2 * pair + e) // nt, (2 * pair + e) % nt].astype(F32) for e in range(2)]
            for k in range(3):
                both = jnp.concatenate([slab[k * share : (k + 1) * share] for slab in slabs])
                w_out[2 * pair * share : 2 * (pair + 1) * share, k * width : (k + 1) * width] = both.astype(BF16)
            gains = gains + (slabs[0] + slabs[1])[3 * share : 3 * share + 8]
        gain_out[...] = gains

    kv_copies = []
    gain = gain_out[:1]
    for s in range(nt):
        source = lax.rem(t + s, nt)
        here = (source == t) & holder
        arrival = remote(
            x_s.at[pl.ds(per * source, per)], x_s.at[pl.ds(per * source, per)], x_send.at[0], x_recv.at[source], (flip(d, 1), t)
        )
        local = pltpu.make_async_copy(tokens.at[0, :, 0], x_s.at[pl.ds(per * source, per)], x_self)
        pl.when(jnp.logical_not(here))(arrival.wait_recv)
        pl.when(here)(local.wait)
        x = x_s[pl.ds(per * source, per)].reshape(per * BLOCK, width)
        rows = pl.ds(pl.multiple_of(source * per * BLOCK, per * BLOCK), per * BLOCK)
        x_out[rows, :] = x
        x = x.astype(F32)
        h = (x * rms_scale(x) * gain).astype(BF16)
        q_out[rows, :] = matmul(h, w_out[:, :width]).astype(BF16)
        for k, out in enumerate((k_out, v_out)):
            value = matmul(h, w_out[:, (k + 1) * width : (k + 2) * width]).astype(BF16)
            kv_s[k, s] = value.reshape(per, BLOCK, width)
            dst = out.at[pl.ds(per * source, per), core]
            near = pltpu.make_async_copy(kv_s.at[k, s], dst, kv_self.at[k, s])
            far = remote(kv_s.at[k, s], dst, kv_send.at[k, s], kv_recv.at[k, s], (flip(d, 1), t))
            near.start()
            far.start()
            kv_copies += [near, far]
    for copy in kv_copies + l_copies:
        copy.wait()
    for here, far, near in sends:
        pl.when(jnp.logical_not(here))(far.wait_send)

    @pl.when(holder)
    def _():
        seg_here.wait()
        seg_there.wait_send()

    @pl.when(jnp.logical_not(holder))
    def _():
        seg_there.wait_recv()


def start(tokens, segments, bundle, later, share):
    micro, _, rows, width = tokens.shape
    nd, nt = lax.axis_size("dp"), lax.axis_size("tensor")
    count = rows * nt // 2
    blocks = count // BLOCK
    per = blocks // nt
    length = bundle.shape[0]
    dma = pltpu.SemaphoreType.DMA
    vmem = pl.BlockSpec(memory_space=pltpu.VMEM)
    shaped = jax.ShapeDtypeStruct
    most = max(nd // 2, nt)
    inside = 2 * share % 16 == 0 and length >= 32
    middle = length // 32 * 16
    if inside:
        halves, given = [(0, middle), (middle, length)], [bundle]
        gathered_specs = [vmem, vmem]
        gathered = [shaped((width, 3 * width), BF16), shaped((8, width), F32)]
        scratch = [
            pltpu.VMEM((nd, nt, length, width), BF16),
            dma((3, nd.bit_length(), most)), dma((3, nd.bit_length(), most)), dma,
        ]
    else:
        slabs = lax.all_gather(bundle, AXES, axis=0, tiled=False)
        w_qkv = slabs[:, : 3 * share].reshape(nd * nt, 3, share, width).transpose(0, 2, 1, 3)
        w_qkv = w_qkv.reshape(width, 3 * width)
        gains = jnp.sum(slabs[:, 3 * share : 3 * share + 8].astype(F32), axis=0)
        halves, given, gathered_specs, gathered, scratch = [], [w_qkv, gains], [], [], []
    results = pl.pallas_call(
        functools.partial(start_kernel, nd, nt, share, halves),
        in_specs=[ANY, ANY] + ([ANY] if inside else [vmem, vmem]) + [ANY],
        out_specs=[vmem, vmem, ANY, ANY, ANY] + gathered_specs + [ANY],
        out_shape=[
            shaped((count, width), BF16),
            shaped((count, width), BF16),
            shaped((blocks, 2, BLOCK, width), BF16),
            shaped((blocks, 2, BLOCK, width), BF16),
            shaped((2 * blocks, BLOCK), jnp.int32),
            *gathered,
            shaped((nt,) + later.shape, BF16),
        ],
        scratch_shapes=scratch + [
            dma((nt,)), dma((nt,)), dma,
            pltpu.VMEM((blocks, BLOCK, width), BF16),
            pltpu.VMEM((2, nt, per, BLOCK, width), BF16),
            dma((nt,)), dma((nt,)), dma,
            dma((2, nt)), dma((2, nt)), dma((2, nt)),
            dma, dma, dma,
        ],
        compiler_params=pltpu.CompilerParams(
            collective_id=0, has_side_effects=True, vmem_limit_bytes=56 << 20
        ),
        name="start",
    )(
        tokens.reshape(micro, rows // TILE, 2, BLOCK, width),
        segments.reshape(micro, 2 * blocks, BLOCK),
        *given,
        later,
    )
    return results if inside else (*results[:5], w_qkv, gains, results[5])


def gelu_parts(v):
    t = 1.0 / (1.0 + 0.23164189 * jnp.abs(v))
    bell = jnp.exp(-0.5 * v * v)
    series = t * (0.127414796 + t * (-0.142248368 + t * (0.7107068705 + t * (-0.7265760135 + t * 0.5307027145))))
    tail = series * bell
    return jnp.where(v < 0.0, tail, 1.0 - tail), 0.3989422804 * bell


def middle_kernel(
    rb, nt, *refs,
):
    x_ref, att_ref, w_out, gain_ref, up_ref, down_ref = refs[:6]
    dys, refs = refs[6 : 6 + nt], refs[6 + nt :]
    outs, refs = refs[:nt], refs[nt:]
    after_ref, datt_ref, dwo_ref, dgain_ref, grads_ref = refs[:5]
    dy_ref, a_s, h_s, ht_s, dyt_s, o_s, dh_s, hid_s, dhid_s, sems = refs[5:]
    step = pl.program_id(0)
    count, width = x_ref.shape
    parts = range(0, count, rb)

    @pl.when(step == 0)
    def _():
        copies = []
        for turn, dy in enumerate(dys):
            rows = pl.ds(pl.multiple_of(seat(turn)[1] * (count // nt), count // nt), count // nt)
            copies.append(pltpu.make_async_copy(dy, dy_ref.at[rows], sems.at[turn]))
        for copy in copies:
            copy.start()
        for copy in copies:
            copy.wait()
        for r in parts:
            rows = slice(r, r + rb)
            after = x_ref[rows, :].astype(F32) + matmul(att_ref[rows, :], w_out[...])
            a_s[rows, :] = after
            o_s[rows, :] = after
            h = (after * rms_scale(after) * gain_ref[...]).astype(BF16)
            h_s[rows, :] = h
            ht_s[:, rows] = h.T
            dyt_s[:, rows] = dy_ref[rows, :].T
            dh_s[rows, :] = jnp.zeros((rb, width), F32)

    up = up_ref[:, 0, 0].reshape(width, -1)
    down = down_ref[:, 0, 0].reshape(width, -1)
    for r in parts:
        rows = slice(r, r + rb)
        v = matmul(h_s[rows, :], up)
        cumulative, density = gelu_parts(v)
        hidden = (v * cumulative).astype(BF16)
        hid_s[rows, :] = hidden
        o_s[rows, :] += right_t(hidden, down)
        d_hidden = (matmul(dy_ref[rows, :], down) * (cumulative + v * density)).astype(BF16)
        dhid_s[rows, :] = d_hidden
        dh_s[rows, :] += right_t(d_hidden, up)
    share = grads_ref.shape[3]
    for r in range(0, width, 2 * share):
        rows = slice(r, r + 2 * share)
        k = r // share
        grads_ref[k : k + 2, 0, 0] = matmul(ht_s[rows, :], dhid_s[...]).astype(BF16).reshape(2, share, -1)
        grads_ref[k : k + 2, 0, 1] = matmul(dyt_s[rows, :], hid_s[...]).astype(BF16).reshape(2, share, -1)

    @pl.when(step == pl.num_programs(0) - 1)
    def _():
        gain = gain_ref[...]
        total = jnp.zeros((8, width), F32)
        for r in parts:
            rows = slice(r, r + rb)
            after = a_s[rows, :]
            scale = rms_scale(after)
            normed = after * scale
            dh = dh_s[rows, :]
            total = total + jnp.sum((dh * normed).reshape(rb // 8, 8, width), axis=0)
            d_after = dy_ref[rows, :].astype(F32) + rms_back(dh, normed, scale, gain)
            after_ref[rows, :] = d_after
            branch = d_after.astype(BF16)
            hid_s[rows, :] = branch
            datt_ref[rows, :] = right_t(branch, w_out[...]).astype(BF16)
        for turn, out in enumerate(outs):
            rows = pl.ds(pl.multiple_of(seat(turn)[1] * (count // nt), count // nt), count // nt)
            out[...] = o_s[rows, :].astype(BF16)
        dgain_ref[...] = total
        dwo_ref[...] = left_t(att_ref[...], hid_s[...]).astype(BF16)


def feed_forward(x, attended, dys, w_out, gain, both):
    count, width = x.shape
    nd, nt, _, share, units = both.shape
    rb = 256
    rows, part = whole((count, width)), whole((count // nt, width))
    return pl.pallas_call(
        functools.partial(middle_kernel, rb, nt),
        grid=(nt,),
        in_specs=[
            rows, rows, whole((width, width)), whole((1, width)),
            pl.BlockSpec((nd, 1, 1, share, units), lambda t: (0, t, 0, 0, 0)),
            pl.BlockSpec((nd, 1, 1, share, units), lambda t: (0, t, 1, 0, 0)),
        ] + [ANY] * nt,
        out_specs=[part] * nt + [
            rows, rows, whole((width, width)), whole((8, width)),
            pl.BlockSpec((nd, 1, 2, share, units), lambda t: (0, t, 0, 0, 0)),
        ],
        out_shape=[jax.ShapeDtypeStruct((count // nt, width), BF16)] * nt + [
            jax.ShapeDtypeStruct((count, width), F32),
            jax.ShapeDtypeStruct((count, width), BF16),
            jax.ShapeDtypeStruct((width, width), BF16),
            jax.ShapeDtypeStruct((8, width), F32),
            jax.ShapeDtypeStruct(both.shape, BF16),
        ],
        scratch_shapes=[
            pltpu.VMEM((count, width), BF16),
            pltpu.VMEM((count, width), F32),
            pltpu.VMEM((count, width), BF16),
            pltpu.VMEM((width, count), BF16),
            pltpu.VMEM((width, count), BF16),
            pltpu.VMEM((count, width), F32),
            pltpu.VMEM((count, width), F32),
            pltpu.VMEM((count, units), BF16),
            pltpu.VMEM((count, units), BF16),
            pltpu.SemaphoreType.DMA((nt,)),
        ],
        compiler_params=pltpu.CompilerParams(vmem_limit_bytes=62 << 20),
        cost_estimate=cost(12 * count * width * nt * units, 4 * nd * nt * share * units),
        name="feed_forward",
    )(x, attended, w_out, gain, both, both, *dys)


def masks_of(bits):
    masks = [0]
    for bit in bits:
        masks = masks + [mask | bit for mask in masks]
    return masks


def flips(index, mask):
    bit = 1
    while bit <= mask:
        if mask & bit:
            index = flip(index, bit)
        bit *= 2
    return index


def finish_kernel(
    nd, nt, share, inside, x_ref, dq_ref, dk_all, dv_all, after_ref, w_ref, gain_ref, dwo_ref, small_ref, *refs,
):
    if inside:
        tok_out, owned_out, small_out = refs[:3]
    else:
        tok_out, dw_out, small_out = refs[:3]
    (own_s, other_s, grads_s, ht_s, tok_s, own_sems, kv_send, kv_recv, tok_send, tok_recv, tok_self) = refs[3:14]
    d, t = lax.axis_index("dp"), lax.axis_index("tensor")
    core = d % 2
    count, width = x_ref.shape
    per = tok_out.shape[1]
    rows_in = per * BLOCK
    holder = t % 2 == core
    greet(nd, nt, d, t)

    order = [lax.rem(t + s, nt) for s in list(range(1, nt)) + [0]]
    own = [pltpu.make_async_copy(a.at[:, core], own_s.at[k], own_sems.at[k]) for k, a in enumerate((dk_all, dv_all))]
    for copy in own:
        copy.start()
    exchanged = []
    for s, source in enumerate(order):
        pair = []
        for k, a in enumerate((dk_all, dv_all)):
            pair.append(
                remote(
                    a.at[pl.ds(per * source, per), 1 - core], other_s.at[k, pl.ds(per * source, per)],
                    kv_send.at[k, s], kv_recv.at[k, s], (flip(d, 1), t),
                )
            )
            pair[-1].start()
        exchanged.append(pair)
    gain = gain_ref[:1]

    def norms(rows):
        x = x_ref[rows, :].astype(F32)
        scale = rms_scale(x)
        return x * scale, scale

    for r in range(0, count, rows_in):
        rows = slice(r, r + rows_in)
        normed, scale = norms(rows)
        ht_s[:, rows] = (normed * gain).astype(BF16).T
        grads_s[rows, :width] = dq_ref[rows, :]
    for copy in own:
        copy.wait()

    d_gain = jnp.zeros((8, width), F32)
    sends = []
    to_core = d - core + t % 2
    for s, source in enumerate(order):
        for copy in exchanged[s]:
            copy.wait()
        rows = pl.ds(pl.multiple_of(source * rows_in, rows_in), rows_in)
        for k in range(2):
            total = own_s[k, pl.ds(per * source, per)].astype(F32) + other_s[k, pl.ds(per * source, per)].astype(F32)
            grads_s[rows, (k + 1) * width : (k + 2) * width] = total.reshape(rows_in, width).astype(BF16)
        dh = right_t(grads_s[rows, :], w_ref[...])
        normed, scale = norms(rows)
        d_gain = d_gain + jnp.sum((dh * normed).reshape(rows_in // 8, 8, width), axis=0)
        tok = after_ref[rows, :] + rms_back(dh, normed, scale, gain)
        tok_s[s] = tok.astype(BF16).reshape(per, BLOCK, width)
        here = (source == t) & holder
        dst = tok_out.at[t // 2, :, core]
        far = remote(tok_s.at[s], dst, tok_send.at[s], tok_recv.at[2 * (t // 2) + core], (to_core, source))
        near = pltpu.make_async_copy(tok_s.at[s], dst, tok_self)
        pl.when(jnp.logical_not(here))(far.start)
        pl.when(here)(near.start)
        sends.append((here, far, near))

    small = small_ref[...]
    line = lax.broadcasted_iota(jnp.int32, small.shape, 0)
    small = small + jnp.where(line == 0, jnp.sum(d_gain, axis=0, keepdims=True), 0.0)
    rows_at = min(width, 8 * share if inside else 256)
    if inside:
        slab_s, core_s, plane_s, z_s, sm_s, sm_in, g_send, g_recv, s_send, s_recv = refs[14:]
    for r in range(0, width, rows_at):
        dw = matmul(ht_s[r : r + rows_at, :], grads_s[...])
        if not inside:
            dw_out[r : r + rows_at, : 3 * width] = dw.astype(BF16)
            dw_out[r : r + rows_at, 3 * width :] = dwo_ref[r : r + rows_at, :]
            continue
        dwo = dwo_ref[r : r + rows_at, :].astype(F32)
        for k in range(rows_at // share):
            lines = slice(k * share, (k + 1) * share)
            parts = [dw[lines, m * width : (m + 1) * width] for m in range(3)] + [dwo[lines]]
            slab = r // share + k
            slab_s[slab // nt, slab % nt] = jnp.concatenate(parts).astype(BF16)
    if not inside:
        small_out[...] = small
    else:
        length = slab_s.shape[2]
        middle = length // 32 * 16
        halves = [(0, middle), (middle, length)]
        bits = [1 << k for k in range(1, nd.bit_length() - 1)]
        routes = [[1] + bits, [1] + bits[::-1]]
        left = [bits + [1], bits + [1]]
        sm_s[...] = small
        for stage in range(len(bits) + 1):
            copies, adds = [], []
            for h, (lo, hi) in enumerate(halves):
                bit = routes[h][stage]
                left[h] = [b for b in left[h] if b != bit]
                for k, mask in enumerate(masks_of(left[h])):
                    away, mine = flips(flip(d, bit), mask), flips(d, mask)
                    buffer = core_s if stage == 0 else plane_s.at[stage - 1]
                    there = buffer.at[k, :, pl.ds(lo, hi - lo)]
                    copies.append(
                        remote(
                            slab_s.at[away, :, pl.ds(lo, hi - lo)], there,
                            g_send.at[h, stage, k], g_recv.at[h, stage, k], (flip(d, bit), t),
                        )
                    )
                    adds.append((mine, lo, hi, buffer, k))
            bit = routes[0][stage]
            tiny = remote(sm_s, sm_in.at[stage], s_send.at[stage], s_recv.at[stage], (flip(d, bit), t))
            for copy in copies + [tiny]:
                copy.start()
            for copy in copies + [tiny]:
                copy.wait()
            for mine, lo, hi, buffer, k in adds:
                both = slab_s[mine, :, lo:hi].astype(F32) + buffer[k, :, lo:hi].astype(F32)
                slab_s[mine, :, lo:hi] = both.astype(BF16)
            sm_s[...] += sm_in[stage]
        copies = []
        for s in range(1, nt):
            to = lax.rem(t + s, nt)
            copies.append(remote(slab_s.at[d, to], z_s.at[s], g_send.at[2, 0, s], g_recv.at[2, 0, s], (d, to)))
            copies.append(
                remote(sm_s, sm_in.at[len(bits) + s], s_send.at[len(bits) + s], s_recv.at[len(bits) + s], (d, to))
            )
        for copy in copies:
            copy.start()
        for copy in copies:
            copy.wait()
        total = slab_s[d, t].astype(F32)
        for s in range(1, nt):
            total = total + z_s[s].astype(F32)
        owned_out[...] = total
        small_out[...] = sm_s[...] + sum(sm_in[len(bits) + s] for s in range(1, nt))

    for here, far, near in sends:
        pl.when(jnp.logical_not(here))(far.wait_send)
        pl.when(here)(near.wait)
    for m in range(tok_out.shape[0]):
        for c in range(2):
            here = (2 * m + core == t) & (c == core)
            dst = tok_out.at[m, :, c]
            back = remote(dst, dst, tok_send.at[0], tok_recv.at[2 * m + c], (flip(d, 1), t))
            pl.when(jnp.logical_not(here))(back.wait_recv)


def finish(x, dq, dk_all, dv_all, after, w_qkv, gains, dwo, small, share, micro):
    count, width = x.shape
    nd, nt = lax.axis_size("dp"), lax.axis_size("tensor")
    inside = 2 * share % 16 == 0
    blocks = count // BLOCK
    per = blocks // nt
    dma = pltpu.SemaphoreType.DMA
    vmem = pl.BlockSpec(memory_space=pltpu.VMEM)
    shaped = jax.ShapeDtypeStruct
    scratch = [
        pltpu.VMEM((2, blocks, BLOCK, width), BF16),
        pltpu.VMEM((2, blocks, BLOCK, width), BF16),
        pltpu.VMEM((count, 3 * width), BF16),
        pltpu.VMEM((width, count), BF16),
        pltpu.VMEM((nt, per, BLOCK, width), BF16),
        dma((2,)), dma((2, nt)), dma((2, nt)), dma((nt,)), dma((nt,)), dma,
    ]
    if inside:
        most = max(nd // 2, nt)
        stages = nd.bit_length() - 1
        scratch += [
            pltpu.VMEM((nd, nt, 4 * share, width), BF16),
            pltpu.VMEM((nd // 2, nt, 4 * share, width), BF16),
            pltpu.VMEM((stages - 1, nd // 4, nt, 4 * share, width), BF16),
            pltpu.VMEM((nt, 4 * share, width), BF16),
            pltpu.VMEM(small.shape, F32),
            pltpu.VMEM((stages + nt,) + small.shape, F32),
            dma((3, stages, most)), dma((3, stages, most)), dma((stages + nt,)), dma((stages + nt,)),
        ]
    return pl.pallas_call(
        functools.partial(finish_kernel, nd, nt, share, inside),
        in_specs=[vmem, vmem, ANY, ANY, vmem, vmem, vmem, vmem, vmem],
        out_specs=[vmem, vmem, vmem],
        out_shape=[
            shaped((micro, per, 2, BLOCK, width), BF16),
            shaped((4 * share, width), F32) if inside else shaped((width, 4 * width), BF16),
            shaped(small.shape, F32),
        ],
        scratch_shapes=scratch,
        compiler_params=pltpu.CompilerParams(
            collective_id=1, has_side_effects=True, vmem_limit_bytes=60 << 20
        ),
        cost_estimate=cost(24 * count * width * width, 16 * count * width),
        name="finish",
    )(x, dq, dk_all, dv_all, after, w_qkv, gains, dwo, small)


def per_device(
    tokens, segments, w_query, w_key, w_value, w_out, norm_attn, norm_ffn, pre_mix, post_mix, w_up, w_down, out_grad,
):
    micro, _, rows, width = tokens.shape
    nd, nt = lax.axis_size("dp"), lax.axis_size("tensor")
    heads = pre_mix.shape[0]
    head_width = width // heads
    length = rows * nt
    count = length // 2
    blocks = count // BLOCK
    share = w_query.shape[0]
    bits = [1 << k for k in range(nd.bit_length() - 1)]
    d, t = lax.axis_index("dp"), lax.axis_index("tensor")
    core = d % 2

    place = (d * nt + t) * share
    gains = lax.dynamic_update_slice(jnp.zeros((8, width), BF16), jnp.stack([norm_attn, norm_ffn]), (0, place))
    fill = jnp.zeros((-(3 * share + 8) % 16, width), BF16)
    bundle = jnp.concatenate([w_query, w_key, w_value, gains, fill])
    units = 2 * w_up.shape[0]
    fill = jnp.zeros((-(units + share) % 16, width), BF16)
    later = jnp.concatenate([w_up, w_down, w_out, fill])
    x, query, k_all, v_all, segs, w_qkv, gains, later = start(tokens, segments, bundle, later, share)
    k_all, v_all = (a.reshape(2 * blocks, BLOCK, width) for a in (k_all, v_all))
    x, out_grad = lax.optimization_barrier((x, out_grad))
    grad_turns = to_sequences(out_grad)
    gathered = lax.all_gather(later, "dp", axis=0, tiled=False)
    all_out = gathered[:, :, units : units + share].reshape(width, width)
    both = gathered[:, :, :units].reshape((nd, nt, 2) + w_up.shape)

    def by_lane(mix):
        return jnp.repeat(mix.astype(F32), head_width, axis=1)

    pre = by_lane(pre_mix.T) * head_width ** (-0.5)
    post = by_lane(post_mix)

    attended, u, lse = attend(query, k_all, v_all, segs, pre, post)
    *out_turns, grad_after, grad_attended, grad_w_out, grad_gain_ffn, grad_both = feed_forward(
        x, attended, grad_turns, all_out, gains[1:2], both
    )
    grad_gain_ffn = jnp.sum(grad_gain_ffn, axis=0)
    out = from_sequences(out_turns, micro)
    part_both = lax.psum_scatter(
        grad_both.reshape((nd * nt,) + grad_both.shape[2:]), AXES, scatter_dimension=0, tiled=False
    ).astype(F32)

    grad_query, grad_key, grad_value, d_pre, d_post = attend_back(
        query, grad_attended, u, lse, k_all, v_all, segs, pre, post
    )

    def spread(d_mix):
        total = d_mix.reshape(heads, 8, heads, head_width).sum((1, 3)).reshape(-1)
        return jnp.pad(total, (0, width - total.shape[0]))

    small = jnp.zeros((8, width), F32).at[1].set(grad_gain_ffn)
    small = small.at[2].set(spread(d_pre)).at[3].set(spread(d_post))
    x, out = lax.optimization_barrier((x, out))
    d_tokens, owned, small = finish(
        x, grad_query, grad_key.reshape(blocks, 2, BLOCK, width), grad_value.reshape(blocks, 2, BLOCK, width),
        grad_after, w_qkv, gains, grad_w_out, small, share, micro,
    )
    d_tokens = d_tokens.reshape(tokens.shape).astype(F32)
    if owned.dtype == BF16:
        owned = lax.psum_scatter(owned, AXES, scatter_dimension=0, tiled=True).astype(F32)
        owned = [owned[:, k * width : (k + 1) * width] for k in range(4)]
        small = lax.psum(small, AXES)
    else:
        owned = [owned[k * share : (k + 1) * share] for k in range(4)]
    gain_grads = lax.dynamic_slice_in_dim(small, place, share, 1)
    pairs = heads * heads
    return (
        out,
        d_tokens,
        owned[0],
        owned[1],
        owned[2],
        owned[3],
        gain_grads[0],
        gain_grads[1],
        small[2, :pairs].reshape(heads, heads).T * head_width ** (-0.5),
        small[3, :pairs].reshape(heads, heads),
        part_both[0],
        part_both[1],
    )


def solution(mesh):
    both = P(("dp", "tensor"), None)
    gain = P(("dp", "tensor"))
    data = P(None, "dp", "tensor", None)
    ffn = P("dp", "tensor")
    return jax.shard_map(
        per_device,
        mesh=mesh,
        in_specs=(data, P(None, "dp", None), both, both, both, both, gain, gain, P(), P(), ffn, ffn, data),
        out_specs=(data, data, both, both, both, both, gain, gain, P(), P(), ffn, ffn),
        check_vma=False,
    )
```

```python
import functools

import jax
import jax.numpy as jnp
from jax import lax
from jax.experimental import pallas as pl
from jax.experimental.pallas import tpu as pltpu
from jax.sharding import PartitionSpec as P

F32 = jnp.float32
BF16 = jnp.bfloat16
BLOCK = 128
TILE = 2 * BLOCK
FORWARD_GROUPS = 6
BACKWARD_GROUPS = 2
AXES = ("plane", "core", "tensor")


def matmul(left, right):
    return jnp.dot(left, right, preferred_element_type=F32)


def right_t(left, right):
    return lax.dot_general(left, right, (((1,), (1,)), ((), ())), preferred_element_type=F32)


def left_t(left, right):
    return lax.dot_general(left, right, (((0,), (0,)), ((), ())), preferred_element_type=F32)


def rms_scale(values):
    return lax.rsqrt(jnp.mean(values * values, axis=-1, keepdims=True) + 1e-06)


def rms_back(grad_norm, normed, scale, gain):
    scaled = grad_norm * gain
    return scale * (scaled - normed * jnp.mean(scaled * normed, axis=-1, keepdims=True))


def gelu_exact(values):
    return jax.nn.gelu(values, approximate=False)


def gelu_back(upper, grad):
    unused, pull = jax.vjp(gelu_exact, upper)
    return pull(grad)[0]


def send(x, to):
    nd, nt = 2 * lax.axis_size("plane"), lax.axis_size("tensor")
    pairs = []
    for d in range(nd):
        for t in range(nt):
            d2, t2 = to(d, t)
            pairs.append((d * nt + t, d2 * nt + t2))
    return lax.ppermute(x, AXES, pairs)


def by_shift(shift):
    nt = lax.axis_size("tensor")
    return lambda d, t: (d, (t + shift) % nt)


def by_bit(bit):
    return lambda d, t: (d ^ bit, t)


def gather(piece, bits):
    nt = lax.axis_size("tensor")
    have = {0: jnp.stack([piece] + [send(piece, by_shift(s)) for s in range(1, nt)])}
    for bit in bits:
        have.update({mask | bit: send(block, by_bit(bit)) for mask, block in have.items()})
    return [have[mask] for mask in range(len(have))]


def pick(x, index, axis):
    return lax.dynamic_index_in_dim(x, index, axis, keepdims=False)


def sum_to_owner(x, bits):
    nt, nd = x.shape[:2]
    d, t = 2 * lax.axis_index("plane") + lax.axis_index("core"), lax.axis_index("tensor")
    rest = x.shape[2:]
    names = [1 << k for k in range(nd.bit_length() - 1)][::-1]
    x = x.reshape((nt,) + (2,) * len(names) + rest)
    for bit in bits:
        axis = 1 + names.index(bit)
        names.remove(bit)
        mine = (d // bit) % 2
        got = send(pick(x, 1 - mine, axis), by_bit(bit))
        x = pick(x, mine, axis).astype(F32) + got.astype(F32)
        if names or nt > 1:
            x = x.astype(BF16)
    total = pick(x, t, 0).astype(F32)
    for shift in range(1, nt):
        total = total + send(pick(x, lax.rem(t + shift, nt), 0), by_shift(shift)).astype(F32)
    return total


def seat(turn):
    nt = lax.axis_size("tensor")
    t, core = lax.axis_index("tensor"), lax.axis_index("core")
    block = lax.rem(turn + t, nt)
    source = lax.rem(2 * (t // 2) + core + nt - turn, nt)
    return block, source


def turn_to(turn):
    nt = lax.axis_size("tensor")

    def to(d, t):
        block = (turn + t) % nt
        return d - d % 2 + block % 2, 2 * (block // 2) + d % 2

    return to


def turn_back(turn):
    nt = lax.axis_size("tensor")

    def to(d, t):
        return d - d % 2 + t % 2, (2 * (t // 2) + d % 2 + nt - turn) % nt

    return to


def split_kernel(x_ref, *outs):
    for turn, out in enumerate(outs):
        block = seat(turn)[0]
        out[...] = x_ref[block // 2, :, block % 2].reshape(out.shape)


def join_kernel(*refs):
    out = refs[-1]
    for turn, piece in enumerate(refs[:-1]):
        block = seat(turn)[0]
        out[block // 2, :, block % 2] = piece[...].reshape(out.shape[1], BLOCK, out.shape[4])


def to_sequences(x):
    micro, _, rows, width = x.shape
    nt = lax.axis_size("tensor")
    pieces = pl.pallas_call(
        split_kernel, out_shape=[jax.ShapeDtypeStruct((rows // 2, width), x.dtype)] * nt, name="split"
    )(x.reshape(micro, rows // TILE, 2, BLOCK, width))
    return [send(piece, turn_to(turn)) for turn, piece in enumerate(pieces)]


def from_sequences(pieces, micro):
    half, width = pieces[0].shape
    back = [send(piece, turn_back(turn)) for turn, piece in enumerate(pieces)]
    out = pl.pallas_call(
        join_kernel,
        out_shape=jax.ShapeDtypeStruct((micro, half // BLOCK, 2, BLOCK, width), pieces[0].dtype),
        name="join",
    )(*back)
    return out.reshape(micro, 1, 2 * half, width)


def arrive(step, sources, scratches, sems, seg_ref, seg_s):
    blocks = sources[0].shape[0]
    copies = []
    for k, (source, scratch) in enumerate(zip(sources, scratches)):
        for part in range(blocks // 2):
            rows = pl.ds(2 * part, 2)
            there = scratch.at[pl.ds(2 * part + 1, 2)]
            copies.append((part, pltpu.make_async_copy(source.at[rows], there, sems.at[k, part])))

    @pl.when(step == 0)
    def _():
        for _, copy in copies:
            copy.start()
        seg_s[0] = jnp.full((1, BLOCK), -1, jnp.int32)
        seg_s[1:] = seg_ref[...]
        for scratch in scratches:
            scratch[0] = jnp.zeros(scratch.shape[1:], BF16)

    for part, copy in copies:
        pl.when(step == part)(copy.wait)


def reach(block, seg_low):
    first = seg_low[block, 0]
    before = 0
    for k in range(seg_low.shape[0]):
        before += (seg_low[k, BLOCK - 1] < first).astype(jnp.int32)
    return (block + 2 - before) // 2


def rows_of(block, seg_s):
    return jnp.broadcast_to(seg_s[block + 1], (BLOCK, BLOCK)).T


def row_mask(row_seg, first, block, seg_s):
    row = lax.broadcasted_iota(jnp.int32, (BLOCK, BLOCK), 0)
    col = lax.broadcasted_iota(jnp.int32, (BLOCK, BLOCK), 1)
    masks = []
    for k in range(2):
        ahead = (first + k - 1 - block) * BLOCK
        allowed = (row_seg == seg_s[first + k]) & (col + ahead <= row)
        masks.append(jnp.where(allowed, 0.0, -1e30).astype(F32))
    return jnp.concatenate(masks, axis=1)


def forward_kernel(
    heads, groups, most, q_ref, k_all, v_all, seg_low, seg_ref, pre_ref, post_ref,
    att_ref, u_ref, lse_ref, k_s, v_s, seg_s, qp_s, m_s, s_s, sems,
):
    step = pl.program_id(0)
    core = lax.axis_index("core")
    block = 2 * step + core
    width = q_ref.shape[1]
    arrive(step, [k_all, v_all], [k_s, v_s], sems, seg_ref, seg_s)
    tiles = reach(block, seg_low)
    row_seg = rows_of(block, seg_s)

    def scores(left, first, mask):
        keys = k_s[pl.ds(first, 2)].reshape(TILE, -1)
        s = right_t(left, keys).reshape(left.shape[0] // BLOCK, BLOCK, TILE)
        return (s + mask[None]).reshape(left.shape[0], TILE)

    def close(g, per, top, total, u, att):
        size = per * BLOCK
        lse_ref[0, g * size : (g + 1) * size, :] = jnp.broadcast_to(top + jnp.log(total), (size, BLOCK))
        for k in range(per):
            h = g * per + k
            part = u[k * BLOCK : (k + 1) * BLOCK]
            u_ref[0, h] = part.astype(BF16)
            att = att + part * post_ref[h : h + 1, :]
        return att

    @pl.when(tiles == 1)
    def _():
        per = heads // groups
        query = q_ref[...]
        mask = row_mask(row_seg, block, block, seg_s)
        att = jnp.zeros((BLOCK, width), F32)
        values = v_s[pl.ds(block, 2)].reshape(TILE, -1)
        for g in range(groups):
            left = jnp.concatenate([query * pre_ref[h : h + 1, :] for h in range(g * per, (g + 1) * per)])
            s = scores(left, block, mask)
            top = jnp.max(s, axis=-1, keepdims=True)
            p = jnp.exp(s - top)
            total = jnp.sum(p, axis=-1, keepdims=True)
            u = matmul((p * (1.0 / total)).astype(BF16), values)
            att = close(g, per, top, total, u, att)
        att_ref[...] = att.astype(BF16)

    @pl.when(tiles > 1)
    def _():
        query = q_ref[...]
        for h in range(heads):
            qp_s[h * BLOCK : (h + 1) * BLOCK, :] = query * pre_ref[h : h + 1, :]
        m_s[...] = jnp.full(m_s.shape, -3e38, F32)
        split = 2
        size = heads // split * BLOCK

        def meet(tile, carry):
            first = block - 2 * tile
            mask = row_mask(row_seg, first, block, seg_s)
            for g in range(split):
                rows = slice(g * size, (g + 1) * size)
                s = scores(qp_s[rows, :], first, mask)
                s_s[tile, rows, :] = s
                m_s[rows, :] = jnp.maximum(m_s[rows, :], jnp.maximum(s[:, :BLOCK], s[:, BLOCK:]))
            return carry

        lax.fori_loop(0, tiles, meet, 0)

    for n in range(2, most + 1):

        @pl.when(tiles == n)
        def _(n=n):
            per = heads // groups
            size = per * BLOCK
            values = v_s[pl.ds(block - 2 * n + 2, 2 * n)].reshape(n * TILE, -1)
            att = jnp.zeros((BLOCK, width), F32)
            for g in range(groups):
                rows = slice(g * size, (g + 1) * size)
                top = jnp.max(m_s[rows, :], axis=-1, keepdims=True)
                parts = [jnp.exp(s_s[tile, rows, :] - top) for tile in range(n)]
                total = jnp.sum(sum(p[:, :BLOCK] + p[:, BLOCK:] for p in parts), axis=-1, keepdims=True)
                p = jnp.concatenate([part.astype(BF16) for part in parts[::-1]], axis=1)
                u = matmul(p, values) * (1.0 / total)
                att = close(g, per, top, total, u, att)
            att_ref[...] = att.astype(BF16)


def whole(shape):
    return pl.BlockSpec(shape, lambda i: (0,) * len(shape), pipeline_mode=pl.Buffered(1))


def cost(flops, moved):
    return pl.CostEstimate(flops=int(flops), bytes_accessed=int(moved), transcendentals=0)


ANY = pl.BlockSpec(memory_space=pl.ANY)
SCALARS = pl.BlockSpec(memory_space=pltpu.SMEM)


def attend(query, k_all, v_all, segs, pre, post):
    heads, width = pre.shape
    rows, stack = query.shape[0], heads * BLOCK
    blocks = rows // BLOCK
    groups = FORWARD_GROUPS
    most = (1024 // BLOCK + 2) // 2
    by_block = pl.BlockSpec((BLOCK, width), lambda i: (i, 0))
    return pl.pallas_call(
        functools.partial(forward_kernel, heads, groups, most),
        grid=(blocks,),
        in_specs=[
            by_block, ANY, ANY, SCALARS, whole((2 * blocks, 1, BLOCK)), whole(pre.shape), whole(post.shape),
        ],
        out_specs=[
            by_block,
            pl.BlockSpec((1, heads, BLOCK, width), lambda i: (i, 0, 0, 0)),
            pl.BlockSpec((1, stack, BLOCK), lambda i: (i, 0, 0)),
        ],
        scratch_shapes=[
            pltpu.VMEM((2 * blocks + 1, BLOCK, width), BF16),
            pltpu.VMEM((2 * blocks + 1, BLOCK, width), BF16),
            pltpu.VMEM((2 * blocks + 1, 1, BLOCK), jnp.int32),
            pltpu.VMEM((stack, width), BF16),
            pltpu.VMEM((stack, BLOCK), F32),
            pltpu.VMEM((most, stack, TILE), F32),
            pltpu.SemaphoreType.DMA((2, blocks)),
        ],
        out_shape=[
            jax.ShapeDtypeStruct((rows, width), BF16),
            jax.ShapeDtypeStruct((blocks, heads, BLOCK, width), BF16),
            jax.ShapeDtypeStruct((blocks, stack, BLOCK), F32),
        ],
        compiler_params=pltpu.CompilerParams(vmem_limit_bytes=60 << 20),
        cost_estimate=cost(4 * rows * 1024 * stack // BLOCK * width, 4 * rows * stack // BLOCK * width),
        name="attend",
    )(query, k_all, v_all, segs, segs[:, None, :], pre, post)


def backward_kernel(
    heads, groups, q_ref, g_ref, u_ref, lse_ref, k_all, v_all, seg_low, seg_ref, pre_ref, post_ref,
    dq_ref, dk_ref, dv_ref, dpre_ref, dpost_ref,
    k_s, v_s, seg_s, dk_s, dv_s, qp_s, gp_s, d_s, t_s, sems,
):
    step = pl.program_id(0)
    core = lax.axis_index("core")
    block = 2 * step + core
    per = heads // groups
    size = per * BLOCK
    width = q_ref.shape[1]
    arrive(step, [k_all, v_all], [k_s, v_s], sems, seg_ref, seg_s)

    @pl.when(step == 0)
    def _():
        dk_s[...] = jnp.zeros(dk_s.shape, F32)
        dv_s[...] = jnp.zeros(dv_s.shape, F32)
        dpre_ref[...] = jnp.zeros(dpre_ref.shape, F32)
        dpost_ref[...] = jnp.zeros(dpost_ref.shape, F32)

    tiles = reach(block, seg_low)
    row_seg = rows_of(block, seg_s)

    def opening(g):
        query, grad_low = q_ref[...], g_ref[...]
        grad = grad_low.astype(F32)
        left, right, terms = [], [], []
        for h in range(g * per, (g + 1) * per):
            gain = post_ref[h : h + 1, :]
            left.append(query * pre_ref[h : h + 1, :])
            right.append(grad_low * gain.astype(BF16))
            both = grad * u_ref[0, h].astype(F32)
            terms.append(jnp.sum(both * gain, axis=-1, keepdims=True))
            dpost_ref[h] += jnp.sum(both.reshape(BLOCK // 8, 8, -1), axis=0)
        return jnp.concatenate(left), jnp.concatenate(right), jnp.concatenate(terms)

    def closing(h, part, dq):
        dpre_ref[h] += jnp.sum((q_ref[...].astype(F32) * part).reshape(BLOCK // 8, 8, -1), axis=0)
        return dq + part * pre_ref[h : h + 1, :].astype(F32)

    def tile_part(first, mask, g, left, right, term):
        keys = k_s[pl.ds(first, 2)].reshape(TILE, -1)
        values = v_s[pl.ds(first, 2)].reshape(TILE, -1)
        s = (right_t(left, keys).reshape(per, BLOCK, TILE) + mask[None]).reshape(size, TILE)
        top = lse_ref[0, g * size : (g + 1) * size, :]
        p = jnp.exp(s - jnp.concatenate([top, top], axis=1))
        dw = right_t(right, values)
        ds = (p * (dw - term)).astype(BF16)
        return matmul(ds, keys), left_t(ds, left), left_t(p.astype(BF16), right)

    def add_up(first, dk, dv):
        dk_s[pl.ds(first, 2)] += dk.reshape(2, BLOCK, -1)
        dv_s[pl.ds(first, 2)] += dv.reshape(2, BLOCK, -1)

    @pl.when(tiles == 1)
    def _():
        mask = row_mask(row_seg, block, block, seg_s)
        dk = dv = jnp.zeros((TILE, width), F32)
        dq = jnp.zeros((BLOCK, width), F32)
        for g in range(groups):
            part, a, b = tile_part(block, mask, g, *opening(g))
            dk, dv = dk + a, dv + b
            for k in range(per):
                dq = closing(g * per + k, part[k * BLOCK : (k + 1) * BLOCK], dq)
        add_up(block, dk, dv)
        dq_ref[...] = dq.astype(BF16)

    @pl.when(tiles > 1)
    def _():
        mask = row_mask(row_seg, block, block, seg_s)
        dk = dv = jnp.zeros((TILE, width), F32)
        for g in range(groups):
            rows = slice(g * size, (g + 1) * size)
            left, right, term = opening(g)
            qp_s[rows, :], gp_s[rows, :] = left, right
            d_s[rows, :] = jnp.broadcast_to(term, (size, BLOCK))
            t_s[rows, :], a, b = tile_part(block, mask, g, left, right, term)
            dk, dv = dk + a, dv + b
        add_up(block, dk, dv)

        def more(tile, carry):
            first = block - 2 * tile
            mask = row_mask(row_seg, first, block, seg_s)
            dk = dv = jnp.zeros((TILE, width), F32)
            for g in range(groups):
                rows = slice(g * size, (g + 1) * size)
                term = jnp.concatenate([d_s[rows, :]] * 2, axis=1)
                part, a, b = tile_part(first, mask, g, qp_s[rows, :], gp_s[rows, :], term)
                t_s[rows, :] += part
                dk, dv = dk + a, dv + b
            add_up(first, dk, dv)
            return carry

        lax.fori_loop(1, tiles, more, 0)
        dq = jnp.zeros((BLOCK, width), F32)
        for h in range(heads):
            dq = closing(h, t_s[h * BLOCK : (h + 1) * BLOCK, :], dq)
        dq_ref[...] = dq.astype(BF16)

    @pl.when(step == pl.num_programs(0) - 1)
    def _():
        for k in range(dk_ref.shape[0]):
            dk_ref[k] = dk_s[k + 1].astype(BF16)
            dv_ref[k] = dv_s[k + 1].astype(BF16)


def attend_back(query, grad, u, lse, k_all, v_all, segs, pre, post):
    heads, width = pre.shape
    rows, stack = query.shape[0], heads * BLOCK
    blocks = rows // BLOCK
    groups = BACKWARD_GROUPS
    by_block = pl.BlockSpec((BLOCK, width), lambda i: (i, 0))
    return pl.pallas_call(
        functools.partial(backward_kernel, heads, groups),
        grid=(blocks,),
        in_specs=[
            by_block,
            by_block,
            pl.BlockSpec((1, heads, BLOCK, width), lambda i: (i, 0, 0, 0)),
            pl.BlockSpec((1, stack, BLOCK), lambda i: (i, 0, 0)),
            ANY, ANY, SCALARS, whole((2 * blocks, 1, BLOCK)), whole(pre.shape), whole(post.shape),
        ],
        out_specs=[
            by_block,
            whole((2 * blocks, BLOCK, width)),
            whole((2 * blocks, BLOCK, width)),
            whole((heads, 8, width)),
            whole((heads, 8, width)),
        ],
        scratch_shapes=[
            pltpu.VMEM((2 * blocks + 1, BLOCK, width), BF16),
            pltpu.VMEM((2 * blocks + 1, BLOCK, width), BF16),
            pltpu.VMEM((2 * blocks + 1, 1, BLOCK), jnp.int32),
            pltpu.VMEM((2 * blocks + 1, BLOCK, width), F32),
            pltpu.VMEM((2 * blocks + 1, BLOCK, width), F32),
            pltpu.VMEM((stack, width), BF16),
            pltpu.VMEM((stack, width), BF16),
            pltpu.VMEM((stack, BLOCK), F32),
            pltpu.VMEM((stack, width), F32),
            pltpu.SemaphoreType.DMA((2, blocks)),
        ],
        out_shape=[
            jax.ShapeDtypeStruct((rows, width), BF16),
            jax.ShapeDtypeStruct((2 * blocks, BLOCK, width), BF16),
            jax.ShapeDtypeStruct((2 * blocks, BLOCK, width), BF16),
            jax.ShapeDtypeStruct((heads, 8, width), F32),
            jax.ShapeDtypeStruct((heads, 8, width), F32),
        ],
        compiler_params=pltpu.CompilerParams(vmem_limit_bytes=62 << 20),
        cost_estimate=cost(10 * rows * 1024 * stack // BLOCK * width, 4 * rows * stack // BLOCK * width),
        name="attend_back",
    )(query, grad, u, lse, k_all, v_all, segs, segs[:, None, :], pre, post)


MESH = pl.DeviceIdType.MESH


def device(place):
    d, t = place
    return d // 2, d % 2, t


def flip(index, bit):
    return index + bit - 2 * bit * ((index // bit) % 2)


def greet(nd, nt, d, t):
    barrier = pltpu.get_barrier_semaphore()
    core = d % 2
    partners = [(d, lax.rem(t + s, nt)) for s in range(1, nt)]
    partners += [(flip(d, 1), lax.rem(t + s, nt)) for s in range(nt)]
    bit = 2
    while bit < nd:
        partners.append((flip(d, bit), t))
        bit *= 2
    for partner in partners:
        pl.semaphore_signal(barrier, inc=1, device_id=device(partner), device_id_type=MESH)
    pl.semaphore_wait(barrier, len(partners))


def remote(src, dst, send_sem, recv_sem, to):
    return pltpu.make_async_remote_copy(
        src_ref=src, dst_ref=dst, send_sem=send_sem, recv_sem=recv_sem, device_id=device(to), device_id_type=MESH
    )


def start_kernel(
    nd, nt, share, halves, *refs,
):
    if halves:
        tokens, segments, bundle, later = refs[:4]
        x_out, q_out, k_out, v_out, seg_out, w_out, o_out, gain_out, later_out = refs[4:13]
        wg_s, w_send, w_recv, w_self = refs[13:17]
    else:
        tokens, segments, w_out, gain_out, later = refs[:5]
        x_out, q_out, k_out, v_out, seg_out, later_out = refs[5:11]
    (l_send, l_recv, x_s, kv_s, x_send, x_recv, x_self, kv_send, kv_recv, kv_self, seg_send, seg_recv, seg_self) = refs[-13:]
    d, t = 2 * lax.axis_index("plane") + lax.axis_index("core"), lax.axis_index("tensor")
    core = d % 2
    width = x_out.shape[1]
    micro = tokens.shape[0]
    per = tokens.shape[1]
    greet(nd, nt, d, t)

    if halves:
        own = pltpu.make_async_copy(bundle, wg_s.at[d, t], w_self)
        own.start()
        z_copies = []
        for s in range(1, nt):
            copy = remote(bundle, wg_s.at[d, t], w_send.at[0, 0, s], w_recv.at[0, 0, s], (d, lax.rem(t + s, nt)))
            copy.start()
            z_copies.append(copy)
        own.wait()
        for copy in z_copies:
            copy.wait()

    sends = []
    for m in range(micro):
        for c in range(2):
            to = (d - core + c, 2 * m + core)
            here = (to[0] == d) & (to[1] == t)
            src, dst = tokens.at[m, :, c], x_s.at[pl.ds(per * t, per)]
            far = remote(src, dst, x_send.at[2 * m + c], x_recv.at[t], to)
            near = pltpu.make_async_copy(src, dst, x_self)
            pl.when(jnp.logical_not(here))(far.start)
            pl.when(here)(near.start)
            sends.append((here, far, near))

    holder = t % 2 == core
    seg_here = pltpu.make_async_copy(segments.at[t // 2], seg_out, seg_self)
    seg_there = remote(segments.at[t // 2], seg_out, seg_send, seg_recv, (flip(d, 1), t))

    @pl.when(holder)
    def _():
        seg_here.start()
        seg_there.start()

    l_copies = []
    for s in range(1, nt):
        l_copies.append(remote(later, later_out.at[s - 1], l_send.at[s], l_recv.at[s], (d, lax.rem(t + s, nt))))
    for copy in l_copies:
        copy.start()

    if halves:
        bits = [1 << k for k in range(1, nd.bit_length() - 1)]
        routes = [bits + [1], bits[::-1] + [1]]
        have = [[0] for _ in halves]
        for stage in range(len(bits) + 1):
            copies = []
            for h, (lo, hi) in enumerate(halves):
                bit = routes[h][stage]
                for k, mask in enumerate(have[h]):
                    slab = d
                    for b in [1 << j for j in range(nd.bit_length() - 1)]:
                        if mask & b:
                            slab = flip(slab, b)
                    ref = wg_s.at[slab, :, pl.ds(lo, hi - lo)]
                    copies.append(
                        remote(ref, ref, w_send.at[1 + h, stage, k], w_recv.at[1 + h, stage, k], (flip(d, bit), t))
                    )
                have[h] = have[h] + [mask | bit for mask in have[h]]
            for copy in copies:
                copy.start()
            for copy in copies:
                copy.wait()

        gains = jnp.zeros((8, width), F32)
        for pair in range(nd * nt // 2):
            slabs = [wg_s[(2 * pair + e) // nt, (2 * pair + e) % nt].astype(F32) for e in range(2)]
            for k in range(3):
                both = jnp.concatenate([slab[k * share : (k + 1) * share] for slab in slabs])
                w_out[2 * pair * share : 2 * (pair + 1) * share, k * width : (k + 1) * width] = both.astype(BF16)
            both = jnp.concatenate([slab[3 * share : 4 * share] for slab in slabs])
            o_out[2 * pair * share : 2 * (pair + 1) * share, :] = both.astype(BF16)
            gains = gains + (slabs[0] + slabs[1])[4 * share : 4 * share + 8]
        gain_out[...] = gains

    kv_copies = []
    gain = gain_out[:1]
    for s in range(nt):
        source = lax.rem(t + s, nt)
        here = (source == t) & holder
        arrival = remote(
            x_s.at[pl.ds(per * source, per)], x_s.at[pl.ds(per * source, per)], x_send.at[0], x_recv.at[source], (flip(d, 1), t)
        )
        local = pltpu.make_async_copy(tokens.at[0, :, 0], x_s.at[pl.ds(per * source, per)], x_self)
        pl.when(jnp.logical_not(here))(arrival.wait_recv)
        pl.when(here)(local.wait)
        x = x_s[pl.ds(per * source, per)].reshape(per * BLOCK, width)
        rows = pl.ds(pl.multiple_of(source * per * BLOCK, per * BLOCK), per * BLOCK)
        x_out[rows, :] = x
        x = x.astype(F32)
        h = (x * rms_scale(x) * gain).astype(BF16)
        q_out[rows, :] = matmul(h, w_out[:, :width]).astype(BF16)
        for k, out in enumerate((k_out, v_out)):
            value = matmul(h, w_out[:, (k + 1) * width : (k + 2) * width]).astype(BF16)
            kv_s[k, s] = value.reshape(per, BLOCK, width)
            dst = out.at[pl.ds(per * source, per), core]
            near = pltpu.make_async_copy(kv_s.at[k, s], dst, kv_self.at[k, s])
            far = remote(kv_s.at[k, s], dst, kv_send.at[k, s], kv_recv.at[k, s], (flip(d, 1), t))
            near.start()
            far.start()
            kv_copies += [near, far]
    for copy in kv_copies + l_copies:
        copy.wait()
    for here, far, near in sends:
        pl.when(jnp.logical_not(here))(far.wait_send)

    @pl.when(holder)
    def _():
        seg_here.wait()
        seg_there.wait_send()

    @pl.when(jnp.logical_not(holder))
    def _():
        seg_there.wait_recv()


def start(tokens, segments, bundle, later, share):
    micro, _, rows, width = tokens.shape
    nd, nt = 2 * lax.axis_size("plane"), lax.axis_size("tensor")
    count = rows * nt // 2
    blocks = count // BLOCK
    per = blocks // nt
    length = bundle.shape[0]
    dma = pltpu.SemaphoreType.DMA
    vmem = pl.BlockSpec(memory_space=pltpu.VMEM)
    shaped = jax.ShapeDtypeStruct
    most = max(nd // 2, nt)
    inside = 2 * share % 16 == 0 and length >= 32
    middle = length // 32 * 16
    if inside:
        halves, given = [(0, middle), (middle, length)], [bundle]
        gathered_specs = [vmem, vmem, vmem]
        gathered = [shaped((width, 3 * width), BF16), shaped((width, width), BF16), shaped((8, width), F32)]
        scratch = [
            pltpu.VMEM((nd, nt, length, width), BF16),
            dma((3, nd.bit_length(), most)), dma((3, nd.bit_length(), most)), dma,
        ]
    else:
        slabs = lax.all_gather(bundle, AXES, axis=0, tiled=False)
        w_qkv = slabs[:, : 3 * share].reshape(nd * nt, 3, share, width).transpose(0, 2, 1, 3)
        w_qkv = w_qkv.reshape(width, 3 * width)
        w_out = slabs[:, 3 * share : 4 * share].reshape(width, width)
        gains = jnp.sum(slabs[:, 4 * share : 4 * share + 8].astype(F32), axis=0)
        halves, given, gathered_specs, gathered, scratch = [], [w_qkv, gains], [], [], []
    results = pl.pallas_call(
        functools.partial(start_kernel, nd, nt, share, halves),
        in_specs=[ANY, ANY] + ([ANY] if inside else [vmem, vmem]) + [ANY],
        out_specs=[vmem, vmem, ANY, ANY, ANY] + gathered_specs + [ANY],
        out_shape=[
            shaped((count, width), BF16),
            shaped((count, width), BF16),
            shaped((blocks, 2, BLOCK, width), BF16),
            shaped((blocks, 2, BLOCK, width), BF16),
            shaped((2 * blocks, BLOCK), jnp.int32),
            *gathered,
            shaped((nt - 1,) + later.shape, BF16),
        ],
        scratch_shapes=scratch + [
            dma((nt,)), dma((nt,)),
            pltpu.VMEM((blocks, BLOCK, width), BF16),
            pltpu.VMEM((2, nt, per, BLOCK, width), BF16),
            dma((nt,)), dma((nt,)), dma,
            dma((2, nt)), dma((2, nt)), dma((2, nt)),
            dma, dma, dma,
        ],
        compiler_params=pltpu.CompilerParams(
            collective_id=0, has_side_effects=True, vmem_limit_bytes=56 << 20
        ),
        name="start",
    )(
        tokens.reshape(micro, rows // TILE, 2, BLOCK, width),
        segments.reshape(micro, 2 * blocks, BLOCK),
        *given,
        later,
    )
    return results if inside else (*results[:5], w_qkv, w_out, gains, results[5])


def gelu_parts(v):
    t = 1.0 / (1.0 + 0.23164189 * jnp.abs(v))
    bell = jnp.exp(-0.5 * v * v)
    series = t * (0.127414796 + t * (-0.142248368 + t * (0.7107068705 + t * (-0.7265760135 + t * 0.5307027145))))
    tail = series * bell
    return jnp.where(v < 0.0, tail, 1.0 - tail), 0.3989422804 * bell


def middle_kernel(rb, nd, nt, share, inside, *refs):
    x_ref, att_ref, w_out, gain_ref, own_ref, rest_ref = refs[:6]
    dys, refs = refs[6 : 6 + nt], refs[6 + nt :]
    outs, refs = refs[:nt], refs[nt:]
    after_ref, datt_ref, dwo_ref, dgain_ref, part_ref = refs[:5]
    dy_ref, h_s, ht_s, dyt_s, o_s, dh_s, hid_s, dhid_s, w_s, sems = refs[5:15]
    if inside:
        g_s, core_s, plane_s, c_send, c_recv, p_send, p_recv = refs[15:]
    step = pl.program_id(0)
    d, t = 2 * lax.axis_index("plane") + lax.axis_index("core"), lax.axis_index("tensor")
    count, width = x_ref.shape
    parts = range(0, count, rb)
    bits = [1 << k for k in range(1, nd.bit_length() - 1)]
    routes = [bits, bits[::-1]]

    @pl.when(step == 0)
    def _():
        if inside:
            greet(nd, nt, d, t)
        copies = []
        for turn, dy in enumerate(dys):
            rows = pl.ds(pl.multiple_of(seat(turn)[1] * (count // nt), count // nt), count // nt)
            copies.append(pltpu.make_async_copy(dy, dy_ref.at[rows], sems.at[turn]))
        for copy in copies:
            copy.start()
        for r in parts:
            rows = slice(r, r + rb)
            after = x_ref[rows, :].astype(F32) + matmul(att_ref[rows, :], w_out[...])
            after_ref[rows, :] = after
            o_s[rows, :] = after
            h = (after * rms_scale(after) * gain_ref[...]).astype(BF16)
            h_s[rows, :] = h
            ht_s[:, rows] = h.T
            dh_s[rows, :] = jnp.zeros((rb, width), F32)
        for k in range(2):
            w_s[k] = own_ref[:, k * share : (k + 1) * share]
        for copy in copies:
            copy.wait()
        for r in parts:
            rows = slice(r, r + rb)
            dyt_s[:, rows] = dy_ref[rows, :].T

    @pl.when((step > 0) & (step < nt))
    def _():
        for k in range(2):
            w_s[k] = rest_ref[:, 0, k * share : (k + 1) * share]

    def core_copies(slot):
        return [
            remote(
                g_s.at[slot, flips(flip(d, 1), mask)], core_s.at[slot, j],
                c_send.at[slot, j], c_recv.at[slot, j], (flip(d, 1), t),
            )
            for j, mask in enumerate(masks_of(bits))
        ]

    def plane_copies(slot, stage):
        copies = []
        for h in range(2):
            bit, rows = routes[h][stage], pl.ds(h * share, share)
            for j, mask in enumerate(masks_of(routes[h][stage + 1 :])):
                copies.append(
                    remote(
                        g_s.at[slot, flips(flip(d, bit), mask), rows], plane_s.at[slot, stage, j, rows],
                        p_send.at[slot, stage, h, j], p_recv.at[slot, stage, h, j], (flip(d, bit), t),
                    )
                )
        return copies

    def core_done(k):
        slot = lax.rem(k, 2)
        for copy in core_copies(slot):
            copy.wait()
        for j, mask in enumerate(masks_of(bits)):
            mine = flips(d, mask)
            g_s[slot, mine] = (g_s[slot, mine].astype(F32) + core_s[slot, j].astype(F32)).astype(BF16)
        for copy in plane_copies(slot, 0):
            copy.start()

    def plane_done(k, stage):
        slot = lax.rem(k, 2)
        for copy in plane_copies(slot, stage):
            copy.wait()
        for h in range(2):
            rows = slice(h * share, (h + 1) * share)
            for j, mask in enumerate(masks_of(routes[h][stage + 1 :])):
                mine = flips(d, mask)
                total = g_s[slot, mine, rows].astype(F32) + plane_s[slot, stage, j, rows].astype(F32)
                g_s[slot, mine, rows] = total.astype(BF16)
        if stage + 1 < len(bits):
            for copy in plane_copies(slot, stage + 1):
                copy.start()
        else:
            part_ref[lax.rem(t + nt - k, nt)] = g_s[slot, d]

    def when(condition, stage, *args):
        if inside:
            pl.when(condition)(functools.partial(stage, *args))

    @pl.when(step < nt)
    def _():
        up, down = (w_s[k].reshape(width, -1) for k in range(2))
        for point, r in enumerate(parts):
            rows = slice(r, r + rb)
            v = matmul(h_s[rows, :], up)
            cumulative, density = gelu_parts(v)
            hid_s[rows, :] = (v * cumulative).astype(BF16)
            d_hidden = matmul(dy_ref[rows, :], down) * (cumulative + v * density)
            dhid_s[rows, :] = d_hidden.astype(BF16)
            if point == 1:
                when(step >= 1, core_done, step - 1)
        when(step >= 2, plane_done, step - 2, len(bits) - 1)
        slot = lax.rem(step, 2)
        for r in range(0, width, 2 * share):
            rows = slice(r, r + 2 * share)
            for k, (left, right) in enumerate(((ht_s, dhid_s), (dyt_s, hid_s))):
                both = matmul(left[rows, :], right[...]).astype(BF16)
                for e in range(2):
                    grad = both[e * share : (e + 1) * share]
                    if inside:
                        g_s[slot, r // share + e, k * share : (k + 1) * share] = grad
                    else:
                        part_ref[r // share + e, 0, k] = grad
        if inside:
            for copy in core_copies(slot):
                copy.start()
        for r in parts:
            rows = slice(r, r + rb)
            o_s[rows, :] += right_t(hid_s[rows, :], down)
            dh_s[rows, :] += right_t(dhid_s[rows, :], up)
        for stage in range(len(bits) - 1):
            when(step >= 1, plane_done, step - 1, stage)

    @pl.when(step == nt)
    def _():
        gain = gain_ref[...]
        total = jnp.zeros((8, width), F32)
        for turn, out in enumerate(outs):
            rows = pl.ds(pl.multiple_of(seat(turn)[1] * (count // nt), count // nt), count // nt)
            out[...] = o_s[rows, :].astype(BF16)
        for point, r in enumerate(parts):
            rows = slice(r, r + rb)
            after = after_ref[rows, :]
            scale = rms_scale(after)
            normed = after * scale
            dh = dh_s[rows, :]
            total = total + jnp.sum((dh * normed).reshape(rb // 8, 8, width), axis=0)
            d_after = dy_ref[rows, :].astype(F32) + rms_back(dh, normed, scale, gain)
            after_ref[rows, :] = d_after
            branch = d_after.astype(BF16)
            hid_s[rows, :] = branch
            datt_ref[rows, :] = right_t(branch, w_out[...]).astype(BF16)
            if inside and point == 0:
                core_done(nt - 1)
        if inside:
            plane_done(step - 2, len(bits) - 1)
        dgain_ref[...] = total
        if inside:
            for stage in range(len(bits) - 1):
                plane_done(nt - 1, stage)
        dwo_ref[...] = left_t(att_ref[...], hid_s[...]).astype(BF16)
        if inside:
            plane_done(nt - 1, len(bits) - 1)


def feed_forward(x, attended, dys, w_out, gain, own, rest):
    count, width = x.shape
    nd, nt, units = own.shape[0], rest.shape[1] + 1, own.shape[2]
    share = own.shape[1] // 2
    inside = share % 16 == 0 and nd >= 8
    rb = 256
    rows, part = whole((count, width)), whole((count // nt, width))
    dma = pltpu.SemaphoreType.DMA
    scratch = [
        pltpu.VMEM((count, width), BF16),
        pltpu.VMEM((count, width), BF16),
        pltpu.VMEM((width, count), BF16),
        pltpu.VMEM((width, count), BF16),
        pltpu.VMEM((count, width), F32),
        pltpu.VMEM((count, width), F32),
        pltpu.VMEM((count, units), BF16),
        pltpu.VMEM((count, units), BF16),
        pltpu.VMEM((2, nd, share, units), BF16),
        dma((nt,)),
    ]
    if inside:
        stages = nd.bit_length() - 2
        grads, grads_spec = jax.ShapeDtypeStruct((nt, 2 * share, units), BF16), whole((nt, 2 * share, units))
        scratch += [
            pltpu.VMEM((2, nd, 2 * share, units), BF16),
            pltpu.VMEM((2, nd // 2, 2 * share, units), BF16),
            pltpu.VMEM((2, stages, nd // 4, 2 * share, units), BF16),
            dma((2, nd // 2)), dma((2, nd // 2)),
            dma((2, stages, 2, nd // 4)), dma((2, stages, 2, nd // 4)),
        ]
        params = dict(collective_id=2, has_side_effects=True)
    else:
        grads = jax.ShapeDtypeStruct((nd, nt, 2, share, units), BF16)
        grads_spec = pl.BlockSpec((nd, 1, 2, share, units), lambda s: (0, jnp.minimum(s, nt - 1), 0, 0, 0))
        params = {}
    return pl.pallas_call(
        functools.partial(middle_kernel, rb, nd, nt, share, inside),
        grid=(nt + 1,),
        in_specs=[
            rows, rows, whole((width, width)), whole((1, width)), whole(own.shape),
            pl.BlockSpec((nd, 1, 2 * share, units), lambda s: (0, jnp.clip(s - 1, 0, nt - 2), 0, 0)),
        ] + [ANY] * nt,
        out_specs=[part] * nt + [rows, rows, whole((width, width)), whole((8, width)), grads_spec],
        out_shape=[jax.ShapeDtypeStruct((count // nt, width), BF16)] * nt + [
            jax.ShapeDtypeStruct((count, width), F32),
            jax.ShapeDtypeStruct((count, width), BF16),
            jax.ShapeDtypeStruct((width, width), BF16),
            jax.ShapeDtypeStruct((8, width), F32),
            grads,
        ],
        scratch_shapes=scratch,
        compiler_params=pltpu.CompilerParams(vmem_limit_bytes=62 << 20, **params),
        cost_estimate=cost(12 * count * width * nt * units, 4 * nd * nt * share * units),
        name="feed_forward",
    )(x, attended, w_out, gain, own, rest, *dys)


def masks_of(bits):
    masks = [0]
    for bit in bits:
        masks = masks + [mask | bit for mask in masks]
    return masks


def flips(index, mask):
    bit = 1
    while bit <= mask:
        if mask & bit:
            index = flip(index, bit)
        bit *= 2
    return index


def finish_kernel(
    nd, nt, share, inside, x_ref, dq_ref, dk_all, dv_all, after_ref, w_ref, gain_ref, dwo_ref, small_ref,
    *refs,
):
    tok_out, dw_out, small_out = refs[:3]
    own_s, other_s, grads_s, ht_s, tok_s, own_sems, kv_send, kv_recv, tok_send, tok_recv, tok_self = refs[3:14]
    if inside:
        slab_s, core_s, plane_s, z_s, sm_s, sm_in, g_send, g_recv, s_send, s_recv = refs[14:]
    d, t = 2 * lax.axis_index("plane") + lax.axis_index("core"), lax.axis_index("tensor")
    core = d % 2
    count, width = x_ref.shape
    per = tok_out.shape[1]
    rows_in = per * BLOCK
    holder = t % 2 == core
    bits = [1 << k for k in range(1, nd.bit_length() - 1)]
    greet(nd, nt, d, t)

    order = [lax.rem(t + s, nt) for s in list(range(1, nt)) + [0]]
    own = [pltpu.make_async_copy(a.at[:, core], own_s.at[k], own_sems.at[k]) for k, a in enumerate((dk_all, dv_all))]
    for copy in own:
        copy.start()
    exchanged = []
    for s, source in enumerate(order):
        pair = []
        for k, a in enumerate((dk_all, dv_all)):
            pair.append(
                remote(
                    a.at[pl.ds(per * source, per), 1 - core], other_s.at[k, pl.ds(per * source, per)],
                    kv_send.at[k, s], kv_recv.at[k, s], (flip(d, 1), t),
                )
            )
            pair[-1].start()
        exchanged.append(pair)
    gain = gain_ref[:1]

    def norms(rows):
        x = x_ref[rows, :].astype(F32)
        scale = rms_scale(x)
        return x * scale, scale

    def fill(bundle, at, source, first):
        lines = source.shape[0] // share
        for k in range(lines):
            slab = first // share + k
            slab_s[bundle, slab // nt, slab % nt, at : at + source.shape[1] // width * share] = jnp.concatenate(
                [
                    source[k * share : (k + 1) * share, m * width : (m + 1) * width]
                    for m in range(source.shape[1] // width)
                ]
            ).astype(BF16)

    halves = [(0, nt // 2), (nt // 2, nt)]
    routes = [[1] + bits, [1] + bits[::-1]]

    def stage_copies(bundle, stage):
        copies, adds = [], []
        for h, (lo, hi) in enumerate(halves):
            bit, part = routes[h][stage], pl.ds(lo, hi - lo)
            for k, mask in enumerate(masks_of(routes[h][stage + 1 :])):
                buffer = core_s.at[bundle] if stage == 0 else plane_s.at[bundle, stage - 1]
                copies.append(
                    remote(
                        slab_s.at[bundle, flips(flip(d, bit), mask), part], buffer.at[k, part],
                        g_send.at[bundle, h, stage, k], g_recv.at[bundle, h, stage, k], (flip(d, bit), t),
                    )
                )
                adds.append((flips(d, mask), lo, hi, buffer, k))
        return copies, adds

    def stage_start(bundle, stage):
        for copy in stage_copies(bundle, stage)[0]:
            copy.start()

    def stage_done(bundle, stage):
        copies, adds = stage_copies(bundle, stage)
        for copy in copies:
            copy.wait()
        for mine, lo, hi, buffer, k in adds:
            both = slab_s[bundle, mine, lo:hi].astype(F32) + buffer[k, lo:hi].astype(F32)
            slab_s[bundle, mine, lo:hi] = both.astype(BF16)

    def z_copies(bundle):
        copies = []
        for s in range(1, nt):
            to = lax.rem(t + s, nt)
            copies.append(
                remote(
                    slab_s.at[bundle, d, to], z_s.at[bundle, s],
                    g_send.at[bundle, 2, 0, s], g_recv.at[bundle, 2, 0, s], (d, to),
                )
            )
        return copies

    def small_copies(stage):
        if stage <= len(bits):
            return [remote(sm_s, sm_in.at[stage], s_send.at[stage], s_recv.at[stage], (flip(d, routes[0][stage]), t))]
        copies = []
        for s in range(1, nt):
            k = len(bits) + s
            copies.append(remote(sm_s, sm_in.at[k], s_send.at[k], s_recv.at[k], (d, lax.rem(t + s, nt))))
        return copies

    d_gain = jnp.zeros((8, width), F32)
    sends = []
    to_core = d - core + t % 2
    for s, source in enumerate(order):
        if s == 0:
            for copy in own:
                copy.wait()
        for copy in exchanged[s]:
            copy.wait()
        rows = pl.ds(pl.multiple_of(source * rows_in, rows_in), rows_in)
        grads_s[rows, :width] = dq_ref[rows, :]
        for k in range(2):
            total = own_s[k, pl.ds(per * source, per)].astype(F32) + other_s[k, pl.ds(per * source, per)].astype(F32)
            grads_s[rows, (k + 1) * width : (k + 2) * width] = total.reshape(rows_in, width).astype(BF16)
        dh = right_t(grads_s[rows, :], w_ref[...])
        normed, scale = norms(rows)
        d_gain = d_gain + jnp.sum((dh * normed).reshape(rows_in // 8, 8, width), axis=0)
        tok = after_ref[rows, :] + rms_back(dh, normed, scale, gain)
        tok_s[s] = tok.astype(BF16).reshape(per, BLOCK, width)
        here = (source == t) & holder
        dst = tok_out.at[t // 2, :, core]
        far = remote(tok_s.at[s], dst, tok_send.at[s], tok_recv.at[2 * (t // 2) + core], (to_core, source))
        near = pltpu.make_async_copy(tok_s.at[s], dst, tok_self)
        pl.when(jnp.logical_not(here))(far.start)
        pl.when(here)(near.start)
        sends.append((here, far, near))
        if s == 0:
            for r in range(0, count, rows_in):
                lines = slice(r, r + rows_in)
                normed, scale = norms(lines)
                ht_s[:, lines] = (normed * gain).astype(BF16).T
            if inside:
                for r in range(0, width, 8 * share):
                    lines = slice(r, r + 8 * share)
                    dwo = dwo_ref[lines, :].astype(F32)
                    fill(0, 0, jnp.concatenate([matmul(ht_s[lines, :], dq_ref[...]), dwo], axis=1), r)
                stage_start(0, 0)
        if s == 1 and inside:
            stage_done(0, 0)
            stage_start(0, 1)

    small = small_ref[...]
    line = lax.broadcasted_iota(jnp.int32, small.shape, 0)
    small = small + jnp.where(line == 0, jnp.sum(d_gain, axis=0, keepdims=True), 0.0)
    if inside:
        sm_s[...] = small
        tiny = small_copies(0)
        for copy in tiny:
            copy.start()
        for stage in range(1, len(bits)):
            stage_done(0, stage)
            stage_start(0, stage + 1)
        for r in range(0, width, 8 * share):
            fill(1, 0, matmul(ht_s[r : r + 8 * share, :], grads_s[:, width:]), r)
        stage_start(1, 0)
        stage_done(0, len(bits))
        first_z = z_copies(0)
        for copy in first_z:
            copy.start()
        for stage in range(len(bits) + 1):
            for copy in tiny:
                copy.wait()
            sm_s[...] += sm_in[stage]
            stage_done(1, stage)
            if stage < len(bits):
                stage_start(1, stage + 1)
            tiny = small_copies(stage + 1)
            for copy in tiny:
                copy.start()
        second_z = z_copies(1)
        for copy in second_z:
            copy.start()
        for copy in first_z + second_z + tiny:
            copy.wait()
        for bundle in range(2):
            total = slab_s[bundle, d, t].astype(F32)
            for s in range(1, nt):
                total = total + z_s[bundle, s].astype(F32)
            dw_out[bundle * 2 * share : (bundle + 1) * 2 * share] = total
        small_out[...] = sm_s[...] + sum(sm_in[len(bits) + s] for s in range(1, nt))
    else:
        small_out[...] = small
        for r in range(0, width, 256):
            lines = slice(r, r + 256)
            dw_out[lines, : 3 * width] = matmul(ht_s[lines, :], grads_s[...]).astype(BF16)
            dw_out[lines, 3 * width :] = dwo_ref[lines, :]

    for here, far, near in sends:
        pl.when(jnp.logical_not(here))(far.wait_send)
        pl.when(here)(near.wait)
    for m in range(tok_out.shape[0]):
        for c in range(2):
            here = (2 * m + core == t) & (c == core)
            dst = tok_out.at[m, :, c]
            back = remote(dst, dst, tok_send.at[0], tok_recv.at[2 * m + c], (flip(d, 1), t))
            pl.when(jnp.logical_not(here))(back.wait_recv)


def finish(x, dq, dk_all, dv_all, after, w_qkv, gains, dwo, small, share, micro):
    count, width = x.shape
    nd, nt = 2 * lax.axis_size("plane"), lax.axis_size("tensor")
    inside = 2 * share % 16 == 0 and nd >= 8
    blocks = count // BLOCK
    per = blocks // nt
    dma = pltpu.SemaphoreType.DMA
    vmem = pl.BlockSpec(memory_space=pltpu.VMEM)
    shaped = jax.ShapeDtypeStruct
    scratch = [
        pltpu.VMEM((2, blocks, BLOCK, width), BF16),
        pltpu.VMEM((2, blocks, BLOCK, width), BF16),
        pltpu.VMEM((count, 3 * width), BF16),
        pltpu.VMEM((width, count), BF16),
        pltpu.VMEM((nt, per, BLOCK, width), BF16),
        dma((2,)), dma((2, nt)), dma((2, nt)), dma((nt,)), dma((nt,)), dma,
    ]
    if inside:
        most = max(nd // 2, nt)
        stages = nd.bit_length() - 1
        scratch += [
            pltpu.VMEM((2, nd, nt, 2 * share, width), BF16),
            pltpu.VMEM((2, nd // 2, nt, 2 * share, width), BF16),
            pltpu.VMEM((2, stages - 1, nd // 4, nt, 2 * share, width), BF16),
            pltpu.VMEM((2, nt, 2 * share, width), BF16),
            pltpu.VMEM(small.shape, F32),
            pltpu.VMEM((stages + nt,) + small.shape, F32),
            dma((2, 3, stages, most)), dma((2, 3, stages, most)), dma((stages + nt,)), dma((stages + nt,)),
        ]
    return pl.pallas_call(
        functools.partial(finish_kernel, nd, nt, share, inside),
        in_specs=[vmem, vmem, ANY, ANY, vmem, vmem, vmem, vmem, vmem],
        out_specs=[vmem, vmem, vmem],
        out_shape=[
            shaped((micro, per, 2, BLOCK, width), BF16),
            shaped((4 * share, width), F32) if inside else shaped((width, 4 * width), BF16),
            shaped(small.shape, F32),
        ],
        scratch_shapes=scratch,
        compiler_params=pltpu.CompilerParams(
            collective_id=1, has_side_effects=True, vmem_limit_bytes=60 << 20
        ),
        cost_estimate=cost(24 * count * width * width, 16 * count * width),
        name="finish",
    )(x, dq, dk_all, dv_all, after, w_qkv, gains, dwo, small)


def per_device(
    tokens, segments, w_query, w_key, w_value, w_out, norm_attn, norm_ffn, pre_mix, post_mix, w_up, w_down, out_grad,
):
    micro, _, rows, width = tokens.shape
    nd, nt = 2 * lax.axis_size("plane"), lax.axis_size("tensor")
    heads = pre_mix.shape[0]
    head_width = width // heads
    length = rows * nt
    count = length // 2
    blocks = count // BLOCK
    share = w_query.shape[0]
    bits = [1 << k for k in range(nd.bit_length() - 1)]
    d, t = 2 * lax.axis_index("plane") + lax.axis_index("core"), lax.axis_index("tensor")
    core = d % 2

    place = (d * nt + t) * share
    gains = lax.dynamic_update_slice(jnp.zeros((8, width), BF16), jnp.stack([norm_attn, norm_ffn]), (0, place))
    fill = jnp.zeros((-(4 * share + 8) % 16, width), BF16)
    bundle = jnp.concatenate([w_query, w_key, w_value, w_out, gains, fill])
    later = jnp.concatenate([w_up, w_down])
    own_rows = lax.all_gather(later, ("plane", "core"), axis=0, tiled=False)
    x, query, k_all, v_all, segs, w_qkv, all_out, gains, later = start(tokens, segments, bundle, later, share)
    k_all, v_all = (a.reshape(2 * blocks, BLOCK, width) for a in (k_all, v_all))
    x, out_grad = lax.optimization_barrier((x, out_grad))
    grad_turns = to_sequences(out_grad)
    rest_rows = lax.all_gather(later, ("plane", "core"), axis=0, tiled=False)

    def by_lane(mix):
        return jnp.repeat(mix.astype(F32), head_width, axis=1)

    pre = (by_lane(pre_mix.T) * head_width ** (-0.5)).astype(BF16)
    post = by_lane(post_mix)

    attended, u, lse = attend(query, k_all, v_all, segs, pre, post)
    *out_turns, grad_after, grad_attended, grad_w_out, grad_gain_ffn, part_both = feed_forward(
        x, attended, grad_turns, all_out, gains[1:2], own_rows, rest_rows
    )
    grad_gain_ffn = jnp.sum(grad_gain_ffn, axis=0)
    out = from_sequences(out_turns, micro)
    if part_both.ndim > 3:
        part_both = lax.dynamic_slice_in_dim(jnp.concatenate([part_both[:, ::-1]] * 2, axis=1), nt - 1 - t, nt, 1)
        part_both = lax.psum_scatter(part_both, ("plane", "core"), scatter_dimension=0, tiled=False)
    part_both = lax.psum_scatter(part_both, "tensor", scatter_dimension=0, tiled=False).astype(F32)
    part_both = part_both.reshape((2,) + w_up.shape)

    grad_query, grad_key, grad_value, d_pre, d_post = attend_back(
        query, grad_attended, u, lse, k_all, v_all, segs, pre, post
    )

    def spread(d_mix):
        total = d_mix.reshape(heads, 8, heads, head_width).sum((1, 3)).reshape(-1)
        return jnp.pad(total, (0, width - total.shape[0]))

    small = jnp.zeros((8, width), F32).at[1].set(grad_gain_ffn)
    small = small.at[2].set(spread(d_pre)).at[3].set(spread(d_post))
    x, out = lax.optimization_barrier((x, out))
    d_tokens, owned, small = finish(
        x, grad_query, grad_key.reshape(blocks, 2, BLOCK, width), grad_value.reshape(blocks, 2, BLOCK, width),
        grad_after, w_qkv, gains, grad_w_out, small, share, micro,
    )
    d_tokens = d_tokens.reshape(tokens.shape).astype(F32)
    if owned.dtype == BF16:
        owned = lax.psum_scatter(owned, AXES, scatter_dimension=0, tiled=True).astype(F32)
        owned = [owned[:, k * width : (k + 1) * width] for k in range(4)]
        small = lax.psum(small, AXES)
    else:
        owned = [owned[k * share : (k + 1) * share] for k in (0, 2, 3, 1)]
    gain_grads = lax.dynamic_slice_in_dim(small, place, share, 1)
    pairs = heads * heads
    return (
        out,
        d_tokens,
        owned[0],
        owned[1],
        owned[2],
        owned[3],
        gain_grads[0],
        gain_grads[1],
        small[2, :pairs].reshape(heads, heads).T * head_width ** (-0.5),
        small[3, :pairs].reshape(heads, heads),
        part_both[0],
        part_both[1],
    )


def solution(mesh):
    devices = mesh.devices
    devices = devices.reshape(devices.shape[0] // 2, 2, devices.shape[1])
    dp = ("plane", "core")
    both = P(AXES, None)
    gain = P(AXES)
    data = P(None, dp, "tensor", None)
    ffn = P(dp, "tensor")
    return jax.shard_map(
        per_device,
        mesh=jax.sharding.Mesh(devices, AXES),
        in_specs=(data, P(None, dp, None), both, both, both, both, gain, gain, P(), P(), ffn, ffn, data),
        out_specs=(data, data, both, both, both, both, gain, gain, P(), P(), ffn, ffn),
        check_vma=False,
    )
```

```python
import functools

import jax
import jax.numpy as jnp
from jax import lax
from jax.experimental import pallas as pl
from jax.experimental.pallas import tpu as pltpu
from jax.sharding import PartitionSpec as P

F32 = jnp.float32
BF16 = jnp.bfloat16
BLOCK = 128
TILE = 2 * BLOCK
FORWARD_GROUPS = 6
BACKWARD_GROUPS = (2, 2, 2)
AXES = ("plane", "core", "tensor")


def matmul(left, right):
    return jnp.dot(left, right, preferred_element_type=F32)


def right_t(left, right):
    return lax.dot_general(left, right, (((1,), (1,)), ((), ())), preferred_element_type=F32)


def left_t(left, right):
    return lax.dot_general(left, right, (((0,), (0,)), ((), ())), preferred_element_type=F32)


def rms_scale(values):
    return lax.rsqrt(jnp.mean(values * values, axis=-1, keepdims=True) + 1e-06)


def rms_back(grad_norm, normed, scale, gain):
    scaled = grad_norm * gain
    return scale * (scaled - normed * jnp.mean(scaled * normed, axis=-1, keepdims=True))


def gelu_exact(values):
    return jax.nn.gelu(values, approximate=False)


def gelu_back(upper, grad):
    unused, pull = jax.vjp(gelu_exact, upper)
    return pull(grad)[0]


def send(x, to):
    nd, nt = 2 * lax.axis_size("plane"), lax.axis_size("tensor")
    pairs = []
    for d in range(nd):
        for t in range(nt):
            d2, t2 = to(d, t)
            pairs.append((d * nt + t, d2 * nt + t2))
    return lax.ppermute(x, AXES, pairs)


def by_shift(shift):
    nt = lax.axis_size("tensor")
    return lambda d, t: (d, (t + shift) % nt)


def by_bit(bit):
    return lambda d, t: (d ^ bit, t)


def gather(piece, bits):
    nt = lax.axis_size("tensor")
    have = {0: jnp.stack([piece] + [send(piece, by_shift(s)) for s in range(1, nt)])}
    for bit in bits:
        have.update({mask | bit: send(block, by_bit(bit)) for mask, block in have.items()})
    return [have[mask] for mask in range(len(have))]


def pick(x, index, axis):
    return lax.dynamic_index_in_dim(x, index, axis, keepdims=False)


def sum_to_owner(x, bits):
    nt, nd = x.shape[:2]
    d, t = 2 * lax.axis_index("plane") + lax.axis_index("core"), lax.axis_index("tensor")
    rest = x.shape[2:]
    names = [1 << k for k in range(nd.bit_length() - 1)][::-1]
    x = x.reshape((nt,) + (2,) * len(names) + rest)
    for bit in bits:
        axis = 1 + names.index(bit)
        names.remove(bit)
        mine = (d // bit) % 2
        got = send(pick(x, 1 - mine, axis), by_bit(bit))
        x = pick(x, mine, axis).astype(F32) + got.astype(F32)
        if names or nt > 1:
            x = x.astype(BF16)
    total = pick(x, t, 0).astype(F32)
    for shift in range(1, nt):
        total = total + send(pick(x, lax.rem(t + shift, nt), 0), by_shift(shift)).astype(F32)
    return total


def arrive(step, sources, scratches, sems, seg_ref, seg_s):
    blocks = sources[0].shape[0]
    copies = []
    for k, (source, scratch) in enumerate(zip(sources, scratches)):
        for part in range(blocks // 2):
            rows = pl.ds(2 * part, 2)
            there = scratch.at[pl.ds(2 * part + 1, 2)]
            copies.append((part, pltpu.make_async_copy(source.at[rows], there, sems.at[k, part])))

    @pl.when(step == 0)
    def _():
        for _, copy in copies:
            copy.start()
        seg_s[0] = jnp.full((1, BLOCK), -1, jnp.int32)
        seg_s[1:] = seg_ref[...]
        for scratch in scratches:
            scratch[0] = jnp.zeros(scratch.shape[1:], BF16)

    for part, copy in copies:
        pl.when(step == part)(copy.wait)


def reach(block, seg_low):
    first = seg_low[block, 0]
    before = 0
    for k in range(seg_low.shape[0]):
        before += (seg_low[k, BLOCK - 1] < first).astype(jnp.int32)
    return (block + 2 - before) // 2


def rows_of(block, seg_s):
    return jnp.broadcast_to(seg_s[block + 1], (BLOCK, BLOCK)).T


def row_mask(row_seg, first, block, seg_s):
    row = lax.broadcasted_iota(jnp.int32, (BLOCK, BLOCK), 0)
    col = lax.broadcasted_iota(jnp.int32, (BLOCK, BLOCK), 1)
    masks = []
    for k in range(2):
        ahead = (first + k - 1 - block) * BLOCK
        allowed = (row_seg == seg_s[first + k]) & (col + ahead <= row)
        masks.append(jnp.where(allowed, 0.0, -1e30).astype(F32))
    return jnp.concatenate(masks, axis=1)


def forward_kernel(
    heads, groups, most, q_ref, k_all, v_all, seg_low, seg_ref, pre_ref, post_ref,
    att_ref, u_ref, lse_ref, k_s, v_s, seg_s, qp_s, m_s, s_s, sems,
):
    step = pl.program_id(0)
    core = lax.axis_index("core")
    block = 2 * step + core
    width = q_ref.shape[1]
    arrive(step, [k_all, v_all], [k_s, v_s], sems, seg_ref, seg_s)
    tiles = reach(block, seg_low)
    row_seg = rows_of(block, seg_s)

    def scores(left, first, mask):
        keys = k_s[pl.ds(first, 2)].reshape(TILE, -1)
        s = right_t(left, keys).reshape(left.shape[0] // BLOCK, BLOCK, TILE)
        return (s + mask[None]).reshape(left.shape[0], TILE)

    def close(g, per, top, total, u, att):
        size = per * BLOCK
        lse_ref[0, g * size : (g + 1) * size, :] = jnp.broadcast_to(top + jnp.log(total), (size, BLOCK))
        for k in range(per):
            h = g * per + k
            part = u[k * BLOCK : (k + 1) * BLOCK]
            u_ref[0, h] = part.astype(BF16)
            att = att + part * post_ref[h : h + 1, :]
        return att

    @pl.when(tiles == 1)
    def _():
        per = heads // groups
        query = q_ref[...]
        mask = row_mask(row_seg, block, block, seg_s)
        att = jnp.zeros((BLOCK, width), F32)
        values = v_s[pl.ds(block, 2)].reshape(TILE, -1)
        for g in range(groups):
            left = jnp.concatenate([query * pre_ref[h : h + 1, :] for h in range(g * per, (g + 1) * per)])
            s = scores(left, block, mask)
            top = jnp.max(s, axis=-1, keepdims=True)
            p = jnp.exp(s - top)
            total = jnp.sum(p, axis=-1, keepdims=True)
            u = matmul((p * (1.0 / total)).astype(BF16), values)
            att = close(g, per, top, total, u, att)
        att_ref[...] = att.astype(BF16)

    @pl.when(tiles > 1)
    def _():
        query = q_ref[...]
        for h in range(heads):
            qp_s[h * BLOCK : (h + 1) * BLOCK, :] = query * pre_ref[h : h + 1, :]
        m_s[...] = jnp.full(m_s.shape, -3e38, F32)
        split = 2
        size = heads // split * BLOCK

        def meet(tile, carry):
            first = block - 2 * tile
            mask = row_mask(row_seg, first, block, seg_s)
            for g in range(split):
                rows = slice(g * size, (g + 1) * size)
                s = scores(qp_s[rows, :], first, mask)
                s_s[tile, rows, :] = s
                m_s[rows, :] = jnp.maximum(m_s[rows, :], jnp.maximum(s[:, :BLOCK], s[:, BLOCK:]))
            return carry

        lax.fori_loop(0, tiles, meet, 0)

    for n in range(2, most + 1):

        @pl.when(tiles == n)
        def _(n=n):
            per = heads // groups
            size = per * BLOCK
            values = v_s[pl.ds(block - 2 * n + 2, 2 * n)].reshape(n * TILE, -1)
            att = jnp.zeros((BLOCK, width), F32)
            for g in range(groups):
                rows = slice(g * size, (g + 1) * size)
                top = jnp.max(m_s[rows, :], axis=-1, keepdims=True)
                parts = [jnp.exp(s_s[tile, rows, :] - top) for tile in range(n)]
                total = jnp.sum(sum(p[:, :BLOCK] + p[:, BLOCK:] for p in parts), axis=-1, keepdims=True)
                p = jnp.concatenate([part.astype(BF16) for part in parts[::-1]], axis=1)
                u = matmul(p, values) * (1.0 / total)
                att = close(g, per, top, total, u, att)
            att_ref[...] = att.astype(BF16)


def whole(shape):
    return pl.BlockSpec(shape, lambda i: (0,) * len(shape), pipeline_mode=pl.Buffered(1))


def cost(flops, moved):
    return pl.CostEstimate(flops=int(flops), bytes_accessed=int(moved), transcendentals=0)


ANY = pl.BlockSpec(memory_space=pl.ANY)
SCALARS = pl.BlockSpec(memory_space=pltpu.SMEM)


def attend(query, k_all, v_all, segs, pre, post):
    heads, width = pre.shape
    rows, stack = query.shape[0], heads * BLOCK
    blocks = rows // BLOCK
    groups = FORWARD_GROUPS
    most = (1024 // BLOCK + 2) // 2
    by_block = pl.BlockSpec((BLOCK, width), lambda i: (i, 0))
    return pl.pallas_call(
        functools.partial(forward_kernel, heads, groups, most),
        grid=(blocks,),
        in_specs=[
            by_block, ANY, ANY, SCALARS, whole((2 * blocks, 1, BLOCK)), whole(pre.shape), whole(post.shape),
        ],
        out_specs=[
            by_block,
            pl.BlockSpec((1, heads, BLOCK, width), lambda i: (i, 0, 0, 0)),
            pl.BlockSpec((1, stack, BLOCK), lambda i: (i, 0, 0)),
        ],
        scratch_shapes=[
            pltpu.VMEM((2 * blocks + 1, BLOCK, width), BF16),
            pltpu.VMEM((2 * blocks + 1, BLOCK, width), BF16),
            pltpu.VMEM((2 * blocks + 1, 1, BLOCK), jnp.int32),
            pltpu.VMEM((stack, width), BF16),
            pltpu.VMEM((stack, BLOCK), F32),
            pltpu.VMEM((most, stack, TILE), F32),
            pltpu.SemaphoreType.DMA((2, blocks)),
        ],
        out_shape=[
            jax.ShapeDtypeStruct((rows, width), BF16),
            jax.ShapeDtypeStruct((blocks, heads, BLOCK, width), BF16),
            jax.ShapeDtypeStruct((blocks, stack, BLOCK), F32),
        ],
        compiler_params=pltpu.CompilerParams(vmem_limit_bytes=62 << 20),
        cost_estimate=cost(4 * rows * 1024 * stack // BLOCK * width, 4 * rows * stack // BLOCK * width),
        name="attend",
    )(query, k_all, v_all, segs, segs[:, None, :], pre, post)


def backward_kernel(
    heads, groups, q_ref, g_ref, u_ref, lse_ref, k_all, v_all, seg_low, seg_ref, pre_ref, post_ref,
    dq_ref, dk_ref, dv_ref, small_ref,
    dpre_ref, dpost_ref, k_s, v_s, seg_s, dk_s, dv_s, qp_s, gp_s, d_s, t_s, sems,
):
    step = pl.program_id(0)
    core = lax.axis_index("core")
    block = 2 * step + core
    width = q_ref.shape[1]
    arrive(step, [k_all, v_all], [k_s, v_s], sems, seg_ref, seg_s)

    @pl.when(step == 0)
    def _():
        dk_s[...] = jnp.zeros(dk_s.shape, F32)
        dv_s[...] = jnp.zeros(dv_s.shape, F32)
        dpre_ref[...] = jnp.zeros(dpre_ref.shape, F32)
        dpost_ref[...] = jnp.zeros(dpost_ref.shape, F32)

    tiles = reach(block, seg_low)
    row_seg = rows_of(block, seg_s)

    def opening(g, per):
        query, grad_low = q_ref[...], g_ref[...]
        grad = grad_low.astype(F32)
        left, right, terms = [], [], []
        for h in range(g * per, (g + 1) * per):
            gain = post_ref[h : h + 1, :]
            left.append(query * pre_ref[h : h + 1, :])
            right.append(grad_low * gain.astype(BF16))
            both = grad * u_ref[0, h].astype(F32)
            terms.append(jnp.sum(both * gain, axis=-1, keepdims=True))
            dpost_ref[h] += jnp.sum(both.reshape(BLOCK // 8, 8, -1), axis=0)
        return jnp.concatenate(left), jnp.concatenate(right), jnp.concatenate(terms)

    def closing(h, part, dq):
        dpre_ref[h] += jnp.sum((q_ref[...].astype(F32) * part).reshape(BLOCK // 8, 8, -1), axis=0)
        return dq + part * pre_ref[h : h + 1, :].astype(F32)

    def tile_part(first, mask, g, left, right, term):
        size = left.shape[0]
        per = size // BLOCK
        keys = k_s[pl.ds(first, 2)].reshape(TILE, -1)
        values = v_s[pl.ds(first, 2)].reshape(TILE, -1)
        s = (right_t(left, keys).reshape(per, BLOCK, TILE) + mask[None]).reshape(size, TILE)
        top = lse_ref[0, g * size : (g + 1) * size, :]
        p = jnp.exp(s - jnp.concatenate([top, top], axis=1))
        dw = right_t(right, values)
        ds = (p * (dw - term)).astype(BF16)
        return matmul(ds, keys), left_t(ds, left), left_t(p.astype(BF16), right)

    def add_up(first, dk, dv):
        dk_s[pl.ds(first, 2)] += dk.reshape(2, BLOCK, -1)
        dv_s[pl.ds(first, 2)] += dv.reshape(2, BLOCK, -1)

    @pl.when(tiles == 1)
    def _():
        mask = row_mask(row_seg, block, block, seg_s)
        dk = dv = jnp.zeros((TILE, width), F32)
        dq = jnp.zeros((BLOCK, width), F32)
        per = heads // groups[0]
        for g in range(groups[0]):
            part, a, b = tile_part(block, mask, g, *opening(g, per))
            dk, dv = dk + a, dv + b
            for k in range(per):
                dq = closing(g * per + k, part[k * BLOCK : (k + 1) * BLOCK], dq)
        add_up(block, dk, dv)
        dq_ref[...] = dq.astype(BF16)

    @pl.when(tiles > 1)
    def _():
        mask = row_mask(row_seg, block, block, seg_s)
        dk = dv = jnp.zeros((TILE, width), F32)
        per = heads // groups[1]
        size = per * BLOCK
        for g in range(groups[1]):
            rows = slice(g * size, (g + 1) * size)
            left, right, term = opening(g, per)
            qp_s[rows, :], gp_s[rows, :] = left, right
            d_s[rows, :] = jnp.broadcast_to(term, (size, BLOCK))
            t_s[rows, :], a, b = tile_part(block, mask, g, left, right, term)
            dk, dv = dk + a, dv + b
        add_up(block, dk, dv)

        def more(tile, carry):
            first = block - 2 * tile
            mask = row_mask(row_seg, first, block, seg_s)
            dk = dv = jnp.zeros((TILE, width), F32)
            size = heads // groups[2] * BLOCK
            for g in range(groups[2]):
                rows = slice(g * size, (g + 1) * size)
                term = jnp.concatenate([d_s[rows, :]] * 2, axis=1)
                part, a, b = tile_part(first, mask, g, qp_s[rows, :], gp_s[rows, :], term)
                t_s[rows, :] += part
                dk, dv = dk + a, dv + b
            add_up(first, dk, dv)
            return carry

        lax.fori_loop(1, tiles, more, 0)
        dq = jnp.zeros((BLOCK, width), F32)
        for h in range(heads):
            dq = closing(h, t_s[h * BLOCK : (h + 1) * BLOCK, :], dq)
        dq_ref[...] = dq.astype(BF16)

    @pl.when(step == pl.num_programs(0) - 1)
    def _():
        for k in range(dk_ref.shape[0]):
            dk_ref[k] = dk_s[k + 1].astype(BF16)
            dv_ref[k] = dv_s[k + 1].astype(BF16)
        sums = [jnp.sum(ref[h], axis=0, keepdims=True) for ref in (dpre_ref, dpost_ref) for h in range(heads)]
        row = lax.broadcasted_iota(jnp.int32, (width, BLOCK), 0)
        col = lax.broadcasted_iota(jnp.int32, (width, BLOCK), 1)
        member = (row // (width // heads) == col).astype(F32)
        mixes = jnp.dot(
            jnp.concatenate(sums), member, preferred_element_type=F32, precision=lax.Precision.HIGHEST
        )
        lines = 2 * heads * BLOCK // width
        small_ref[...] = jnp.zeros(small_ref.shape, F32)
        small_ref[:lines, :] = jnp.concatenate(
            [mixes[k * lines : (k + 1) * lines] for k in range(width // BLOCK)], axis=1
        )


def attend_back(query, grad, u, lse, k_all, v_all, segs, pre, post):
    heads, width = pre.shape
    rows, stack = query.shape[0], heads * BLOCK
    blocks = rows // BLOCK
    groups = BACKWARD_GROUPS
    lines = 2 * heads * BLOCK // width + 2
    lines += -lines % 8
    by_block = pl.BlockSpec((BLOCK, width), lambda i: (i, 0))
    return pl.pallas_call(
        functools.partial(backward_kernel, heads, groups),
        grid=(blocks,),
        in_specs=[
            by_block,
            by_block,
            pl.BlockSpec((1, heads, BLOCK, width), lambda i: (i, 0, 0, 0)),
            pl.BlockSpec((1, stack, BLOCK), lambda i: (i, 0, 0)),
            ANY, ANY, SCALARS, whole((2 * blocks, 1, BLOCK)), whole(pre.shape), whole(post.shape),
        ],
        out_specs=[
            by_block,
            whole((2 * blocks, BLOCK, width)),
            whole((2 * blocks, BLOCK, width)),
            whole((lines, width)),
        ],
        scratch_shapes=[
            pltpu.VMEM((heads, 8, width), F32),
            pltpu.VMEM((heads, 8, width), F32),
            pltpu.VMEM((2 * blocks + 1, BLOCK, width), BF16),
            pltpu.VMEM((2 * blocks + 1, BLOCK, width), BF16),
            pltpu.VMEM((2 * blocks + 1, 1, BLOCK), jnp.int32),
            pltpu.VMEM((2 * blocks + 1, BLOCK, width), F32),
            pltpu.VMEM((2 * blocks + 1, BLOCK, width), F32),
            pltpu.VMEM((stack, width), BF16),
            pltpu.VMEM((stack, width), BF16),
            pltpu.VMEM((stack, BLOCK), F32),
            pltpu.VMEM((stack, width), F32),
            pltpu.SemaphoreType.DMA((2, blocks)),
        ],
        out_shape=[
            jax.ShapeDtypeStruct((rows, width), BF16),
            jax.ShapeDtypeStruct((2 * blocks, BLOCK, width), BF16),
            jax.ShapeDtypeStruct((2 * blocks, BLOCK, width), BF16),
            jax.ShapeDtypeStruct((lines, width), F32),
        ],
        compiler_params=pltpu.CompilerParams(vmem_limit_bytes=62 << 20),
        cost_estimate=cost(10 * rows * 1024 * stack // BLOCK * width, 4 * rows * stack // BLOCK * width),
        name="attend_back",
    )(query, grad, u, lse, k_all, v_all, segs, segs[:, None, :], pre, post)


MESH = pl.DeviceIdType.MESH


def device(place):
    d, t = place
    return d // 2, d % 2, t


def flip(index, bit):
    return index + bit - 2 * bit * ((index // bit) % 2)


def greet(nd, nt, d, t):
    barrier = pltpu.get_barrier_semaphore()
    core = d % 2
    partners = [(d, lax.rem(t + s, nt)) for s in range(1, nt)]
    partners += [(flip(d, 1), lax.rem(t + s, nt)) for s in range(nt)]
    bit = 2
    while bit < nd:
        partners.append((flip(d, bit), t))
        bit *= 2
    for partner in partners:
        pl.semaphore_signal(barrier, inc=1, device_id=device(partner), device_id_type=MESH)
    pl.semaphore_wait(barrier, len(partners))


def remote(src, dst, send_sem, recv_sem, to):
    return pltpu.make_async_remote_copy(
        src_ref=src, dst_ref=dst, send_sem=send_sem, recv_sem=recv_sem, device_id=device(to), device_id_type=MESH
    )


def start_kernel(
    nd, nt, share, halves, *refs,
):
    tokens, grads, segments, later = refs[:4]
    if halves:
        weights, norms = refs[4:8], refs[8]
        x_out, q_out, k_out, v_out, seg_out, mail_out, later_out, w_out, o_out, gain_out = refs[9:19]
        wg_s, w_send, w_recv = refs[19:22]
    else:
        w_out, gain_out = refs[4:6]
        x_out, q_out, k_out, v_out, seg_out, mail_out, later_out = refs[6:13]
    (g_send, g_recv, g_self, l_send, l_recv, x_s, kv_s, x_send, x_recv, x_self, kv_send, kv_recv, kv_self, seg_send, seg_recv, seg_self) = refs[-16:]
    d, t = 2 * lax.axis_index("plane") + lax.axis_index("core"), lax.axis_index("tensor")
    core = d % 2
    width = x_out.shape[1]
    micro = tokens.shape[0]
    per = tokens.shape[1]
    greet(nd, nt, d, t)

    if halves:
        line = lax.broadcasted_iota(jnp.int32, (8, width), 0)
        lane = lax.broadcasted_iota(jnp.int32, (8, width), 1)
        gains = jnp.zeros((8, width), F32)
        for n in range(2):
            for k in range(share):
                here = (line == n) & (lane == (d * nt + t) * share + k)
                gains = jnp.where(here, norms[n, k], gains)
        own = [weight[...].astype(F32) for weight in weights] + [gains]
        rest = wg_s.shape[2] - 4 * share - 8
        own = own + ([jnp.zeros((rest, width), F32)] if rest else [])
        wg_s[d, t] = jnp.concatenate(own).astype(BF16)
        z_copies = []
        for s in range(1, nt):
            slab = wg_s.at[d, t]
            copy = remote(slab, slab, w_send.at[0, 0, s], w_recv.at[0, 0, s], (d, lax.rem(t + s, nt)))
            copy.start()
            z_copies.append(copy)
        for copy in z_copies:
            copy.wait()

    g_copies = []
    for m in range(micro):
        there = mail_out.at[2 * m + core]
        g_copies.append(pltpu.make_async_copy(grads.at[m, :, core], there, g_self.at[m]))
        g_copies.append(remote(grads.at[m, :, 1 - core], there, g_send.at[m], g_recv.at[m], (flip(d, 1), t)))
    for copy in g_copies:
        copy.start()

    sends = []
    for m in range(micro):
        for c in range(2):
            to = (d - core + c, 2 * m + core)
            here = (to[0] == d) & (to[1] == t)
            src, dst = tokens.at[m, :, c], x_s.at[pl.ds(per * t, per)]
            far = remote(src, dst, x_send.at[2 * m + c], x_recv.at[t], to)
            near = pltpu.make_async_copy(src, dst, x_self)
            pl.when(jnp.logical_not(here))(far.start)
            pl.when(here)(near.start)
            sends.append((here, far, near))

    holder = t % 2 == core
    seg_here = pltpu.make_async_copy(segments.at[t // 2], seg_out, seg_self)
    seg_there = remote(segments.at[t // 2], seg_out, seg_send, seg_recv, (flip(d, 1), t))

    @pl.when(holder)
    def _():
        seg_here.start()
        seg_there.start()

    l_copies = []
    for s in range(1, nt):
        l_copies.append(remote(later, later_out.at[s - 1], l_send.at[s], l_recv.at[s], (d, lax.rem(t + s, nt))))
    for copy in l_copies:
        copy.start()

    if halves:
        bits = [1 << k for k in range(1, nd.bit_length() - 1)]
        routes = [bits + [1], bits[::-1] + [1]]
        have = [[0] for _ in halves]
        for stage in range(len(bits) + 1):
            copies = []
            for h, (lo, hi) in enumerate(halves):
                bit = routes[h][stage]
                for k, mask in enumerate(have[h]):
                    slab = d
                    for b in [1 << j for j in range(nd.bit_length() - 1)]:
                        if mask & b:
                            slab = flip(slab, b)
                    ref = wg_s.at[slab, :, pl.ds(lo, hi - lo)]
                    copies.append(
                        remote(ref, ref, w_send.at[1 + h, stage, k], w_recv.at[1 + h, stage, k], (flip(d, bit), t))
                    )
                have[h] = have[h] + [mask | bit for mask in have[h]]
            for copy in copies:
                copy.start()
            for copy in copies:
                copy.wait()

        gains = jnp.zeros((8, width), F32)
        for pair in range(nd * nt // 2):
            slabs = [wg_s[(2 * pair + e) // nt, (2 * pair + e) % nt].astype(F32) for e in range(2)]
            for k in range(3):
                both = jnp.concatenate([slab[k * share : (k + 1) * share] for slab in slabs])
                w_out[2 * pair * share : 2 * (pair + 1) * share, k * width : (k + 1) * width] = both.astype(BF16)
            both = jnp.concatenate([slab[3 * share : 4 * share] for slab in slabs])
            o_out[2 * pair * share : 2 * (pair + 1) * share, :] = both.astype(BF16)
            gains = gains + (slabs[0] + slabs[1])[4 * share : 4 * share + 8]
        gain_out[...] = gains

    kv_copies = []
    gain = gain_out[:1]
    for s in range(nt):
        source = lax.rem(t + s, nt)
        here = (source == t) & holder
        arrival = remote(
            x_s.at[pl.ds(per * source, per)], x_s.at[pl.ds(per * source, per)], x_send.at[0], x_recv.at[source], (flip(d, 1), t)
        )
        local = pltpu.make_async_copy(tokens.at[0, :, 0], x_s.at[pl.ds(per * source, per)], x_self)
        pl.when(jnp.logical_not(here))(arrival.wait_recv)
        pl.when(here)(local.wait)
        x = x_s[pl.ds(per * source, per)].reshape(per * BLOCK, width)
        rows = pl.ds(pl.multiple_of(source * per * BLOCK, per * BLOCK), per * BLOCK)
        x_out[rows, :] = x
        x = x.astype(F32)
        h = (x * rms_scale(x) * gain).astype(BF16)
        q_out[rows, :] = matmul(h, w_out[:, :width]).astype(BF16)
        for k, out in enumerate((k_out, v_out)):
            value = matmul(h, w_out[:, (k + 1) * width : (k + 2) * width]).astype(BF16)
            kv_s[k, s] = value.reshape(per, BLOCK, width)
            dst = out.at[pl.ds(per * source, per), core]
            near = pltpu.make_async_copy(kv_s.at[k, s], dst, kv_self.at[k, s])
            far = remote(kv_s.at[k, s], dst, kv_send.at[k, s], kv_recv.at[k, s], (flip(d, 1), t))
            near.start()
            far.start()
            kv_copies += [near, far]
    for copy in kv_copies + l_copies + g_copies:
        copy.wait()
    for here, far, near in sends:
        pl.when(jnp.logical_not(here))(far.wait_send)

    @pl.when(holder)
    def _():
        seg_here.wait()
        seg_there.wait_send()

    @pl.when(jnp.logical_not(holder))
    def _():
        seg_there.wait_recv()


def start(tokens, grads, segments, weights, norms, later):
    micro, _, rows, width = tokens.shape
    nd, nt = 2 * lax.axis_size("plane"), lax.axis_size("tensor")
    count = rows * nt // 2
    blocks = count // BLOCK
    per = blocks // nt
    share = weights[0].shape[0]
    length = 4 * share + 8 + -(4 * share + 8) % 16
    dma = pltpu.SemaphoreType.DMA
    vmem = pl.BlockSpec(memory_space=pltpu.VMEM)
    shaped = jax.ShapeDtypeStruct
    most = max(nd // 2, nt)
    inside = 2 * share % 16 == 0 and length >= 32
    middle = length // 32 * 16
    if inside:
        halves, given = [(0, middle), (middle, length)], [*weights, jnp.stack(norms).astype(F32)]
        given_specs = [vmem] * 4 + [SCALARS]
        gathered_specs = [vmem, vmem, vmem]
        gathered = [shaped((width, 3 * width), BF16), shaped((width, width), BF16), shaped((8, width), F32)]
        scratch = [
            pltpu.VMEM((nd, nt, length, width), BF16),
            dma((3, nd.bit_length(), most)), dma((3, nd.bit_length(), most)),
        ]
    else:
        place = (lax.axis_index("plane") * 2 * nt + lax.axis_index("core") * nt + lax.axis_index("tensor")) * share
        gains = lax.dynamic_update_slice(jnp.zeros((8, width), BF16), jnp.stack(norms), (0, place))
        slabs = lax.all_gather(jnp.concatenate([*weights, gains]), AXES, axis=0, tiled=False)
        w_qkv = slabs[:, : 3 * share].reshape(nd * nt, 3, share, width).transpose(0, 2, 1, 3)
        w_qkv = w_qkv.reshape(width, 3 * width)
        w_out = slabs[:, 3 * share : 4 * share].reshape(width, width)
        gains = jnp.sum(slabs[:, 4 * share : 4 * share + 8].astype(F32), axis=0)
        halves, given, given_specs, gathered_specs, gathered, scratch = [], [w_qkv, gains], [vmem, vmem], [], [], []
    results = pl.pallas_call(
        functools.partial(start_kernel, nd, nt, share, halves),
        in_specs=[ANY, ANY, ANY, ANY] + given_specs,
        out_specs=[vmem, vmem, ANY, ANY, ANY, vmem, ANY] + gathered_specs,
        out_shape=[
            shaped((count, width), BF16),
            shaped((count, width), BF16),
            shaped((blocks, 2, BLOCK, width), BF16),
            shaped((blocks, 2, BLOCK, width), BF16),
            shaped((2 * blocks, BLOCK), jnp.int32),
            shaped((nt, per, BLOCK, width), BF16),
            shaped((nt - 1,) + later.shape, BF16),
            *gathered,
        ],
        scratch_shapes=scratch + [
            dma((micro,)), dma((micro,)), dma((micro,)),
            dma((nt,)), dma((nt,)),
            pltpu.VMEM((blocks, BLOCK, width), BF16),
            pltpu.VMEM((2, nt, per, BLOCK, width), BF16),
            dma((nt,)), dma((nt,)), dma,
            dma((2, nt)), dma((2, nt)), dma((2, nt)),
            dma, dma, dma,
        ],
        compiler_params=pltpu.CompilerParams(
            collective_id=0, has_side_effects=True, vmem_limit_bytes=62 << 20
        ),
        name="start",
    )(
        tokens.reshape(micro, rows // TILE, 2, BLOCK, width),
        grads.reshape(micro, rows // TILE, 2, BLOCK, width),
        segments.reshape(micro, 2 * blocks, BLOCK),
        later,
        *given,
    )
    return results if inside else (*results, w_qkv, w_out, gains)


def gelu_parts(v):
    t = 1.0 / (1.0 + 0.23164189 * jnp.abs(v))
    bell = jnp.exp(-0.5 * v * v)
    series = t * (0.127414796 + t * (-0.142248368 + t * (0.7107068705 + t * (-0.7265760135 + t * 0.5307027145))))
    tail = series * bell
    return jnp.where(v < 0.0, tail, 1.0 - tail), 0.3989422804 * bell


def middle_kernel(rb, nd, nt, share, inside, *refs):
    x_ref, att_ref, w_out, gain_ref, own_ref, rest_ref, dy_all = refs[:7]
    out_ref, after_ref, datt_ref, dwo_ref, dgain_ref, part_ref = refs[7:13]
    dy_ref, h_s, ht_s, dyt_s, o_s, dh_s, hid_s, dhid_s, w_s, dy_sem = refs[13:23]
    if inside:
        g_s, core_s, plane_s, c_send, c_recv, p_send, p_recv = refs[23:]
    step = pl.program_id(0)
    d, t = 2 * lax.axis_index("plane") + lax.axis_index("core"), lax.axis_index("tensor")
    count, width = x_ref.shape
    parts = range(0, count, rb)
    bits = [1 << k for k in range(1, nd.bit_length() - 1)]
    routes = [bits, bits[::-1]]

    @pl.when(step == 0)
    def _():
        if inside:
            greet(nd, nt, d, t)
        dy_copy = pltpu.make_async_copy(dy_all, dy_ref, dy_sem)
        dy_copy.start()
        for r in parts:
            rows = slice(r, r + rb)
            after = x_ref[rows, :].astype(F32) + matmul(att_ref[rows, :], w_out[...])
            after_ref[rows, :] = after
            o_s[rows, :] = after
            h = (after * rms_scale(after) * gain_ref[...]).astype(BF16)
            h_s[rows, :] = h
            ht_s[:, rows] = h.T
            dh_s[rows, :] = jnp.zeros((rb, width), F32)
        for k in range(2):
            w_s[k] = own_ref[:, k * share : (k + 1) * share]
        dy_copy.wait()
        for r in parts:
            rows = slice(r, r + rb)
            dyt_s[:, rows] = dy_ref[rows, :].T

    @pl.when((step > 0) & (step < nt))
    def _():
        for k in range(2):
            w_s[k] = rest_ref[:, 0, k * share : (k + 1) * share]

    def core_copies(slot):
        return [
            remote(
                g_s.at[slot, flips(flip(d, 1), mask)], core_s.at[slot, j],
                c_send.at[slot, j], c_recv.at[slot, j], (flip(d, 1), t),
            )
            for j, mask in enumerate(masks_of(bits))
        ]

    def plane_copies(slot, stage):
        copies = []
        for h in range(2):
            bit, rows = routes[h][stage], pl.ds(h * share, share)
            for j, mask in enumerate(masks_of(routes[h][stage + 1 :])):
                copies.append(
                    remote(
                        g_s.at[slot, flips(flip(d, bit), mask), rows], plane_s.at[slot, stage, j, rows],
                        p_send.at[slot, stage, h, j], p_recv.at[slot, stage, h, j], (flip(d, bit), t),
                    )
                )
        return copies

    def core_done(k):
        slot = lax.rem(k, 2)
        for copy in core_copies(slot):
            copy.wait()
        for j, mask in enumerate(masks_of(bits)):
            mine = flips(d, mask)
            g_s[slot, mine] = (g_s[slot, mine].astype(F32) + core_s[slot, j].astype(F32)).astype(BF16)
        for copy in plane_copies(slot, 0):
            copy.start()

    def plane_done(k, stage):
        slot = lax.rem(k, 2)
        for copy in plane_copies(slot, stage):
            copy.wait()
        for h in range(2):
            rows = slice(h * share, (h + 1) * share)
            for j, mask in enumerate(masks_of(routes[h][stage + 1 :])):
                mine = flips(d, mask)
                total = g_s[slot, mine, rows].astype(F32) + plane_s[slot, stage, j, rows].astype(F32)
                g_s[slot, mine, rows] = total.astype(BF16)
        if stage + 1 < len(bits):
            for copy in plane_copies(slot, stage + 1):
                copy.start()
        else:
            part_ref[lax.rem(t + nt - k, nt)] = g_s[slot, d]

    def when(condition, stage, *args):
        if inside:
            pl.when(condition)(functools.partial(stage, *args))

    @pl.when(step < nt)
    def _():
        up, down = (w_s[k].reshape(width, -1) for k in range(2))
        for point, r in enumerate(parts):
            rows = slice(r, r + rb)
            v = matmul(h_s[rows, :], up)
            cumulative, density = gelu_parts(v)
            hid_s[rows, :] = (v * cumulative).astype(BF16)
            d_hidden = matmul(dy_ref[rows, :], down) * (cumulative + v * density)
            dhid_s[rows, :] = d_hidden.astype(BF16)
            if point == 1:
                when(step >= 1, core_done, step - 1)
        when(step >= 2, plane_done, step - 2, len(bits) - 1)
        slot = lax.rem(step, 2)
        for r in range(0, width, 2 * share):
            rows = slice(r, r + 2 * share)
            for k, (left, right) in enumerate(((ht_s, dhid_s), (dyt_s, hid_s))):
                both = matmul(left[rows, :], right[...]).astype(BF16)
                for e in range(2):
                    grad = both[e * share : (e + 1) * share]
                    if inside:
                        g_s[slot, r // share + e, k * share : (k + 1) * share] = grad
                    else:
                        part_ref[r // share + e, 0, k] = grad
        if inside:
            for copy in core_copies(slot):
                copy.start()
        for r in parts:
            rows = slice(r, r + rb)
            o_s[rows, :] += right_t(hid_s[rows, :], down)
            dh_s[rows, :] += right_t(dhid_s[rows, :], up)
        for stage in range(len(bits) - 1):
            when(step >= 1, plane_done, step - 1, stage)

    @pl.when(step == nt)
    def _():
        gain = gain_ref[...]
        total = jnp.zeros((8, width), F32)
        out_ref[...] = o_s[...].astype(BF16)
        for point, r in enumerate(parts):
            rows = slice(r, r + rb)
            after = after_ref[rows, :]
            scale = rms_scale(after)
            normed = after * scale
            dh = dh_s[rows, :]
            total = total + jnp.sum((dh * normed).reshape(rb // 8, 8, width), axis=0)
            d_after = dy_ref[rows, :].astype(F32) + rms_back(dh, normed, scale, gain)
            after_ref[rows, :] = d_after
            branch = d_after.astype(BF16)
            hid_s[rows, :] = branch
            datt_ref[rows, :] = right_t(branch, w_out[...]).astype(BF16)
            if inside and point == 0:
                core_done(nt - 1)
        if inside:
            plane_done(step - 2, len(bits) - 1)
        dgain_ref[...] = total
        if inside:
            for stage in range(len(bits) - 1):
                plane_done(nt - 1, stage)
        dwo_ref[...] = left_t(att_ref[...], hid_s[...]).astype(BF16)
        if inside:
            plane_done(nt - 1, len(bits) - 1)


def feed_forward(x, attended, dy, w_out, gain, own, rest):
    count, width = x.shape
    nd, nt, units = own.shape[0], rest.shape[1] + 1, own.shape[2]
    share = own.shape[1] // 2
    inside = share % 16 == 0 and nd >= 8
    rb = 256
    rows = whole((count, width))
    dma = pltpu.SemaphoreType.DMA
    scratch = [
        pltpu.VMEM((count, width), BF16),
        pltpu.VMEM((count, width), BF16),
        pltpu.VMEM((width, count), BF16),
        pltpu.VMEM((width, count), BF16),
        pltpu.VMEM((count, width), F32),
        pltpu.VMEM((count, width), F32),
        pltpu.VMEM((count, units), BF16),
        pltpu.VMEM((count, units), BF16),
        pltpu.VMEM((2, nd, share, units), BF16),
        dma,
    ]
    if inside:
        stages = nd.bit_length() - 2
        grads, grads_spec = jax.ShapeDtypeStruct((nt, 2 * share, units), BF16), whole((nt, 2 * share, units))
        scratch += [
            pltpu.VMEM((2, nd, 2 * share, units), BF16),
            pltpu.VMEM((2, nd // 2, 2 * share, units), BF16),
            pltpu.VMEM((2, stages, nd // 4, 2 * share, units), BF16),
            dma((2, nd // 2)), dma((2, nd // 2)),
            dma((2, stages, 2, nd // 4)), dma((2, stages, 2, nd // 4)),
        ]
        params = dict(collective_id=2, has_side_effects=True)
    else:
        grads = jax.ShapeDtypeStruct((nd, nt, 2, share, units), BF16)
        grads_spec = pl.BlockSpec((nd, 1, 2, share, units), lambda s: (0, jnp.minimum(s, nt - 1), 0, 0, 0))
        params = {}
    return pl.pallas_call(
        functools.partial(middle_kernel, rb, nd, nt, share, inside),
        grid=(nt + 1,),
        in_specs=[
            rows, rows, whole((width, width)), whole((1, width)), whole(own.shape),
            pl.BlockSpec((nd, 1, 2 * share, units), lambda s: (0, jnp.clip(s - 1, 0, nt - 2), 0, 0)),
            ANY,
        ],
        out_specs=[rows, rows, rows, whole((width, width)), whole((8, width)), grads_spec],
        out_shape=[
            jax.ShapeDtypeStruct((count, width), BF16),
            jax.ShapeDtypeStruct((count, width), F32),
            jax.ShapeDtypeStruct((count, width), BF16),
            jax.ShapeDtypeStruct((width, width), BF16),
            jax.ShapeDtypeStruct((8, width), F32),
            grads,
        ],
        scratch_shapes=scratch,
        compiler_params=pltpu.CompilerParams(vmem_limit_bytes=62 << 20, **params),
        cost_estimate=cost(12 * count * width * nt * units, 4 * nd * nt * share * units),
        name="feed_forward",
    )(x, attended, w_out, gain, own, rest, dy)


def masks_of(bits):
    masks = [0]
    for bit in bits:
        masks = masks + [mask | bit for mask in masks]
    return masks


def flips(index, mask):
    bit = 1
    while bit <= mask:
        if mask & bit:
            index = flip(index, bit)
        bit *= 2
    return index


def finish_kernel(
    nd, nt, share, inside, x_all, dq_all, dk_all, dv_all, after_all, w_all, gain_ref, dwo_all, small_ref,
    ffn_ref, back, *refs,
):
    tok_out, out_out, dw_out, small_out = refs[:4]
    own_s, other_s, grads_s, ht_s, tok_s, own_sems, kv_send, kv_recv, tok_send, tok_recv, tok_self = refs[4:15]
    b_send, b_recv, b_self, x_ref, dq_ref, after_ref, w_ref, dwo_ref, in_sems = refs[15:24]
    if inside:
        slab_s, core_s, plane_s, mine_s, z_s, sm_s, sm_in, g_send, g_recv, s_send, s_recv = refs[24:]
    d, t = 2 * lax.axis_index("plane") + lax.axis_index("core"), lax.axis_index("tensor")
    core = d % 2
    count, width = x_all.shape
    per = tok_out.shape[1]
    rows_in = per * BLOCK
    holder = t % 2 == core
    bits = [1 << k for k in range(1, nd.bit_length() - 1)]
    loads = [
        pltpu.make_async_copy(far, near, in_sems.at[k])
        for k, (far, near) in enumerate(
            ((dq_all, dq_ref), (w_all, w_ref), (x_all, x_ref), (after_all, after_ref), (dwo_all, dwo_ref))
        )
    ]
    own = [pltpu.make_async_copy(a.at[:, core], own_s.at[k], own_sems.at[k]) for k, a in enumerate((dk_all, dv_all))]
    for copy in own + loads:
        copy.start()
    greet(nd, nt, d, t)

    order = [lax.rem(t + s, nt) for s in list(range(1, nt)) + [0]]
    exchanged = []
    for s, source in enumerate(order):
        pair = []
        for k, a in enumerate((dk_all, dv_all)):
            pair.append(
                remote(
                    a.at[pl.ds(per * source, per), 1 - core], other_s.at[k, pl.ds(per * source, per)],
                    kv_send.at[k, s], kv_recv.at[k, s], (flip(d, 1), t),
                )
            )
        exchanged.append(pair)
    for copy in exchanged[0] + exchanged[1]:
        copy.start()
    b_copies = []
    for m in range(out_out.shape[0]):
        there = out_out.at[m, :, core]
        b_copies.append(pltpu.make_async_copy(back.at[2 * m + core], there, b_self.at[m]))
        b_copies.append(remote(back.at[2 * m + 1 - core], there, b_send.at[m], b_recv.at[m], (flip(d, 1), t)))
    gain = gain_ref[:1]

    def norms(rows):
        x = x_ref[rows, :].astype(F32)
        scale = rms_scale(x)
        return x * scale, scale

    routes = [[1] + bits, [1] + bits[::-1]]
    rows_of_slab = width // nd

    def fill(bundle, which, left, right):
        for k in range(nd):
            lines = slice(k * rows_of_slab, (k + 1) * rows_of_slab)
            if k % 2 == 0:
                both = matmul(left[lines.start : lines.stop + rows_of_slab, :], right)
                slab_s[bundle, which, k : k + 2] = both.astype(BF16).reshape(2, rows_of_slab, width)

    def stage_copies(bundle, stage):
        copies, adds = [], []
        for h in range(2):
            bit = routes[h][stage]
            for k, mask in enumerate(masks_of(routes[h][stage + 1 :])):
                buffer = core_s.at[bundle] if stage == 0 else plane_s.at[bundle, stage - 1]
                copies.append(
                    remote(
                        slab_s.at[bundle, h, flips(flip(d, bit), mask)], buffer.at[h, k],
                        g_send.at[bundle, h, stage, k], g_recv.at[bundle, h, stage, k], (flip(d, bit), t),
                    )
                )
                adds.append((h, flips(d, mask), buffer, k))
        return copies, adds

    def stage_start(bundle, stage):
        for copy in stage_copies(bundle, stage)[0]:
            copy.start()

    def stage_done(bundle, stage):
        copies, adds = stage_copies(bundle, stage)
        for copy in copies:
            copy.wait()
        last = stage == len(bits)
        totals = []
        for h, mine, buffer, k in adds:
            total = slab_s[bundle, h, mine].astype(F32) + buffer[h, k].astype(F32)
            if last:
                totals.append(total.reshape(nt, share, width))
            else:
                slab_s[bundle, h, mine] = total.astype(BF16)
        if last:
            mine_s[bundle] = jnp.concatenate(totals, axis=1).astype(BF16)

    def z_copies(bundle):
        copies = []
        for s in range(1, nt):
            to = lax.rem(t + s, nt)
            copies.append(
                remote(
                    mine_s.at[bundle, to], z_s.at[bundle, s],
                    g_send.at[bundle, 2, 0, s], g_recv.at[bundle, 2, 0, s], (d, to),
                )
            )
        return copies

    def small_copies(stage):
        if stage <= len(bits):
            return [remote(sm_s, sm_in.at[stage], s_send.at[stage], s_recv.at[stage], (flip(d, routes[0][stage]), t))]
        copies = []
        for s in range(1, nt):
            k = len(bits) + s
            copies.append(remote(sm_s, sm_in.at[k], s_send.at[k], s_recv.at[k], (d, lax.rem(t + s, nt))))
        return copies

    sends, gains = [], []
    to_core = d - core + t % 2

    def sum_group(s):
        source = order[s]
        for copy in exchanged[s]:
            copy.wait()
        for copy in exchanged[s + 2] if s + 2 < nt else []:
            copy.start()
        rows = pl.ds(pl.multiple_of(source * rows_in, rows_in), rows_in)
        grads_s[rows, :width] = dq_ref[rows, :]
        for k in range(2):
            total = own_s[k, pl.ds(per * source, per)].astype(F32) + other_s[k, pl.ds(per * source, per)].astype(F32)
            grads_s[rows, (k + 1) * width : (k + 2) * width] = total.reshape(rows_in, width).astype(BF16)

    def token_group(s):
        source = order[s]
        rows = pl.ds(pl.multiple_of(source * rows_in, rows_in), rows_in)
        dh = right_t(grads_s[rows, :], w_ref[...])
        normed, scale = norms(rows)
        gains.append(jnp.sum((dh * normed).reshape(rows_in // 8, 8, width), axis=0))
        tok = after_ref[rows, :] + rms_back(dh, normed, scale, gain)
        tok_s[s] = tok.astype(BF16).reshape(per, BLOCK, width)
        here = (source == t) & holder
        dst = tok_out.at[t // 2, :, core]
        far = remote(tok_s.at[s], dst, tok_send.at[s], tok_recv.at[2 * (t // 2) + core], (to_core, source))
        near = pltpu.make_async_copy(tok_s.at[s], dst, tok_self)
        pl.when(jnp.logical_not(here))(far.start)
        pl.when(here)(near.start)
        sends.append((here, far, near))

    for copy in own + loads:
        copy.wait()
    for r in range(0, count, rows_in):
        lines = slice(r, r + rows_in)
        normed, scale = norms(lines)
        ht_s[:, lines] = (normed * gain).astype(BF16).T
    if inside:
        slab_s[0, 1] = dwo_ref[...].reshape(nd, rows_of_slab, width)
        fill(0, 0, ht_s, dq_ref[...])
        stage_start(0, 0)
    for s in range(nt // 2):
        sum_group(s)
        token_group(s)
    if inside:
        stage_done(0, 0)
        stage_start(0, 1)
    for s in range(nt // 2, nt):
        sum_group(s)
    if inside:
        for which in range(2):
            fill(1, which, ht_s, grads_s[:, (which + 1) * width : (which + 2) * width])
        stage_start(1, 0)
    for s in range(nt // 2, nt):
        token_group(s)

    for copy in b_copies:
        copy.start()
    small = small_ref[...]
    line = lax.broadcasted_iota(jnp.int32, small.shape, 0)
    small = small + jnp.where(line == small.shape[0] - 2, jnp.sum(sum(gains), axis=0, keepdims=True), 0.0)
    small = small + jnp.where(line == small.shape[0] - 1, jnp.sum(ffn_ref[...], axis=0, keepdims=True), 0.0)
    if inside:
        sm_s[...] = small
        tiny = small_copies(0)
        for copy in tiny:
            copy.start()
        for stage in range(len(bits) + 1):
            for copy in tiny:
                copy.wait()
            sm_s[...] += sm_in[stage]
            tiny = small_copies(stage + 1)
            for copy in tiny:
                copy.start()
            stage_done(1, stage)
            if stage < len(bits):
                stage_start(1, stage + 1)
                stage_done(0, stage + 1)
                if stage + 1 < len(bits):
                    stage_start(0, stage + 2)
                else:
                    first_z = z_copies(0)
                    for copy in first_z:
                        copy.start()
        second_z = z_copies(1)
        for copy in second_z:
            copy.start()
        for copy in first_z + second_z + tiny:
            copy.wait()
        for bundle in range(2):
            total = mine_s[bundle, t].astype(F32)
            for s in range(1, nt):
                total = total + z_s[bundle, s].astype(F32)
            dw_out[bundle * 2 * share : (bundle + 1) * 2 * share] = total
        small_out[...] = sm_s[...] + sum(sm_in[len(bits) + s] for s in range(1, nt))
    else:
        small_out[...] = small
        for r in range(0, width, 256):
            lines = slice(r, r + 256)
            dw_out[lines, : 3 * width] = matmul(ht_s[lines, :], grads_s[...]).astype(BF16)
            dw_out[lines, 3 * width :] = dwo_ref[lines, :]

    for copy in b_copies:
        copy.wait()
    for here, far, near in sends:
        pl.when(jnp.logical_not(here))(far.wait_send)
        pl.when(here)(near.wait)
    for m in range(tok_out.shape[0]):
        for c in range(2):
            here = (2 * m + core == t) & (c == core)
            dst = tok_out.at[m, :, c]
            back = remote(dst, dst, tok_send.at[0], tok_recv.at[2 * m + c], (flip(d, 1), t))
            pl.when(jnp.logical_not(here))(back.wait_recv)


def finish(x, dq, dk_all, dv_all, after, w_qkv, gains, dwo, small, gain_ffn, back, share, micro):
    count, width = x.shape
    nd, nt = 2 * lax.axis_size("plane"), lax.axis_size("tensor")
    inside = 2 * share % 16 == 0 and nd >= 8
    blocks = count // BLOCK
    per = blocks // nt
    dma = pltpu.SemaphoreType.DMA
    vmem = pl.BlockSpec(memory_space=pltpu.VMEM)
    shaped = jax.ShapeDtypeStruct
    scratch = [
        pltpu.VMEM((2, blocks, BLOCK, width), BF16),
        pltpu.VMEM((2, blocks, BLOCK, width), BF16),
        pltpu.VMEM((count, 3 * width), BF16),
        pltpu.VMEM((width, count), BF16),
        pltpu.VMEM((nt, per, BLOCK, width), BF16),
        dma((2,)), dma((2, nt)), dma((2, nt)), dma((nt,)), dma((nt,)), dma,
        dma((micro,)), dma((micro,)), dma((micro,)),
        pltpu.VMEM(x.shape, x.dtype), pltpu.VMEM(dq.shape, dq.dtype), pltpu.VMEM(after.shape, after.dtype),
        pltpu.VMEM(w_qkv.shape, w_qkv.dtype), pltpu.VMEM(dwo.shape, dwo.dtype), dma((5,)),
    ]
    if inside:
        most = max(nd // 2, nt)
        stages = nd.bit_length() - 1
        scratch += [
            pltpu.VMEM((2, 2, nd, nt * share, width), BF16),
            pltpu.VMEM((2, 2, nd // 2, nt * share, width), BF16),
            pltpu.VMEM((2, stages - 1, 2, nd // 4, nt * share, width), BF16),
            pltpu.VMEM((2, nt, 2 * share, width), BF16),
            pltpu.VMEM((2, nt, 2 * share, width), BF16),
            pltpu.VMEM(small.shape, F32),
            pltpu.VMEM((stages + nt,) + small.shape, F32),
            dma((2, 3, stages, most)), dma((2, 3, stages, most)), dma((stages + nt,)), dma((stages + nt,)),
        ]
    return pl.pallas_call(
        functools.partial(finish_kernel, nd, nt, share, inside),
        in_specs=[ANY, ANY, ANY, ANY, ANY, ANY, vmem, ANY, vmem, vmem, ANY],
        out_specs=[vmem, vmem, vmem, vmem],
        out_shape=[
            shaped((micro, per, 2, BLOCK, width), BF16),
            shaped((micro, per, 2, BLOCK, width), BF16),
            shaped((4 * share, width), F32) if inside else shaped((width, 4 * width), BF16),
            shaped(small.shape, F32),
        ],
        scratch_shapes=scratch,
        compiler_params=pltpu.CompilerParams(
            collective_id=1, has_side_effects=True, vmem_limit_bytes=62 << 20
        ),
        cost_estimate=cost(24 * count * width * width, 16 * count * width),
        name="finish",
    )(x, dq, dk_all, dv_all, after, w_qkv, gains, dwo, small, gain_ffn, back.reshape(nt, per, BLOCK, width))


def emit_kernel(heads, share, tok_ref, out_ref, dw_ref, ffn_ref, small_ref, tok, out, *rest):
    grads, ups, gains, mixes = rest[:4], rest[4:6], rest[6:8], rest[8:10]
    tok[...] = tok_ref[...].astype(F32)
    out[...] = out_ref[...]

    @pl.when(pl.program_id(0) == 0)
    def _():
        for grad, k in zip(grads, (0, 2, 3, 1)):
            grad[...] = dw_ref[k * share : (k + 1) * share]
        half = ffn_ref.shape[0] // 2
        for k, up in enumerate(ups):
            up[...] = ffn_ref[k * half : (k + 1) * half].astype(F32)
        width = small_ref.shape[1]
        place = (
            (lax.axis_index("plane") * 2 + lax.axis_index("core")) * lax.axis_size("tensor") + lax.axis_index("tensor")
        ) * share
        row = lax.broadcasted_iota(jnp.int32, (width, share), 0)
        col = lax.broadcasted_iota(jnp.int32, (width, share), 1)
        exact = dict(preferred_element_type=F32, precision=lax.Precision.HIGHEST)
        own = jnp.dot(small_ref[small_ref.shape[0] - 8 :, :], (row == place + col).astype(F32), **exact)
        for k, gain in enumerate(gains):
            gain[...] = own[6 + k : 7 + k]
        lines = 2 * heads * BLOCK // width
        sums = jnp.concatenate(
            [small_ref[:lines, k * BLOCK : (k + 1) * BLOCK] for k in range(width // BLOCK)]
        )[:, :heads]
        mixes[0][...] = sums[:heads].T * (width // heads) ** (-0.5)
        mixes[1][...] = sums[heads:]


def emit(tok, out, dw, ffn, small, heads, share):
    width = small.shape[1]
    micro, per, cores, block, _ = tok.shape
    rows = per * cores * block

    def part(k):
        return pl.BlockSpec((1, rows, width), lambda i: (i, 0, 0))

    shaped = jax.ShapeDtypeStruct
    small_shapes = [(share, width)] * 4 + [(ffn.shape[0] // 2, width)] * 2 + [(1, share)] * 2 + [(heads, heads)] * 2
    return pl.pallas_call(
        functools.partial(emit_kernel, heads, share),
        grid=(micro,),
        in_specs=[part(0), part(1), whole(dw.shape), whole(ffn.shape), whole(small.shape)],
        out_specs=[part(0), part(1)] + [whole(shape) for shape in small_shapes],
        out_shape=[shaped((micro, rows, width), F32), shaped((micro, rows, width), BF16)]
        + [shaped(shape, F32) for shape in small_shapes],
        compiler_params=pltpu.CompilerParams(vmem_limit_bytes=62 << 20),
        name="emit",
    )(tok.reshape(micro, rows, width), out.reshape(micro, rows, width), dw, ffn, small)


def per_device(
    tokens, segments, w_query, w_key, w_value, w_out, norm_attn, norm_ffn, pre_mix, post_mix, w_up, w_down, out_grad,
):
    micro, _, rows, width = tokens.shape
    nd, nt = 2 * lax.axis_size("plane"), lax.axis_size("tensor")
    heads = pre_mix.shape[0]
    head_width = width // heads
    length = rows * nt
    count = length // 2
    blocks = count // BLOCK
    share = w_query.shape[0]
    bits = [1 << k for k in range(nd.bit_length() - 1)]
    d, t = 2 * lax.axis_index("plane") + lax.axis_index("core"), lax.axis_index("tensor")
    core = d % 2

    later = jnp.concatenate([w_up, w_down])
    own_rows = lax.all_gather(later, ("plane", "core"), axis=0, tiled=False)
    x, query, k_all, v_all, segs, mail, later, w_qkv, all_out, gains = start(
        tokens, out_grad, segments, [w_query, w_key, w_value, w_out], [norm_attn, norm_ffn], later
    )
    k_all, v_all = (a.reshape(2 * blocks, BLOCK, width) for a in (k_all, v_all))
    dy = lax.all_to_all(mail, "tensor", 0, 0, tiled=True).reshape(count, width)
    rest_rows = lax.all_gather(later, ("plane", "core"), axis=0, tiled=False)

    def by_lane(mix):
        return jnp.repeat(mix.astype(F32), head_width, axis=1)

    pre = (by_lane(pre_mix.T) * head_width ** (-0.5)).astype(BF16)
    post = by_lane(post_mix)

    attended, u, lse = attend(query, k_all, v_all, segs, pre, post)
    output, grad_after, grad_attended, grad_w_out, grad_gain_ffn, part_both = feed_forward(
        x, attended, dy, all_out, gains[1:2], own_rows, rest_rows
    )
    back = lax.all_to_all(output.reshape(nt, count // nt, width), "tensor", 0, 0, tiled=True)
    if part_both.ndim > 3:
        part_both = lax.dynamic_slice_in_dim(jnp.concatenate([part_both[:, ::-1]] * 2, axis=1), nt - 1 - t, nt, 1)
        part_both = lax.psum_scatter(part_both, ("plane", "core"), scatter_dimension=0, tiled=False)
    part_both = lax.psum_scatter(part_both, "tensor", scatter_dimension=0, tiled=False)
    part_both = part_both.reshape(2 * w_up.shape[0], w_up.shape[1])

    grad_query, grad_key, grad_value, small = attend_back(
        query, grad_attended, u, lse, k_all, v_all, segs, pre, post
    )
    d_tokens, out, owned, small = finish(
        x, grad_query, grad_key.reshape(blocks, 2, BLOCK, width), grad_value.reshape(blocks, 2, BLOCK, width),
        grad_after, w_qkv, gains, grad_w_out, small, grad_gain_ffn, back, share, micro,
    )
    if owned.dtype == BF16:
        owned = lax.psum_scatter(owned, AXES, scatter_dimension=0, tiled=True).astype(F32)
        owned = jnp.concatenate([owned[:, k * width : (k + 1) * width] for k in (0, 3, 1, 2)])
        small = lax.psum(small, AXES)
    d_tokens, out, *grads = emit(d_tokens, out, owned, part_both, small, heads, share)
    d_query, d_key, d_value, d_out, d_up, d_down, d_gain_attn, d_gain_ffn, d_pre, d_post = grads
    return (
        out.reshape(tokens.shape),
        d_tokens.reshape(tokens.shape),
        d_query,
        d_key,
        d_value,
        d_out,
        d_gain_attn.reshape(share),
        d_gain_ffn.reshape(share),
        d_pre,
        d_post,
        d_up,
        d_down,
    )


def solution(mesh):
    devices = mesh.devices
    devices = devices.reshape(devices.shape[0] // 2, 2, devices.shape[1])
    dp = ("plane", "core")
    both = P(AXES, None)
    gain = P(AXES)
    data = P(None, dp, "tensor", None)
    ffn = P(dp, "tensor")
    return jax.shard_map(
        per_device,
        mesh=jax.sharding.Mesh(devices, AXES),
        in_specs=(data, P(None, dp, None), both, both, both, both, gain, gain, P(), P(), ffn, ffn, data),
        out_specs=(data, data, both, both, both, both, gain, gain, P(), P(), ffn, ffn),
        check_vma=False,
    )
```

```python
import functools

import jax
import jax.numpy as jnp
from jax import lax
from jax.experimental import pallas as pl
from jax.experimental.pallas import tpu as pltpu
from jax.sharding import PartitionSpec as P

F32 = jnp.float32
BF16 = jnp.bfloat16
BLOCK = 128
TILE = 2 * BLOCK
FORWARD_GROUPS = 6
BACKWARD_GROUPS = (2, 2, 2)
AXES = ("plane", "core", "tensor")


def matmul(left, right):
    return jnp.dot(left, right, preferred_element_type=F32)


def right_t(left, right):
    return lax.dot_general(left, right, (((1,), (1,)), ((), ())), preferred_element_type=F32)


def left_t(left, right):
    return lax.dot_general(left, right, (((0,), (0,)), ((), ())), preferred_element_type=F32)


def rms_scale(values):
    return lax.rsqrt(jnp.mean(values * values, axis=-1, keepdims=True) + 1e-06)


def rms_back(grad_norm, normed, scale, gain):
    scaled = grad_norm * gain
    return scale * (scaled - normed * jnp.mean(scaled * normed, axis=-1, keepdims=True))


def gelu_exact(values):
    return jax.nn.gelu(values, approximate=False)


def gelu_back(upper, grad):
    unused, pull = jax.vjp(gelu_exact, upper)
    return pull(grad)[0]


def send(x, to):
    nd, nt = 2 * lax.axis_size("plane"), lax.axis_size("tensor")
    pairs = []
    for d in range(nd):
        for t in range(nt):
            d2, t2 = to(d, t)
            pairs.append((d * nt + t, d2 * nt + t2))
    return lax.ppermute(x, AXES, pairs)


def by_shift(shift):
    nt = lax.axis_size("tensor")
    return lambda d, t: (d, (t + shift) % nt)


def by_bit(bit):
    return lambda d, t: (d ^ bit, t)


def gather(piece, bits):
    nt = lax.axis_size("tensor")
    have = {0: jnp.stack([piece] + [send(piece, by_shift(s)) for s in range(1, nt)])}
    for bit in bits:
        have.update({mask | bit: send(block, by_bit(bit)) for mask, block in have.items()})
    return [have[mask] for mask in range(len(have))]


def pick(x, index, axis):
    return lax.dynamic_index_in_dim(x, index, axis, keepdims=False)


def sum_to_owner(x, bits):
    nt, nd = x.shape[:2]
    d, t = 2 * lax.axis_index("plane") + lax.axis_index("core"), lax.axis_index("tensor")
    rest = x.shape[2:]
    names = [1 << k for k in range(nd.bit_length() - 1)][::-1]
    x = x.reshape((nt,) + (2,) * len(names) + rest)
    for bit in bits:
        axis = 1 + names.index(bit)
        names.remove(bit)
        mine = (d // bit) % 2
        got = send(pick(x, 1 - mine, axis), by_bit(bit))
        x = pick(x, mine, axis).astype(F32) + got.astype(F32)
        if names or nt > 1:
            x = x.astype(BF16)
    total = pick(x, t, 0).astype(F32)
    for shift in range(1, nt):
        total = total + send(pick(x, lax.rem(t + shift, nt), 0), by_shift(shift)).astype(F32)
    return total


def arrive(step, sources, scratches, sems, seg_ref, seg_s):
    blocks = sources[0].shape[0]
    copies = []
    for k, (source, scratch) in enumerate(zip(sources, scratches)):
        for part in range(blocks // 2):
            rows = pl.ds(2 * part, 2)
            there = scratch.at[pl.ds(2 * part + 1, 2)]
            copies.append((part, pltpu.make_async_copy(source.at[rows], there, sems.at[k, part])))

    @pl.when(step == 0)
    def _():
        for _, copy in copies:
            copy.start()
        seg_s[0] = jnp.full((1, BLOCK), -1, jnp.int32)
        seg_s[1:] = seg_ref[...]
        for scratch in scratches:
            scratch[0] = jnp.zeros(scratch.shape[1:], BF16)

    for part, copy in copies:
        pl.when(step == part)(copy.wait)


def reach(block, seg_low):
    first = seg_low[block, 0]
    before = 0
    for k in range(seg_low.shape[0]):
        before += (seg_low[k, BLOCK - 1] < first).astype(jnp.int32)
    return (block + 2 - before) // 2


def rows_of(block, seg_s):
    return jnp.broadcast_to(seg_s[block + 1], (BLOCK, BLOCK)).T


def row_mask(row_seg, first, block, seg_s):
    row = lax.broadcasted_iota(jnp.int32, (BLOCK, BLOCK), 0)
    col = lax.broadcasted_iota(jnp.int32, (BLOCK, BLOCK), 1)
    masks = []
    for k in range(2):
        ahead = (first + k - 1 - block) * BLOCK
        allowed = (row_seg == seg_s[first + k]) & (col + ahead <= row)
        masks.append(jnp.where(allowed, 0.0, -1e30).astype(F32))
    return jnp.concatenate(masks, axis=1)


def forward_kernel(
    heads, groups, most, q_ref, k_all, v_all, seg_low, seg_ref, pre_ref, post_ref,
    att_ref, u_ref, lse_ref, k_s, v_s, seg_s, qp_s, m_s, s_s, sems,
):
    step = pl.program_id(0)
    core = lax.axis_index("core")
    block = 2 * step + core
    width = q_ref.shape[1]
    arrive(step, [k_all, v_all], [k_s, v_s], sems, seg_ref, seg_s)
    tiles = reach(block, seg_low)
    row_seg = rows_of(block, seg_s)

    def scores(left, first, mask):
        keys = k_s[pl.ds(first, 2)].reshape(TILE, -1)
        s = right_t(left, keys).reshape(left.shape[0] // BLOCK, BLOCK, TILE)
        return (s + mask[None]).reshape(left.shape[0], TILE)

    def close(g, per, top, total, u, att):
        size = per * BLOCK
        lse_ref[0, g * size : (g + 1) * size, :] = jnp.broadcast_to(top + jnp.log(total), (size, BLOCK))
        for k in range(per):
            h = g * per + k
            part = u[k * BLOCK : (k + 1) * BLOCK]
            u_ref[0, h] = part.astype(BF16)
            att = att + part * post_ref[h : h + 1, :]
        return att

    @pl.when(tiles == 1)
    def _():
        per = heads // groups
        query = q_ref[...]
        mask = row_mask(row_seg, block, block, seg_s)
        att = jnp.zeros((BLOCK, width), F32)
        values = v_s[pl.ds(block, 2)].reshape(TILE, -1)
        for g in range(groups):
            left = jnp.concatenate([query * pre_ref[h : h + 1, :] for h in range(g * per, (g + 1) * per)])
            s = scores(left, block, mask)
            top = jnp.max(s, axis=-1, keepdims=True)
            p = jnp.exp(s - top)
            total = jnp.sum(p, axis=-1, keepdims=True)
            u = matmul((p * (1.0 / total)).astype(BF16), values)
            att = close(g, per, top, total, u, att)
        att_ref[...] = att.astype(BF16)

    @pl.when(tiles > 1)
    def _():
        query = q_ref[...]
        for h in range(heads):
            qp_s[h * BLOCK : (h + 1) * BLOCK, :] = query * pre_ref[h : h + 1, :]
        m_s[...] = jnp.full(m_s.shape, -3e38, F32)
        split = 2
        size = heads // split * BLOCK

        def meet(tile, carry):
            first = block - 2 * tile
            mask = row_mask(row_seg, first, block, seg_s)
            for g in range(split):
                rows = slice(g * size, (g + 1) * size)
                s = scores(qp_s[rows, :], first, mask)
                s_s[tile, rows, :] = s
                m_s[rows, :] = jnp.maximum(m_s[rows, :], jnp.maximum(s[:, :BLOCK], s[:, BLOCK:]))
            return carry

        lax.fori_loop(0, tiles, meet, 0)

    for n in range(2, most + 1):

        @pl.when(tiles == n)
        def _(n=n):
            per = heads // groups
            size = per * BLOCK
            values = v_s[pl.ds(block - 2 * n + 2, 2 * n)].reshape(n * TILE, -1)
            att = jnp.zeros((BLOCK, width), F32)
            for g in range(groups):
                rows = slice(g * size, (g + 1) * size)
                top = jnp.max(m_s[rows, :], axis=-1, keepdims=True)
                parts = [jnp.exp(s_s[tile, rows, :] - top) for tile in range(n)]
                total = jnp.sum(sum(p[:, :BLOCK] + p[:, BLOCK:] for p in parts), axis=-1, keepdims=True)
                p = jnp.concatenate([part.astype(BF16) for part in parts[::-1]], axis=1)
                u = matmul(p, values) * (1.0 / total)
                att = close(g, per, top, total, u, att)
            att_ref[...] = att.astype(BF16)


def whole(shape):
    return pl.BlockSpec(shape, lambda i: (0,) * len(shape), pipeline_mode=pl.Buffered(1))


def cost(flops, moved):
    return pl.CostEstimate(flops=int(flops), bytes_accessed=int(moved), transcendentals=0)


ANY = pl.BlockSpec(memory_space=pl.ANY)
SCALARS = pl.BlockSpec(memory_space=pltpu.SMEM)


def attend(query, k_all, v_all, segs, pre, post):
    heads, width = pre.shape
    rows, stack = query.shape[0], heads * BLOCK
    blocks = rows // BLOCK
    groups = FORWARD_GROUPS
    most = (1024 // BLOCK + 2) // 2
    by_block = pl.BlockSpec((BLOCK, width), lambda i: (i, 0))
    return pl.pallas_call(
        functools.partial(forward_kernel, heads, groups, most),
        grid=(blocks,),
        in_specs=[
            by_block, ANY, ANY, SCALARS, whole((2 * blocks, 1, BLOCK)), whole(pre.shape), whole(post.shape),
        ],
        out_specs=[
            by_block,
            pl.BlockSpec((1, heads, BLOCK, width), lambda i: (i, 0, 0, 0)),
            pl.BlockSpec((1, stack, BLOCK), lambda i: (i, 0, 0)),
        ],
        scratch_shapes=[
            pltpu.VMEM((2 * blocks + 1, BLOCK, width), BF16),
            pltpu.VMEM((2 * blocks + 1, BLOCK, width), BF16),
            pltpu.VMEM((2 * blocks + 1, 1, BLOCK), jnp.int32),
            pltpu.VMEM((stack, width), BF16),
            pltpu.VMEM((stack, BLOCK), F32),
            pltpu.VMEM((most, stack, TILE), F32),
            pltpu.SemaphoreType.DMA((2, blocks)),
        ],
        out_shape=[
            jax.ShapeDtypeStruct((rows, width), BF16),
            jax.ShapeDtypeStruct((blocks, heads, BLOCK, width), BF16),
            jax.ShapeDtypeStruct((blocks, stack, BLOCK), F32),
        ],
        compiler_params=pltpu.CompilerParams(vmem_limit_bytes=62 << 20),
        cost_estimate=cost(4 * rows * 1024 * stack // BLOCK * width, 4 * rows * stack // BLOCK * width),
        name="attend",
    )(query, k_all, v_all, segs, segs[:, None, :], pre, post)


def backward_kernel(
    heads, groups, q_ref, g_ref, u_ref, lse_ref, k_all, v_all, seg_low, seg_ref, pre_ref, post_ref,
    dq_ref, dk_ref, dv_ref, small_ref,
    dpre_ref, dpost_ref, k_s, v_s, seg_s, dk_s, dv_s, qp_s, gp_s, d_s, t_s, sems,
):
    step = pl.program_id(0)
    core = lax.axis_index("core")
    block = 2 * step + core
    width = q_ref.shape[1]
    arrive(step, [k_all, v_all], [k_s, v_s], sems, seg_ref, seg_s)

    @pl.when(step == 0)
    def _():
        dk_s[...] = jnp.zeros(dk_s.shape, F32)
        dv_s[...] = jnp.zeros(dv_s.shape, F32)
        dpre_ref[...] = jnp.zeros(dpre_ref.shape, F32)
        dpost_ref[...] = jnp.zeros(dpost_ref.shape, F32)

    tiles = reach(block, seg_low)
    row_seg = rows_of(block, seg_s)

    def opening(g, per):
        query, grad_low = q_ref[...], g_ref[...]
        grad = grad_low.astype(F32)
        left, right, terms = [], [], []
        for h in range(g * per, (g + 1) * per):
            gain = post_ref[h : h + 1, :]
            left.append(query * pre_ref[h : h + 1, :])
            right.append(grad_low * gain.astype(BF16))
            both = grad * u_ref[0, h].astype(F32)
            terms.append(jnp.sum(both * gain, axis=-1, keepdims=True))
            dpost_ref[h] += jnp.sum(both.reshape(BLOCK // 8, 8, -1), axis=0)
        return jnp.concatenate(left), jnp.concatenate(right), jnp.concatenate(terms)

    def closing(h, part, dq):
        dpre_ref[h] += jnp.sum((q_ref[...].astype(F32) * part).reshape(BLOCK // 8, 8, -1), axis=0)
        return dq + part * pre_ref[h : h + 1, :].astype(F32)

    def tile_part(first, mask, g, left, right, term):
        size = left.shape[0]
        per = size // BLOCK
        keys = k_s[pl.ds(first, 2)].reshape(TILE, -1)
        values = v_s[pl.ds(first, 2)].reshape(TILE, -1)
        s = (right_t(left, keys).reshape(per, BLOCK, TILE) + mask[None]).reshape(size, TILE)
        top = lse_ref[0, g * size : (g + 1) * size, :]
        p = jnp.exp(s - jnp.concatenate([top, top], axis=1))
        dw = right_t(right, values)
        ds = (p * (dw - term)).astype(BF16)
        return matmul(ds, keys), left_t(ds, left), left_t(p.astype(BF16), right)

    def add_up(first, dk, dv):
        dk_s[pl.ds(first, 2)] += dk.reshape(2, BLOCK, -1)
        dv_s[pl.ds(first, 2)] += dv.reshape(2, BLOCK, -1)

    @pl.when(tiles == 1)
    def _():
        mask = row_mask(row_seg, block, block, seg_s)
        dk = dv = jnp.zeros((TILE, width), F32)
        dq = jnp.zeros((BLOCK, width), F32)
        per = heads // groups[0]
        for g in range(groups[0]):
            part, a, b = tile_part(block, mask, g, *opening(g, per))
            dk, dv = dk + a, dv + b
            for k in range(per):
                dq = closing(g * per + k, part[k * BLOCK : (k + 1) * BLOCK], dq)
        add_up(block, dk, dv)
        dq_ref[...] = dq.astype(BF16)

    @pl.when(tiles > 1)
    def _():
        mask = row_mask(row_seg, block, block, seg_s)
        dk = dv = jnp.zeros((TILE, width), F32)
        per = heads // groups[1]
        size = per * BLOCK
        for g in range(groups[1]):
            rows = slice(g * size, (g + 1) * size)
            left, right, term = opening(g, per)
            qp_s[rows, :], gp_s[rows, :] = left, right
            d_s[rows, :] = jnp.broadcast_to(term, (size, BLOCK))
            t_s[rows, :], a, b = tile_part(block, mask, g, left, right, term)
            dk, dv = dk + a, dv + b
        add_up(block, dk, dv)

        def more(tile, carry):
            first = block - 2 * tile
            mask = row_mask(row_seg, first, block, seg_s)
            dk = dv = jnp.zeros((TILE, width), F32)
            size = heads // groups[2] * BLOCK
            for g in range(groups[2]):
                rows = slice(g * size, (g + 1) * size)
                term = jnp.concatenate([d_s[rows, :]] * 2, axis=1)
                part, a, b = tile_part(first, mask, g, qp_s[rows, :], gp_s[rows, :], term)
                t_s[rows, :] += part
                dk, dv = dk + a, dv + b
            add_up(first, dk, dv)
            return carry

        lax.fori_loop(1, tiles, more, 0)
        dq = jnp.zeros((BLOCK, width), F32)
        for h in range(heads):
            dq = closing(h, t_s[h * BLOCK : (h + 1) * BLOCK, :], dq)
        dq_ref[...] = dq.astype(BF16)

    @pl.when(step == pl.num_programs(0) - 1)
    def _():
        for k in range(dk_ref.shape[0]):
            dk_ref[k] = dk_s[k + 1].astype(BF16)
            dv_ref[k] = dv_s[k + 1].astype(BF16)
        sums = [jnp.sum(ref[h], axis=0, keepdims=True) for ref in (dpre_ref, dpost_ref) for h in range(heads)]
        row = lax.broadcasted_iota(jnp.int32, (width, BLOCK), 0)
        col = lax.broadcasted_iota(jnp.int32, (width, BLOCK), 1)
        member = (row // (width // heads) == col).astype(F32)
        mixes = jnp.dot(
            jnp.concatenate(sums), member, preferred_element_type=F32, precision=lax.Precision.HIGHEST
        )
        lines = 2 * heads * BLOCK // width
        small_ref[...] = jnp.zeros(small_ref.shape, F32)
        small_ref[:lines, :] = jnp.concatenate(
            [mixes[k * lines : (k + 1) * lines] for k in range(width // BLOCK)], axis=1
        )


def attend_back(query, grad, u, lse, k_all, v_all, segs, pre, post):
    heads, width = pre.shape
    rows, stack = query.shape[0], heads * BLOCK
    blocks = rows // BLOCK
    groups = BACKWARD_GROUPS
    lines = 2 * heads * BLOCK // width + 2
    lines += -lines % 8
    by_block = pl.BlockSpec((BLOCK, width), lambda i: (i, 0))
    return pl.pallas_call(
        functools.partial(backward_kernel, heads, groups),
        grid=(blocks,),
        in_specs=[
            by_block,
            by_block,
            pl.BlockSpec((1, heads, BLOCK, width), lambda i: (i, 0, 0, 0)),
            pl.BlockSpec((1, stack, BLOCK), lambda i: (i, 0, 0)),
            ANY, ANY, SCALARS, whole((2 * blocks, 1, BLOCK)), whole(pre.shape), whole(post.shape),
        ],
        out_specs=[
            by_block,
            whole((2 * blocks, BLOCK, width)),
            whole((2 * blocks, BLOCK, width)),
            whole((lines, width)),
        ],
        scratch_shapes=[
            pltpu.VMEM((heads, 8, width), F32),
            pltpu.VMEM((heads, 8, width), F32),
            pltpu.VMEM((2 * blocks + 1, BLOCK, width), BF16),
            pltpu.VMEM((2 * blocks + 1, BLOCK, width), BF16),
            pltpu.VMEM((2 * blocks + 1, 1, BLOCK), jnp.int32),
            pltpu.VMEM((2 * blocks + 1, BLOCK, width), F32),
            pltpu.VMEM((2 * blocks + 1, BLOCK, width), F32),
            pltpu.VMEM((stack, width), BF16),
            pltpu.VMEM((stack, width), BF16),
            pltpu.VMEM((stack, BLOCK), F32),
            pltpu.VMEM((stack, width), F32),
            pltpu.SemaphoreType.DMA((2, blocks)),
        ],
        out_shape=[
            jax.ShapeDtypeStruct((rows, width), BF16),
            jax.ShapeDtypeStruct((2 * blocks, BLOCK, width), BF16),
            jax.ShapeDtypeStruct((2 * blocks, BLOCK, width), BF16),
            jax.ShapeDtypeStruct((lines, width), F32),
        ],
        compiler_params=pltpu.CompilerParams(vmem_limit_bytes=62 << 20),
        cost_estimate=cost(10 * rows * 1024 * stack // BLOCK * width, 4 * rows * stack // BLOCK * width),
        name="attend_back",
    )(query, grad, u, lse, k_all, v_all, segs, segs[:, None, :], pre, post)


MESH = pl.DeviceIdType.MESH


def device(place):
    d, t = place
    return d // 2, d % 2, t


def flip(index, bit):
    return index + bit - 2 * bit * ((index // bit) % 2)


def greet(nd, nt, d, t):
    barrier = pltpu.get_barrier_semaphore()
    core = d % 2
    partners = [(d, lax.rem(t + s, nt)) for s in range(1, nt)]
    partners += [(flip(d, 1), lax.rem(t + s, nt)) for s in range(nt)]
    partners += [(flips(d, mask), t) for mask in range(2, nd, 2)]
    for partner in partners:
        pl.semaphore_signal(barrier, inc=1, device_id=device(partner), device_id_type=MESH)
    pl.semaphore_wait(barrier, len(partners))


def remote(src, dst, send_sem, recv_sem, to):
    return pltpu.make_async_remote_copy(
        src_ref=src, dst_ref=dst, send_sem=send_sem, recv_sem=recv_sem, device_id=device(to), device_id_type=MESH
    )


def start_kernel(
    nd, nt, share, halves, *refs,
):
    tokens, grads, segments, later, pre_mix, post_mix = refs[:6]
    refs = refs[2:]
    if halves:
        weights, norms = refs[4:8], refs[8]
        x_out, q_out, k_out, v_out, seg_out, pre_out, post_out, mail_out, later_out, w_out, o_out, gain_out, near_out = refs[9:22]
        wg_s, w_send, w_recv, n_send, n_recv, n_self = refs[22:28]
    else:
        w_out, gain_out = refs[4:6]
        x_out, q_out, k_out, v_out, seg_out, pre_out, post_out, mail_out, later_out = refs[6:15]
    (g_send, g_recv, g_self, l_send, l_recv, x_s, kv_s, x_send, x_recv, x_self, kv_send, kv_recv, kv_self, seg_send, seg_recv, seg_self) = refs[-16:]
    d, t = 2 * lax.axis_index("plane") + lax.axis_index("core"), lax.axis_index("tensor")
    core = d % 2
    width = x_out.shape[1]
    micro = tokens.shape[0]
    per = tokens.shape[1]
    greet(nd, nt, d, t)

    if halves:
        line = lax.broadcasted_iota(jnp.int32, (8, width), 0)
        lane = lax.broadcasted_iota(jnp.int32, (8, width), 1)
        gains = jnp.zeros((8, width), F32)
        for n in range(2):
            for k in range(share):
                here = (line == n) & (lane == (d * nt + t) * share + k)
                gains = jnp.where(here, norms[n, k], gains)
        own = [weight[...].astype(F32) for weight in weights] + [gains]
        rest = wg_s.shape[2] - 4 * share - 8
        own = own + ([jnp.zeros((rest, width), F32)] if rest else [])
        wg_s[d, t] = jnp.concatenate(own).astype(BF16)
        z_copies = []
        for s in range(1, nt):
            slab = wg_s.at[d, t]
            copy = remote(slab, slab, w_send.at[0, 0, s], w_recv.at[0, 0, s], (d, lax.rem(t + s, nt)))
            copy.start()
            z_copies.append(copy)

    heads = pre_mix.shape[0]
    lane = lax.broadcasted_iota(jnp.int32, (heads, width), 1) // (width // heads)
    member = (lane == lax.broadcasted_iota(jnp.int32, (heads, width), 0)).astype(BF16)
    pre_out[...] = (left_t(pre_mix[...], member) * (width // heads) ** (-0.5)).astype(BF16)
    post_out[...] = matmul(post_mix[...], member)

    g_copies = []
    for m in range(micro):
        there = mail_out.at[2 * m + core]
        g_copies.append(pltpu.make_async_copy(grads.at[m, :, core], there, g_self.at[m]))
        g_copies.append(remote(grads.at[m, :, 1 - core], there, g_send.at[m], g_recv.at[m], (flip(d, 1), t)))
    for copy in g_copies:
        copy.start()

    sends = []
    for m in range(micro):
        for c in range(2):
            to = (d - core + c, 2 * m + core)
            here = (to[0] == d) & (to[1] == t)
            src, dst = tokens.at[m, :, c], x_s.at[pl.ds(per * t, per)]
            far = remote(src, dst, x_send.at[2 * m + c], x_recv.at[t], to)
            near = pltpu.make_async_copy(src, dst, x_self)
            pl.when(jnp.logical_not(here))(far.start)
            pl.when(here)(near.start)
            sends.append((here, far, near))

    holder = t % 2 == core
    seg_here = pltpu.make_async_copy(segments.at[t // 2], seg_out, seg_self)
    seg_there = remote(segments.at[t // 2], seg_out, seg_send, seg_recv, (flip(d, 1), t))

    @pl.when(holder)
    def _():
        seg_here.start()
        seg_there.start()

    l_copies = []
    for s in range(1, nt):
        l_copies.append(remote(later, later_out.at[s - 1], l_send.at[s], l_recv.at[s], (d, lax.rem(t + s, nt))))
    if halves:
        l_copies.append(pltpu.make_async_copy(later, near_out.at[d // 2], n_self))
        for mask in range(2, nd, 2):
            to = (flips(d, mask), t)
            l_copies.append(remote(later, near_out.at[d // 2], n_send.at[mask // 2], n_recv.at[mask // 2], to))
    for copy in l_copies:
        copy.start()

    if halves:
        bits = [1 << k for k in range(1, nd.bit_length() - 1)]
        routes = [bits + [1], bits[::-1] + [1]]
        have = [[0] for _ in halves]
        for copy in z_copies:
            copy.wait()
        for stage in range(len(bits) + 1):
            copies = []
            for h, (lo, hi) in enumerate(halves):
                bit = routes[h][stage]
                for k, mask in enumerate(have[h]):
                    slab = d
                    for b in [1 << j for j in range(nd.bit_length() - 1)]:
                        if mask & b:
                            slab = flip(slab, b)
                    ref = wg_s.at[slab, :, pl.ds(lo, hi - lo)]
                    copies.append(
                        remote(ref, ref, w_send.at[1 + h, stage, k], w_recv.at[1 + h, stage, k], (flip(d, bit), t))
                    )
                have[h] = have[h] + [mask | bit for mask in have[h]]
            for copy in copies:
                copy.start()
            for copy in copies:
                copy.wait()

        gains = jnp.zeros((8, width), F32)
        for pair in range(nd * nt // 2):
            slabs = [wg_s[(2 * pair + e) // nt, (2 * pair + e) % nt].astype(F32) for e in range(2)]
            for k in range(3):
                both = jnp.concatenate([slab[k * share : (k + 1) * share] for slab in slabs])
                w_out[2 * pair * share : 2 * (pair + 1) * share, k * width : (k + 1) * width] = both.astype(BF16)
            both = jnp.concatenate([slab[3 * share : 4 * share] for slab in slabs])
            o_out[2 * pair * share : 2 * (pair + 1) * share, :] = both.astype(BF16)
            gains = gains + (slabs[0] + slabs[1])[4 * share : 4 * share + 8]
        gain_out[...] = gains

    kv_copies = []
    gain = gain_out[:1]
    for s in range(nt):
        source = lax.rem(t + s, nt)
        here = (source == t) & holder
        arrival = remote(
            x_s.at[pl.ds(per * source, per)], x_s.at[pl.ds(per * source, per)], x_send.at[0], x_recv.at[source], (flip(d, 1), t)
        )
        local = pltpu.make_async_copy(tokens.at[0, :, 0], x_s.at[pl.ds(per * source, per)], x_self)
        pl.when(jnp.logical_not(here))(arrival.wait_recv)
        pl.when(here)(local.wait)
        x = x_s[pl.ds(per * source, per)].reshape(per * BLOCK, width)
        rows = pl.ds(pl.multiple_of(source * per * BLOCK, per * BLOCK), per * BLOCK)
        x_out[rows, :] = x
        x = x.astype(F32)
        h = (x * rms_scale(x) * gain).astype(BF16)
        q_out[rows, :] = matmul(h, w_out[:, :width]).astype(BF16)
        for k, out in enumerate((k_out, v_out)):
            value = matmul(h, w_out[:, (k + 1) * width : (k + 2) * width]).astype(BF16)
            kv_s[k, s] = value.reshape(per, BLOCK, width)
            dst = out.at[pl.ds(per * source, per), core]
            near = pltpu.make_async_copy(kv_s.at[k, s], dst, kv_self.at[k, s])
            far = remote(kv_s.at[k, s], dst, kv_send.at[k, s], kv_recv.at[k, s], (flip(d, 1), t))
            near.start()
            far.start()
            kv_copies += [near, far]
    for copy in kv_copies + l_copies + g_copies:
        copy.wait()
    for here, far, near in sends:
        pl.when(jnp.logical_not(here))(far.wait_send)

    @pl.when(holder)
    def _():
        seg_here.wait()
        seg_there.wait_send()

    @pl.when(jnp.logical_not(holder))
    def _():
        seg_there.wait_recv()


def start(tokens, grads, segments, pre_mix, post_mix, weights, norms, later):
    micro, _, rows, width = tokens.shape
    nd, nt = 2 * lax.axis_size("plane"), lax.axis_size("tensor")
    count = rows * nt // 2
    blocks = count // BLOCK
    per = blocks // nt
    share = weights[0].shape[0]
    length = 4 * share + 8 + -(4 * share + 8) % 16
    dma = pltpu.SemaphoreType.DMA
    vmem = pl.BlockSpec(memory_space=pltpu.VMEM)
    shaped = jax.ShapeDtypeStruct
    most = max(nd // 2, nt)
    inside = 2 * share % 16 == 0 and length >= 32
    middle = length // 32 * 16
    if inside:
        halves, given = [(0, middle), (middle, length)], [*weights, jnp.stack(norms).astype(F32)]
        given_specs = [vmem] * 4 + [SCALARS]
        gathered_specs = [vmem, vmem, vmem, vmem]
        gathered = [shaped((width, 3 * width), BF16), shaped((width, width), BF16), shaped((8, width), F32)]
        gathered.append(shaped((nd // 2,) + later.shape, BF16))
        scratch = [
            pltpu.VMEM((nd, nt, length, width), BF16),
            dma((3, nd.bit_length(), most)), dma((3, nd.bit_length(), most)),
            dma((nd // 2,)), dma((nd // 2,)), dma,
        ]
    else:
        place = (lax.axis_index("plane") * 2 * nt + lax.axis_index("core") * nt + lax.axis_index("tensor")) * share
        gains = lax.dynamic_update_slice(jnp.zeros((8, width), BF16), jnp.stack(norms), (0, place))
        slabs = lax.all_gather(jnp.concatenate([*weights, gains]), AXES, axis=0, tiled=False)
        w_qkv = slabs[:, : 3 * share].reshape(nd * nt, 3, share, width).transpose(0, 2, 1, 3)
        w_qkv = w_qkv.reshape(width, 3 * width)
        w_out = slabs[:, 3 * share : 4 * share].reshape(width, width)
        gains = jnp.sum(slabs[:, 4 * share : 4 * share + 8].astype(F32), axis=0)
        halves, given, given_specs, gathered_specs, gathered, scratch = [], [w_qkv, gains], [vmem, vmem], [], [], []
    results = pl.pallas_call(
        functools.partial(start_kernel, nd, nt, share, halves),
        in_specs=[ANY, ANY, ANY, ANY, vmem, vmem] + given_specs,
        out_specs=[vmem, vmem, ANY, ANY, ANY, vmem, vmem, vmem, ANY] + gathered_specs,
        out_shape=[
            shaped((count, width), BF16),
            shaped((count, width), BF16),
            shaped((blocks, 2, BLOCK, width), BF16),
            shaped((blocks, 2, BLOCK, width), BF16),
            shaped((2 * blocks, BLOCK), jnp.int32),
            shaped((pre_mix.shape[0], width), BF16),
            shaped((pre_mix.shape[0], width), F32),
            shaped((nt, per, BLOCK, width), BF16),
            shaped((nt - 1,) + later.shape, BF16),
            *gathered,
        ],
        scratch_shapes=scratch + [
            dma((micro,)), dma((micro,)), dma((micro,)),
            dma((nt,)), dma((nt,)),
            pltpu.VMEM((blocks, BLOCK, width), BF16),
            pltpu.VMEM((2, nt, per, BLOCK, width), BF16),
            dma((nt,)), dma((nt,)), dma,
            dma((2, nt)), dma((2, nt)), dma((2, nt)),
            dma, dma, dma,
        ],
        compiler_params=pltpu.CompilerParams(
            collective_id=0, has_side_effects=True, vmem_limit_bytes=62 << 20
        ),
        name="start",
    )(
        tokens.reshape(micro, rows // TILE, 2, BLOCK, width),
        grads.reshape(micro, rows // TILE, 2, BLOCK, width),
        segments.reshape(micro, 2 * blocks, BLOCK),
        later,
        pre_mix,
        post_mix,
        *given,
    )
    if inside:
        rest = [results[8]] + [send(results[8], by_bit(mask)) for mask in range(2, nd, 2)]
        return (*results[:8], results[12], rest, *results[9:12])
    near = lax.all_gather(later, ("plane", "core"), axis=0, tiled=False).reshape(nd // 2, 2, *later.shape)
    rest = lax.all_gather(results[8], ("plane", "core"), axis=0, tiled=False).reshape(nd // 2, 2, *results[8].shape)
    return (*results[:8], near, [rest], w_qkv, w_out, gains)


def gelu_parts(v):
    t = 1.0 / (1.0 + 0.23164189 * jnp.abs(v))
    bell = jnp.exp(-0.5 * v * v)
    series = t * (0.127414796 + t * (-0.142248368 + t * (0.7107068705 + t * (-0.7265760135 + t * 0.5307027145))))
    tail = series * bell
    return jnp.where(v < 0.0, tail, 1.0 - tail), 0.3989422804 * bell


def middle_kernel(rb, nd, nt, share, inside, *refs):
    x_ref, att_ref, w_out, gain_ref, near_all, dy_all = refs[:6]
    pieces = nd // 2 if inside else 1
    rest_all, refs = refs[6 : 6 + pieces], refs[pieces - 1 :]
    mail_ref, after_ref, datt_ref, dwo_ref, dgain_ref, part_ref, last_ref = refs[7:14]
    dy_ref, h_s, ht_s, dyt_s, o_s, dh_s, hid_s, dhid_s, w_s, dy_sem, w_self = refs[14:25]
    if inside:
        g_s, core_s, plane_s, c_send, c_recv, p_send, p_recv, w_send, w_recv = refs[25:]
    step = pl.program_id(0)
    d, t = 2 * lax.axis_index("plane") + lax.axis_index("core"), lax.axis_index("tensor")
    count, width = x_ref.shape
    parts = range(0, count, rb)
    bits = [1 << k for k in range(1, nd.bit_length() - 1)]
    routes = [bits, bits[::-1]]

    def weight_copies(k):
        if not inside:
            return [pltpu.make_async_copy(rest_all[0].at[:, :, k - 1] if k else near_all, w_s.at[k], w_self.at[k, 0])]
        pairs = [(near_all, w_s.at[k, :, d % 2])]
        if k:
            pairs = [(rest_all[j].at[k - 1], w_s.at[k, flips(d, 2 * j) // 2, d % 2]) for j in range(pieces)]
        copies = []
        for j, (rows, there) in enumerate(pairs):
            copies.append(pltpu.make_async_copy(rows, there, w_self.at[k, j]))
            copies.append(remote(rows, there, w_send.at[k, j], w_recv.at[k, j], (flip(d, 1), t)))
        return copies

    @pl.when(step == 0)
    def _():
        if inside:
            greet(nd, nt, d, t)
        for k in range(nt):
            for copy in weight_copies(k):
                copy.start()
        dy_copy = pltpu.make_async_copy(dy_all, dy_ref, dy_sem)
        dy_copy.start()
        for r in parts:
            rows = slice(r, r + rb)
            after = x_ref[rows, :].astype(F32) + matmul(att_ref[rows, :], w_out[...])
            after_ref[rows, :] = after
            o_s[rows, :] = after
            h = (after * rms_scale(after) * gain_ref[1:2]).astype(BF16)
            h_s[rows, :] = h
            ht_s[:, rows] = h.T
            dh_s[rows, :] = jnp.zeros((rb, width), F32)
        dy_copy.wait()
        for r in parts:
            rows = slice(r, r + rb)
            dyt_s[:, rows] = dy_ref[rows, :].T

    for k in range(nt):

        @pl.when(step == k)
        def _(k=k):
            for copy in weight_copies(k):
                copy.wait()

    def core_copies(slot):
        return [
            remote(
                g_s.at[slot, flips(flip(d, 1), mask)], core_s.at[slot, j],
                c_send.at[slot, j], c_recv.at[slot, j], (flip(d, 1), t),
            )
            for j, mask in enumerate(masks_of(bits))
        ]

    def plane_copies(slot, stage):
        copies = []
        for h in range(2):
            bit, rows = routes[h][stage], pl.ds(h * share, share)
            for j, mask in enumerate(masks_of(routes[h][stage + 1 :])):
                copies.append(
                    remote(
                        g_s.at[slot, flips(flip(d, bit), mask), rows], plane_s.at[slot, stage, j, rows],
                        p_send.at[slot, stage, h, j], p_recv.at[slot, stage, h, j], (flip(d, bit), t),
                    )
                )
        return copies

    def core_done(k):
        slot = lax.rem(k, 2)
        for copy in core_copies(slot):
            copy.wait()
        for j, mask in enumerate(masks_of(bits)):
            mine = flips(d, mask)
            total = (g_s[slot, mine].astype(F32) + core_s[slot, j].astype(F32)).astype(BF16)
            if isinstance(k, int):
                last_ref[j] = total
            else:
                g_s[slot, mine] = total
        for copy in [] if isinstance(k, int) else plane_copies(slot, 0):
            copy.start()

    def plane_done(k, stage):
        slot = lax.rem(k, 2)
        for copy in plane_copies(slot, stage):
            copy.wait()
        for h in range(2):
            rows = slice(h * share, (h + 1) * share)
            for j, mask in enumerate(masks_of(routes[h][stage + 1 :])):
                mine = flips(d, mask)
                total = g_s[slot, mine, rows].astype(F32) + plane_s[slot, stage, j, rows].astype(F32)
                g_s[slot, mine, rows] = total.astype(BF16)
        if stage + 1 < len(bits):
            for copy in plane_copies(slot, stage + 1):
                copy.start()
        else:
            mail_ref[lax.rem(t + nt - k, nt), : 2 * share] = g_s[slot, d]

    def when(condition, stage, *args):
        if inside:
            pl.when(condition)(functools.partial(stage, *args))

    @pl.when(step < nt)
    def _():
        up, down = (w_s[step, :, :, k * share : (k + 1) * share].reshape(width, -1) for k in range(2))
        for point, r in enumerate(parts):
            rows = slice(r, r + rb)
            v = matmul(h_s[rows, :], up)
            cumulative, density = gelu_parts(v)
            hid_s[rows, :] = (v * cumulative).astype(BF16)
            d_hidden = matmul(dy_ref[rows, :], down) * (cumulative + v * density)
            dhid_s[rows, :] = d_hidden.astype(BF16)
            if point == 1:
                when(step >= 1, core_done, step - 1)
        when(step >= 2, plane_done, step - 2, len(bits) - 1)
        slot = lax.rem(step, 2)
        for r in range(0, width, 2 * share):
            rows = slice(r, r + 2 * share)
            for k, (left, right) in enumerate(((ht_s, dhid_s), (dyt_s, hid_s))):
                both = matmul(left[rows, :], right[...]).astype(BF16)
                for e in range(2):
                    grad = both[e * share : (e + 1) * share]
                    if inside:
                        g_s[slot, r // share + e, k * share : (k + 1) * share] = grad
                    else:
                        part_ref[r // share + e, 0, k] = grad
                        last_ref[...] = jnp.zeros(last_ref.shape, BF16)
        if inside:
            for copy in core_copies(slot):
                copy.start()
        for r in parts:
            rows = slice(r, r + rb)
            o_s[rows, :] += right_t(hid_s[rows, :], down)
            dh_s[rows, :] += right_t(dhid_s[rows, :], up)
        for stage in range(len(bits) - 1):
            when(step >= 1, plane_done, step - 1, stage)

    @pl.when(step == nt)
    def _():
        gain = gain_ref[1:2]
        total = jnp.zeros((8, width), F32)
        mail_ref[:, mail_ref.shape[1] - count // nt :] = o_s[...].astype(BF16).reshape(nt, count // nt, width)
        for point, r in enumerate(parts):
            rows = slice(r, r + rb)
            after = after_ref[rows, :]
            scale = rms_scale(after)
            normed = after * scale
            dh = dh_s[rows, :]
            total = total + jnp.sum((dh * normed).reshape(rb // 8, 8, width), axis=0)
            d_after = dy_ref[rows, :].astype(F32) + rms_back(dh, normed, scale, gain)
            after_ref[rows, :] = d_after
            branch = d_after.astype(BF16)
            hid_s[rows, :] = branch
            datt_ref[rows, :] = right_t(branch, w_out[...]).astype(BF16)
            if inside and point == 0:
                core_done(nt - 1)
        if inside:
            plane_done(step - 2, len(bits) - 1)
        dgain_ref[...] = total
        dwo_ref[...] = left_t(att_ref[...], hid_s[...]).astype(BF16)
        if inside:
            part_ref[...] = jnp.zeros(part_ref.shape, BF16)
            mail_ref[lax.rem(t + 1, nt), : 2 * share] = jnp.zeros((2 * share, width), BF16)


def feed_forward(x, attended, dy, w_out, gain, near, rest, nd):
    count, width = x.shape
    nt, units = rest[0].shape[-3] + 1, rest[0].shape[-1]
    share = rest[0].shape[-2] // 2
    inside = share % 16 == 0 and nd >= 8
    rb = 256
    rows = whole((count, width))
    mail = (nt, count // nt + (2 * share if inside else 0), width)
    dma = pltpu.SemaphoreType.DMA
    scratch = [
        pltpu.VMEM((count, width), BF16),
        pltpu.VMEM((count, width), BF16),
        pltpu.VMEM((width, count), BF16),
        pltpu.VMEM((width, count), BF16),
        pltpu.VMEM((count, width), F32),
        pltpu.VMEM((count, width), F32),
        pltpu.VMEM((count, units), BF16),
        pltpu.VMEM((count, units), BF16),
        pltpu.VMEM((nt, nd // 2, 2, 2 * share, units), BF16),
        dma, dma((nt, nd // 2)),
    ]
    if inside:
        stages = nd.bit_length() - 2
        grads, grads_spec = jax.ShapeDtypeStruct((8, units), BF16), whole((8, units))
        scratch += [
            pltpu.VMEM((2, nd, 2 * share, units), BF16),
            pltpu.VMEM((2, nd // 2, 2 * share, units), BF16),
            pltpu.VMEM((2, stages, nd // 4, 2 * share, units), BF16),
            dma((2, nd // 2)), dma((2, nd // 2)),
            dma((2, stages, 2, nd // 4)), dma((2, stages, 2, nd // 4)),
            dma((nt, nd // 2)), dma((nt, nd // 2)),
        ]
        params = dict(collective_id=2, has_side_effects=True)
    else:
        grads = jax.ShapeDtypeStruct((nd, nt, 2, share, units), BF16)
        grads_spec = pl.BlockSpec((nd, 1, 2, share, units), lambda s: (0, jnp.minimum(s, nt - 1), 0, 0, 0))
        params = {}
    return pl.pallas_call(
        functools.partial(middle_kernel, rb, nd, nt, share, inside),
        grid=(nt + 1,),
        in_specs=[
            rows, rows, whole((width, width)), whole((8, width)), ANY, ANY,
        ] + [ANY] * len(rest),
        out_specs=[whole(mail), rows, rows, whole((width, width)), whole((8, width)), grads_spec, whole((nd // 2, 2 * share, units))],
        out_shape=[
            jax.ShapeDtypeStruct(mail, BF16),
            jax.ShapeDtypeStruct((count, width), F32),
            jax.ShapeDtypeStruct((count, width), BF16),
            jax.ShapeDtypeStruct((width, width), BF16),
            jax.ShapeDtypeStruct((8, width), F32),
            grads,
            jax.ShapeDtypeStruct((nd // 2, 2 * share, units), BF16),
        ],
        scratch_shapes=scratch,
        compiler_params=pltpu.CompilerParams(vmem_limit_bytes=62 << 20, **params),
        cost_estimate=cost(12 * count * width * nt * units, 4 * nd * nt * share * units),
        name="feed_forward",
    )(x, attended, w_out, gain, near, dy, *rest)


def masks_of(bits):
    masks = [0]
    for bit in bits:
        masks = masks + [mask | bit for mask in masks]
    return masks


def flips(index, mask):
    bit = 1
    while bit <= mask:
        if mask & bit:
            index = flip(index, bit)
        bit *= 2
    return index


def finish_kernel(
    nd, nt, share, inside, x_all, dq_all, dk_all, dv_all, after_all, w_all, gain_ref, dwo_all, small_ref,
    ffn_ref, back, *refs,
):
    last_refs, refs = refs[: nd // 2], refs[nd // 2 :]
    tok_out, out_out, dw_out, small_out, last_out = refs[:5]
    own_s, other_s, grads_s, ht_s, tok_s, own_sems, kv_send, kv_recv, tok_send, tok_recv, tok_self = refs[5:16]
    b_send, b_recv, b_self, x_ref, dq_ref, after_ref, w_ref, dwo_ref, in_sems, last4_s, last_sems, last_s, l_send, l_recv = refs[16:30]
    if inside:
        slab_s, core_s, plane_s, mine_s, z_s, sm_s, sm_in, g_send, g_recv, s_send, s_recv = refs[30:]
    d, t = 2 * lax.axis_index("plane") + lax.axis_index("core"), lax.axis_index("tensor")
    core = d % 2
    count, width = x_all.shape
    per = tok_out.shape[1]
    rows_in = per * BLOCK
    holder = t % 2 == core
    bits = [1 << k for k in range(1, nd.bit_length() - 1)]
    loads = [
        pltpu.make_async_copy(far, near, in_sems.at[k])
        for k, (far, near) in enumerate(
            ((dq_all, dq_ref), (w_all, w_ref), (x_all, x_ref), (after_all, after_ref), (dwo_all, dwo_ref))
        )
    ]
    own = [pltpu.make_async_copy(a.at[:, core], own_s.at[k], own_sems.at[k]) for k, a in enumerate((dk_all, dv_all))]
    loads += [pltpu.make_async_copy(far, last4_s.at[k], last_sems.at[k]) for k, far in enumerate(last_refs)]
    for copy in own + loads:
        copy.start()
    greet(nd, nt, d, t)

    order = [lax.rem(t + s, nt) for s in list(range(1, nt)) + [0]]
    exchanged = []
    for s, source in enumerate(order):
        pair = []
        for k, a in enumerate((dk_all, dv_all)):
            pair.append(
                remote(
                    a.at[pl.ds(per * source, per), 1 - core], other_s.at[k, pl.ds(per * source, per)],
                    kv_send.at[k, s], kv_recv.at[k, s], (flip(d, 1), t),
                )
            )
        exchanged.append(pair)
    for copy in exchanged[0] + exchanged[1]:
        copy.start()
    b_copies = []
    skip = back.shape[1] - rows_in
    for m in range(out_out.shape[0]):
        for k in range(per):
            there, lines = out_out.at[m, k, core], pl.ds(skip + k * BLOCK, BLOCK)
            b_copies.append(pltpu.make_async_copy(back.at[2 * m + core, lines], there, b_self.at[m, k]))
            b_copies.append(
                remote(back.at[2 * m + 1 - core, lines], there, b_send.at[m, k], b_recv.at[m, k], (flip(d, 1), t))
            )
    gain = gain_ref[:1]

    def norms(rows):
        x = x_ref[rows, :].astype(F32)
        scale = rms_scale(x)
        return x * scale, scale

    routes = [[1] + bits, [1] + bits[::-1]]
    rows_of_slab = width // nd

    def fill(bundle, which, left, right):
        for k in range(nd):
            lines = slice(k * rows_of_slab, (k + 1) * rows_of_slab)
            if k % 2 == 0:
                both = matmul(left[lines.start : lines.stop + rows_of_slab, :], right)
                slab_s[bundle, which, k : k + 2] = both.astype(BF16).reshape(2, rows_of_slab, width)

    def stage_copies(bundle, stage):
        copies, adds = [], []
        for h in range(2):
            bit = routes[h][stage]
            for k, mask in enumerate(masks_of(routes[h][stage + 1 :])):
                buffer = core_s.at[bundle] if stage == 0 else plane_s.at[bundle, stage - 1]
                copies.append(
                    remote(
                        slab_s.at[bundle, h, flips(flip(d, bit), mask)], buffer.at[h, k],
                        g_send.at[bundle, h, stage, k], g_recv.at[bundle, h, stage, k], (flip(d, bit), t),
                    )
                )
                adds.append((h, flips(d, mask), buffer, k))
        return copies, adds

    def stage_start(bundle, stage):
        for copy in stage_copies(bundle, stage)[0]:
            copy.start()

    def stage_done(bundle, stage):
        copies, adds = stage_copies(bundle, stage)
        for copy in copies:
            copy.wait()
        last = stage == len(bits)
        totals = []
        for h, mine, buffer, k in adds:
            total = slab_s[bundle, h, mine].astype(F32) + buffer[h, k].astype(F32)
            if last:
                totals.append(total.reshape(nt, share, width))
            else:
                slab_s[bundle, h, mine] = total.astype(BF16)
        if last:
            mine_s[bundle] = jnp.concatenate(totals, axis=1).astype(BF16)

    def z_copies(bundle):
        copies = []
        for s in range(1, nt):
            to = lax.rem(t + s, nt)
            copies.append(
                remote(
                    mine_s.at[bundle, to], z_s.at[bundle, s],
                    g_send.at[bundle, 2, 0, s], g_recv.at[bundle, 2, 0, s], (d, to),
                )
            )
        return copies

    def small_copies(stage):
        if stage <= len(bits):
            return [remote(sm_s, sm_in.at[stage], s_send.at[stage], s_recv.at[stage], (flip(d, routes[0][stage]), t))]
        copies = []
        for s in range(1, nt):
            k = len(bits) + s
            copies.append(remote(sm_s, sm_in.at[k], s_send.at[k], s_recv.at[k], (d, lax.rem(t + s, nt))))
        return copies

    sends, gains = [], []
    to_core = d - core + t % 2

    def sum_group(s):
        source = order[s]
        for copy in exchanged[s]:
            copy.wait()
        for copy in exchanged[s + 2] if s + 2 < nt else []:
            copy.start()
        rows = pl.ds(pl.multiple_of(source * rows_in, rows_in), rows_in)
        grads_s[rows, :width] = dq_ref[rows, :]
        for k in range(2):
            total = own_s[k, pl.ds(per * source, per)].astype(F32) + other_s[k, pl.ds(per * source, per)].astype(F32)
            grads_s[rows, (k + 1) * width : (k + 2) * width] = total.reshape(rows_in, width).astype(BF16)

    def token_group(s):
        source = order[s]
        rows = pl.ds(pl.multiple_of(source * rows_in, rows_in), rows_in)
        dh = right_t(grads_s[rows, :], w_ref[...])
        normed, scale = norms(rows)
        gains.append(jnp.sum((dh * normed).reshape(rows_in // 8, 8, width), axis=0))
        tok = after_ref[rows, :] + rms_back(dh, normed, scale, gain)
        tok_s[s] = tok.astype(BF16).reshape(per, BLOCK, width)
        here = (source == t) & holder
        dst = tok_out.at[t // 2, :, core]
        far = remote(tok_s.at[s], dst, tok_send.at[s], tok_recv.at[2 * (t // 2) + core], (to_core, source))
        near = pltpu.make_async_copy(tok_s.at[s], dst, tok_self)
        pl.when(jnp.logical_not(here))(far.start)
        pl.when(here)(near.start)
        sends.append((here, far, near))

    for copy in own + loads:
        copy.wait()
    last_s[...] = sum(last4_s[k].astype(F32) for k in range(last4_s.shape[0])).astype(BF16)
    last = remote(last_s, last_out, l_send, l_recv, (d, lax.rem(t + 1, nt)))
    last.start()
    for r in range(0, count, rows_in):
        lines = slice(r, r + rows_in)
        normed, scale = norms(lines)
        ht_s[:, lines] = (normed * gain).astype(BF16).T
    if inside:
        slab_s[0, 1] = dwo_ref[...].reshape(nd, rows_of_slab, width)
        fill(0, 0, ht_s, dq_ref[...])
        stage_start(0, 0)
    for s in range(nt // 2):
        sum_group(s)
        token_group(s)
    if inside:
        stage_done(0, 0)
        stage_start(0, 1)
    for s in range(nt // 2, nt):
        sum_group(s)
    if inside:
        for which in range(2):
            fill(1, which, ht_s, grads_s[:, (which + 1) * width : (which + 2) * width])
        stage_start(1, 0)
    for s in range(nt // 2, nt):
        token_group(s)

    for copy in b_copies:
        copy.start()
    small = small_ref[...]
    line = lax.broadcasted_iota(jnp.int32, small.shape, 0)
    small = small + jnp.where(line == small.shape[0] - 2, jnp.sum(sum(gains), axis=0, keepdims=True), 0.0)
    small = small + jnp.where(line == small.shape[0] - 1, jnp.sum(ffn_ref[...], axis=0, keepdims=True), 0.0)
    if inside:
        sm_s[...] = small
        tiny = small_copies(0)
        for copy in tiny:
            copy.start()
        for stage in range(len(bits) + 1):
            for copy in tiny:
                copy.wait()
            sm_s[...] += sm_in[stage]
            tiny = small_copies(stage + 1)
            for copy in tiny:
                copy.start()
            stage_done(1, stage)
            if stage < len(bits):
                stage_start(1, stage + 1)
                stage_done(0, stage + 1)
                if stage + 1 < len(bits):
                    stage_start(0, stage + 2)
                else:
                    first_z = z_copies(0)
                    for copy in first_z:
                        copy.start()
        second_z = z_copies(1)
        for copy in second_z:
            copy.start()
        for copy in first_z + second_z + tiny:
            copy.wait()
        for bundle in range(2):
            total = mine_s[bundle, t].astype(F32)
            for s in range(1, nt):
                total = total + z_s[bundle, s].astype(F32)
            dw_out[bundle * 2 * share : (bundle + 1) * 2 * share] = total
        small_out[...] = sm_s[...] + sum(sm_in[len(bits) + s] for s in range(1, nt))
    else:
        small_out[...] = small
        for r in range(0, width, 256):
            lines = slice(r, r + 256)
            dw_out[lines, : 3 * width] = matmul(ht_s[lines, :], grads_s[...]).astype(BF16)
            dw_out[lines, 3 * width :] = dwo_ref[lines, :]

    for copy in b_copies + [last]:
        copy.wait()
    for here, far, near in sends:
        pl.when(jnp.logical_not(here))(far.wait_send)
        pl.when(here)(near.wait)
    for m in range(tok_out.shape[0]):
        for c in range(2):
            here = (2 * m + core == t) & (c == core)
            dst = tok_out.at[m, :, c]
            back = remote(dst, dst, tok_send.at[0], tok_recv.at[2 * m + c], (flip(d, 1), t))
            pl.when(jnp.logical_not(here))(back.wait_recv)


def finish(x, dq, dk_all, dv_all, after, w_qkv, gains, dwo, small, gain_ffn, back, last, share, micro):
    count, width = x.shape
    nd, nt = 2 * lax.axis_size("plane"), lax.axis_size("tensor")
    inside = 2 * share % 16 == 0 and nd >= 8
    blocks = count // BLOCK
    per = blocks // nt
    dma = pltpu.SemaphoreType.DMA
    vmem = pl.BlockSpec(memory_space=pltpu.VMEM)
    shaped = jax.ShapeDtypeStruct
    scratch = [
        pltpu.VMEM((2, blocks, BLOCK, width), BF16),
        pltpu.VMEM((2, blocks, BLOCK, width), BF16),
        pltpu.VMEM((count, 3 * width), BF16),
        pltpu.VMEM((width, count), BF16),
        pltpu.VMEM((nt, per, BLOCK, width), BF16),
        dma((2,)), dma((2, nt)), dma((2, nt)), dma((nt,)), dma((nt,)), dma,
        dma((micro, per)), dma((micro, per)), dma((micro, per)),
        pltpu.VMEM(x.shape, x.dtype), pltpu.VMEM(dq.shape, dq.dtype), pltpu.VMEM(after.shape, after.dtype),
        pltpu.VMEM(w_qkv.shape, w_qkv.dtype), pltpu.VMEM(dwo.shape, dwo.dtype), dma((5,)),
        pltpu.VMEM((nd // 2,) + last[0].shape, BF16), dma((nd // 2,)), pltpu.VMEM(last[0].shape, BF16), dma, dma,
    ]
    if inside:
        most = max(nd // 2, nt)
        stages = nd.bit_length() - 1
        scratch += [
            pltpu.VMEM((2, 2, nd, nt * share, width), BF16),
            pltpu.VMEM((2, 2, nd // 2, nt * share, width), BF16),
            pltpu.VMEM((2, stages - 1, 2, nd // 4, nt * share, width), BF16),
            pltpu.VMEM((2, nt, 2 * share, width), BF16),
            pltpu.VMEM((2, nt, 2 * share, width), BF16),
            pltpu.VMEM(small.shape, F32),
            pltpu.VMEM((stages + nt,) + small.shape, F32),
            dma((2, 3, stages, most)), dma((2, 3, stages, most)), dma((stages + nt,)), dma((stages + nt,)),
        ]
    return pl.pallas_call(
        functools.partial(finish_kernel, nd, nt, share, inside),
        in_specs=[ANY, ANY, ANY, ANY, ANY, ANY, vmem, ANY, vmem, vmem, ANY] + [ANY] * len(last),
        out_specs=[vmem, vmem, vmem, vmem, vmem],
        out_shape=[
            shaped((micro, per, 2, BLOCK, width), BF16),
            shaped((micro, per, 2, BLOCK, width), BF16),
            shaped((4 * share, width), F32) if inside else shaped((width, 4 * width), BF16),
            shaped(small.shape, F32),
            shaped(last[0].shape, BF16),
        ],
        scratch_shapes=scratch,
        compiler_params=pltpu.CompilerParams(
            collective_id=1, has_side_effects=True, vmem_limit_bytes=62 << 20
        ),
        cost_estimate=cost(24 * count * width * width, 16 * count * width),
        name="finish",
    )(x, dq, dk_all, dv_all, after, w_qkv, gains, dwo, small, gain_ffn, back, *last)


def emit_kernel(heads, share, tok_ref, out_ref, dw_ref, ffn_ref, last_ref, small_ref, tok, out, *rest):
    grads, ups, gains, mixes = rest[:4], rest[4:6], rest[6:8], rest[8:10]
    tok[...] = tok_ref[...].astype(F32)
    out[...] = out_ref[...]

    @pl.when(pl.program_id(0) == 0)
    def _():
        for grad, k in zip(grads, (0, 2, 3, 1)):
            grad[...] = dw_ref[k * share : (k + 1) * share]
        half = last_ref.shape[0] // 2
        for k, up in enumerate(ups):
            lines = slice(k * half, (k + 1) * half)
            total = last_ref[lines].astype(F32)
            for z in range(ffn_ref.shape[0]):
                total = total + ffn_ref[z, lines].astype(F32)
            up[...] = total
        width = small_ref.shape[1]
        place = (
            (lax.axis_index("plane") * 2 + lax.axis_index("core")) * lax.axis_size("tensor") + lax.axis_index("tensor")
        ) * share
        row = lax.broadcasted_iota(jnp.int32, (width, share), 0)
        col = lax.broadcasted_iota(jnp.int32, (width, share), 1)
        exact = dict(preferred_element_type=F32, precision=lax.Precision.HIGHEST)
        own = jnp.dot(small_ref[small_ref.shape[0] - 8 :, :], (row == place + col).astype(F32), **exact)
        for k, gain in enumerate(gains):
            gain[...] = own[6 + k : 7 + k]
        lines = 2 * heads * BLOCK // width
        sums = jnp.concatenate(
            [small_ref[:lines, k * BLOCK : (k + 1) * BLOCK] for k in range(width // BLOCK)]
        )[:, :heads]
        mixes[0][...] = sums[:heads].T * (width // heads) ** (-0.5)
        mixes[1][...] = sums[heads:]


def emit(tok, out, dw, ffn, last, small, heads, share):
    width = small.shape[1]
    micro, per, cores, block, _ = tok.shape
    rows = per * cores * block

    def part(k):
        return pl.BlockSpec((1, rows, width), lambda i: (i, 0, 0))

    shaped = jax.ShapeDtypeStruct
    small_shapes = [(share, width)] * 4 + [(last.shape[0] // 2, width)] * 2 + [(1, share)] * 2 + [(heads, heads)] * 2
    return pl.pallas_call(
        functools.partial(emit_kernel, heads, share),
        grid=(micro,),
        in_specs=[part(0), part(1), whole(dw.shape), whole((ffn.shape[0],) + last.shape), whole(last.shape), whole(small.shape)],
        out_specs=[part(0), part(1)] + [whole(shape) for shape in small_shapes],
        out_shape=[shaped((micro, rows, width), F32), shaped((micro, rows, width), BF16)]
        + [shaped(shape, F32) for shape in small_shapes],
        compiler_params=pltpu.CompilerParams(vmem_limit_bytes=62 << 20),
        name="emit",
    )(tok.reshape(micro, rows, width), out.reshape(micro, rows, width), dw, ffn, last, small)


def per_device(
    tokens, segments, w_query, w_key, w_value, w_out, norm_attn, norm_ffn, pre_mix, post_mix, w_up, w_down, out_grad,
):
    micro, _, rows, width = tokens.shape
    nd, nt = 2 * lax.axis_size("plane"), lax.axis_size("tensor")
    heads = pre_mix.shape[0]
    head_width = width // heads
    length = rows * nt
    count = length // 2
    blocks = count // BLOCK
    share = w_query.shape[0]
    bits = [1 << k for k in range(nd.bit_length() - 1)]
    d, t = 2 * lax.axis_index("plane") + lax.axis_index("core"), lax.axis_index("tensor")
    core = d % 2

    later = jnp.concatenate([w_up, w_down])
    x, query, k_all, v_all, segs, pre, post, mail, near, rest, w_qkv, all_out, gains = start(
        tokens, out_grad, segments, pre_mix, post_mix, [w_query, w_key, w_value, w_out], [norm_attn, norm_ffn], later
    )
    k_all, v_all = (a.reshape(2 * blocks, BLOCK, width) for a in (k_all, v_all))
    dy = lax.all_to_all(mail, "tensor", 0, 0, tiled=True).reshape(count, width)
    attended, u, lse = attend(query, k_all, v_all, segs, pre, post)
    mail, grad_after, grad_attended, grad_w_out, grad_gain_ffn, part_both, last_both = feed_forward(
        x, attended, dy, all_out, gains, near, rest, nd
    )
    back = lax.all_to_all(mail, "tensor", 0, 0, tiled=True)
    last_both = [last_both[0]] + [send(last_both[k], by_bit(2 * k)) for k in range(1, nd // 2)]
    if part_both.ndim > 3:
        part_both = lax.dynamic_slice_in_dim(jnp.concatenate([part_both[:, ::-1]] * 2, axis=1), nt - 1 - t, nt, 1)
        part_both = lax.psum_scatter(part_both, ("plane", "core"), scatter_dimension=0, tiled=False)
        part_both = lax.psum_scatter(part_both, "tensor", scatter_dimension=0, tiled=False)
        part_both = part_both.reshape(1, 2 * w_up.shape[0], w_up.shape[1])
    else:
        part_both = back

    grad_query, grad_key, grad_value, small = attend_back(
        query, grad_attended, u, lse, k_all, v_all, segs, pre, post
    )
    d_tokens, out, owned, small, last_both = finish(
        x, grad_query, grad_key.reshape(blocks, 2, BLOCK, width), grad_value.reshape(blocks, 2, BLOCK, width),
        grad_after, w_qkv, gains, grad_w_out, small, grad_gain_ffn, back, last_both, share, micro,
    )
    if owned.dtype == BF16:
        owned = lax.psum_scatter(owned, AXES, scatter_dimension=0, tiled=True).astype(F32)
        owned = jnp.concatenate([owned[:, k * width : (k + 1) * width] for k in (0, 3, 1, 2)])
        small = lax.psum(small, AXES)
    d_tokens, out, *grads = emit(d_tokens, out, owned, part_both, last_both, small, heads, share)
    d_query, d_key, d_value, d_out, d_up, d_down, d_gain_attn, d_gain_ffn, d_pre, d_post = grads
    return (
        out.reshape(tokens.shape),
        d_tokens.reshape(tokens.shape),
        d_query,
        d_key,
        d_value,
        d_out,
        d_gain_attn.reshape(share),
        d_gain_ffn.reshape(share),
        d_pre,
        d_post,
        d_up,
        d_down,
    )


def solution(mesh):
    devices = mesh.devices
    devices = devices.reshape(devices.shape[0] // 2, 2, devices.shape[1])
    dp = ("plane", "core")
    both = P(AXES, None)
    gain = P(AXES)
    data = P(None, dp, "tensor", None)
    ffn = P(dp, "tensor")
    return jax.shard_map(
        per_device,
        mesh=jax.sharding.Mesh(devices, AXES),
        in_specs=(data, P(None, dp, None), both, both, both, both, gain, gain, P(), P(), ffn, ffn, data),
        out_specs=(data, data, both, both, both, both, gain, gain, P(), P(), ffn, ffn),
        check_vma=False,
    )
```

```python
import functools

import jax
import jax.numpy as jnp
from jax import lax
from jax.experimental import pallas as pl
from jax.experimental.pallas import tpu as pltpu
from jax.sharding import PartitionSpec as P

F32 = jnp.float32
BF16 = jnp.bfloat16
BLOCK = 128
TILE = 2 * BLOCK
FORWARD_GROUPS = 6
BACKWARD_GROUPS = (2, 2, 2)
AXES = ("plane", "core", "tensor")


def matmul(left, right):
    return jnp.dot(left, right, preferred_element_type=F32)


def right_t(left, right):
    return lax.dot_general(left, right, (((1,), (1,)), ((), ())), preferred_element_type=F32)


def left_t(left, right):
    return lax.dot_general(left, right, (((0,), (0,)), ((), ())), preferred_element_type=F32)


def rms_scale(values):
    return lax.rsqrt(jnp.mean(values * values, axis=-1, keepdims=True) + 1e-06)


def rms_back(grad_norm, normed, scale, gain):
    scaled = grad_norm * gain
    return scale * (scaled - normed * jnp.mean(scaled * normed, axis=-1, keepdims=True))


def gelu_exact(values):
    return jax.nn.gelu(values, approximate=False)


def gelu_back(upper, grad):
    unused, pull = jax.vjp(gelu_exact, upper)
    return pull(grad)[0]


def send(x, to):
    nd, nt = 2 * lax.axis_size("plane"), lax.axis_size("tensor")
    pairs = []
    for d in range(nd):
        for t in range(nt):
            d2, t2 = to(d, t)
            pairs.append((d * nt + t, d2 * nt + t2))
    return lax.ppermute(x, AXES, pairs)


def by_shift(shift):
    nt = lax.axis_size("tensor")
    return lambda d, t: (d, (t + shift) % nt)


def by_bit(bit):
    return lambda d, t: (d ^ bit, t)


def gather(piece, bits):
    nt = lax.axis_size("tensor")
    have = {0: jnp.stack([piece] + [send(piece, by_shift(s)) for s in range(1, nt)])}
    for bit in bits:
        have.update({mask | bit: send(block, by_bit(bit)) for mask, block in have.items()})
    return [have[mask] for mask in range(len(have))]


def pick(x, index, axis):
    return lax.dynamic_index_in_dim(x, index, axis, keepdims=False)


def sum_to_owner(x, bits):
    nt, nd = x.shape[:2]
    d, t = 2 * lax.axis_index("plane") + lax.axis_index("core"), lax.axis_index("tensor")
    rest = x.shape[2:]
    names = [1 << k for k in range(nd.bit_length() - 1)][::-1]
    x = x.reshape((nt,) + (2,) * len(names) + rest)
    for bit in bits:
        axis = 1 + names.index(bit)
        names.remove(bit)
        mine = (d // bit) % 2
        got = send(pick(x, 1 - mine, axis), by_bit(bit))
        x = pick(x, mine, axis).astype(F32) + got.astype(F32)
        if names or nt > 1:
            x = x.astype(BF16)
    total = pick(x, t, 0).astype(F32)
    for shift in range(1, nt):
        total = total + send(pick(x, lax.rem(t + shift, nt), 0), by_shift(shift)).astype(F32)
    return total


def arrive(step, sources, scratches, sems, seg_ref, seg_s):
    blocks = sources[0].shape[0]
    copies = []
    for k, (source, scratch) in enumerate(zip(sources, scratches)):
        for part in range(blocks // 2):
            rows = pl.ds(2 * part, 2)
            there = scratch.at[pl.ds(2 * part + 1, 2)]
            copies.append((part, pltpu.make_async_copy(source.at[rows], there, sems.at[k, part])))

    @pl.when(step == 0)
    def _():
        for _, copy in copies:
            copy.start()
        seg_s[0] = jnp.full((1, BLOCK), -1, jnp.int32)
        seg_s[1:] = seg_ref[...]
        for scratch in scratches:
            scratch[0] = jnp.zeros(scratch.shape[1:], BF16)

    for part, copy in copies:
        pl.when(step == part)(copy.wait)


def reach(block, seg_low):
    first = seg_low[block, 0]
    before = 0
    for k in range(seg_low.shape[0]):
        before += (seg_low[k, BLOCK - 1] < first).astype(jnp.int32)
    return (block + 2 - before) // 2


def rows_of(block, seg_s):
    return jnp.broadcast_to(seg_s[block + 1], (BLOCK, BLOCK)).T


def row_mask(row_seg, first, block, seg_s):
    row = lax.broadcasted_iota(jnp.int32, (BLOCK, BLOCK), 0)
    col = lax.broadcasted_iota(jnp.int32, (BLOCK, BLOCK), 1)
    masks = []
    for k in range(2):
        ahead = (first + k - 1 - block) * BLOCK
        allowed = (row_seg == seg_s[first + k]) & (col + ahead <= row)
        masks.append(jnp.where(allowed, 0.0, -1e30).astype(F32))
    return jnp.concatenate(masks, axis=1)


def forward_kernel(
    heads, groups, most, q_ref, k_all, v_all, seg_low, seg_ref, pre_ref, post_ref,
    att_ref, u_ref, lse_ref, k_s, v_s, seg_s, qp_s, m_s, s_s, sems,
):
    step = pl.program_id(0)
    core = lax.axis_index("core")
    block = 2 * step + core
    width = q_ref.shape[1]
    arrive(step, [k_all, v_all], [k_s, v_s], sems, seg_ref, seg_s)
    tiles = reach(block, seg_low)
    row_seg = rows_of(block, seg_s)

    def scores(left, first, mask):
        keys = k_s[pl.ds(first, 2)].reshape(TILE, -1)
        s = right_t(left, keys).reshape(left.shape[0] // BLOCK, BLOCK, TILE)
        return (s + mask[None]).reshape(left.shape[0], TILE)

    def close(g, per, top, total, u, att):
        size = per * BLOCK
        lse_ref[0, g * size : (g + 1) * size, :] = jnp.broadcast_to(top + jnp.log(total), (size, BLOCK))
        for k in range(per):
            h = g * per + k
            part = u[k * BLOCK : (k + 1) * BLOCK]
            u_ref[0, h] = part.astype(BF16)
            att = att + part * post_ref[h : h + 1, :]
        return att

    @pl.when(tiles == 1)
    def _():
        per = heads // groups
        query = q_ref[...]
        mask = row_mask(row_seg, block, block, seg_s)
        att = jnp.zeros((BLOCK, width), F32)
        values = v_s[pl.ds(block, 2)].reshape(TILE, -1)
        for g in range(groups):
            left = jnp.concatenate([query * pre_ref[h : h + 1, :] for h in range(g * per, (g + 1) * per)])
            s = scores(left, block, mask)
            top = jnp.max(s, axis=-1, keepdims=True)
            p = jnp.exp(s - top)
            total = jnp.sum(p, axis=-1, keepdims=True)
            u = matmul((p * (1.0 / total)).astype(BF16), values)
            att = close(g, per, top, total, u, att)
        att_ref[...] = att.astype(BF16)

    @pl.when(tiles > 1)
    def _():
        query = q_ref[...]
        for h in range(heads):
            qp_s[h * BLOCK : (h + 1) * BLOCK, :] = query * pre_ref[h : h + 1, :]
        m_s[...] = jnp.full(m_s.shape, -3e38, F32)
        split = 2
        size = heads // split * BLOCK

        def meet(tile, carry):
            first = block - 2 * tile
            mask = row_mask(row_seg, first, block, seg_s)
            for g in range(split):
                rows = slice(g * size, (g + 1) * size)
                s = scores(qp_s[rows, :], first, mask)
                s_s[tile, rows, :] = s
                m_s[rows, :] = jnp.maximum(m_s[rows, :], jnp.maximum(s[:, :BLOCK], s[:, BLOCK:]))
            return carry

        lax.fori_loop(0, tiles, meet, 0)

    for n in range(2, most + 1):

        @pl.when(tiles == n)
        def _(n=n):
            per = heads // groups
            size = per * BLOCK
            values = v_s[pl.ds(block - 2 * n + 2, 2 * n)].reshape(n * TILE, -1)
            att = jnp.zeros((BLOCK, width), F32)
            for g in range(groups):
                rows = slice(g * size, (g + 1) * size)
                top = jnp.max(m_s[rows, :], axis=-1, keepdims=True)
                parts = [jnp.exp(s_s[tile, rows, :] - top) for tile in range(n)]
                total = jnp.sum(sum(p[:, :BLOCK] + p[:, BLOCK:] for p in parts), axis=-1, keepdims=True)
                p = jnp.concatenate([part.astype(BF16) for part in parts[::-1]], axis=1)
                u = matmul(p, values) * (1.0 / total)
                att = close(g, per, top, total, u, att)
            att_ref[...] = att.astype(BF16)


def whole(shape):
    return pl.BlockSpec(shape, lambda i: (0,) * len(shape), pipeline_mode=pl.Buffered(1))


def cost(flops, moved):
    return pl.CostEstimate(flops=int(flops), bytes_accessed=int(moved), transcendentals=0)


ANY = pl.BlockSpec(memory_space=pl.ANY)
SCALARS = pl.BlockSpec(memory_space=pltpu.SMEM)


def attend(query, k_all, v_all, segs, pre, post):
    heads, width = pre.shape
    rows, stack = query.shape[0], heads * BLOCK
    blocks = rows // BLOCK
    groups = FORWARD_GROUPS
    most = (1024 // BLOCK + 2) // 2
    by_block = pl.BlockSpec((BLOCK, width), lambda i: (i, 0))
    return pl.pallas_call(
        functools.partial(forward_kernel, heads, groups, most),
        grid=(blocks,),
        in_specs=[
            by_block, ANY, ANY, SCALARS, whole((2 * blocks, 1, BLOCK)), whole(pre.shape), whole(post.shape),
        ],
        out_specs=[
            by_block,
            pl.BlockSpec((1, heads, BLOCK, width), lambda i: (i, 0, 0, 0)),
            pl.BlockSpec((1, stack, BLOCK), lambda i: (i, 0, 0)),
        ],
        scratch_shapes=[
            pltpu.VMEM((2 * blocks + 1, BLOCK, width), BF16),
            pltpu.VMEM((2 * blocks + 1, BLOCK, width), BF16),
            pltpu.VMEM((2 * blocks + 1, 1, BLOCK), jnp.int32),
            pltpu.VMEM((stack, width), BF16),
            pltpu.VMEM((stack, BLOCK), F32),
            pltpu.VMEM((most, stack, TILE), F32),
            pltpu.SemaphoreType.DMA((2, blocks)),
        ],
        out_shape=[
            jax.ShapeDtypeStruct((rows, width), BF16),
            jax.ShapeDtypeStruct((blocks, heads, BLOCK, width), BF16),
            jax.ShapeDtypeStruct((blocks, stack, BLOCK), F32),
        ],
        compiler_params=pltpu.CompilerParams(vmem_limit_bytes=62 << 20),
        cost_estimate=cost(4 * rows * 1024 * stack // BLOCK * width, 4 * rows * stack // BLOCK * width),
        name="attend",
    )(query, k_all, v_all, segs, segs[:, None, :], pre, post)


def backward_kernel(
    heads, groups, q_ref, g_ref, u_ref, lse_ref, k_all, v_all, seg_low, seg_ref, pre_ref, post_ref,
    dq_ref, dk_ref, dv_ref, small_ref,
    dpre_ref, dpost_ref, k_s, v_s, seg_s, dk_s, dv_s, qp_s, gp_s, d_s, t_s, sems,
):
    step = pl.program_id(0)
    core = lax.axis_index("core")
    block = 2 * step + core
    width = q_ref.shape[1]
    arrive(step, [k_all, v_all], [k_s, v_s], sems, seg_ref, seg_s)

    @pl.when(step == 0)
    def _():
        dk_s[...] = jnp.zeros(dk_s.shape, F32)
        dv_s[...] = jnp.zeros(dv_s.shape, F32)
        dpre_ref[...] = jnp.zeros(dpre_ref.shape, F32)
        dpost_ref[...] = jnp.zeros(dpost_ref.shape, F32)

    tiles = reach(block, seg_low)
    row_seg = rows_of(block, seg_s)

    def opening(g, per):
        query, grad_low = q_ref[...], g_ref[...]
        grad = grad_low.astype(F32)
        left, right, terms = [], [], []
        for h in range(g * per, (g + 1) * per):
            gain = post_ref[h : h + 1, :]
            left.append(query * pre_ref[h : h + 1, :])
            right.append(grad_low * gain.astype(BF16))
            both = grad * u_ref[0, h].astype(F32)
            terms.append(jnp.sum(both * gain, axis=-1, keepdims=True))
            dpost_ref[h] += jnp.sum(both.reshape(BLOCK // 8, 8, -1), axis=0)
        return jnp.concatenate(left), jnp.concatenate(right), jnp.concatenate(terms)

    def closing(h, part, dq):
        dpre_ref[h] += jnp.sum((q_ref[...].astype(F32) * part).reshape(BLOCK // 8, 8, -1), axis=0)
        return dq + part * pre_ref[h : h + 1, :].astype(F32)

    def tile_part(first, mask, g, left, right, term):
        size = left.shape[0]
        per = size // BLOCK
        keys = k_s[pl.ds(first, 2)].reshape(TILE, -1)
        values = v_s[pl.ds(first, 2)].reshape(TILE, -1)
        s = (right_t(left, keys).reshape(per, BLOCK, TILE) + mask[None]).reshape(size, TILE)
        top = lse_ref[0, g * size : (g + 1) * size, :]
        p = jnp.exp(s - jnp.concatenate([top, top], axis=1))
        dw = right_t(right, values)
        ds = (p * (dw - term)).astype(BF16)
        return matmul(ds, keys), left_t(ds, left), left_t(p.astype(BF16), right)

    def add_up(first, dk, dv):
        dk_s[pl.ds(first, 2)] += dk.reshape(2, BLOCK, -1)
        dv_s[pl.ds(first, 2)] += dv.reshape(2, BLOCK, -1)

    @pl.when(tiles == 1)
    def _():
        mask = row_mask(row_seg, block, block, seg_s)
        dk = dv = jnp.zeros((TILE, width), F32)
        dq = jnp.zeros((BLOCK, width), F32)
        per = heads // groups[0]
        for g in range(groups[0]):
            part, a, b = tile_part(block, mask, g, *opening(g, per))
            dk, dv = dk + a, dv + b
            for k in range(per):
                dq = closing(g * per + k, part[k * BLOCK : (k + 1) * BLOCK], dq)
        add_up(block, dk, dv)
        dq_ref[...] = dq.astype(BF16)

    @pl.when(tiles > 1)
    def _():
        mask = row_mask(row_seg, block, block, seg_s)
        dk = dv = jnp.zeros((TILE, width), F32)
        per = heads // groups[1]
        size = per * BLOCK
        for g in range(groups[1]):
            rows = slice(g * size, (g + 1) * size)
            left, right, term = opening(g, per)
            qp_s[rows, :], gp_s[rows, :] = left, right
            d_s[rows, :] = jnp.broadcast_to(term, (size, BLOCK))
            t_s[rows, :], a, b = tile_part(block, mask, g, left, right, term)
            dk, dv = dk + a, dv + b
        add_up(block, dk, dv)

        def more(tile, carry):
            first = block - 2 * tile
            mask = row_mask(row_seg, first, block, seg_s)
            dk = dv = jnp.zeros((TILE, width), F32)
            size = heads // groups[2] * BLOCK
            for g in range(groups[2]):
                rows = slice(g * size, (g + 1) * size)
                term = jnp.concatenate([d_s[rows, :]] * 2, axis=1)
                part, a, b = tile_part(first, mask, g, qp_s[rows, :], gp_s[rows, :], term)
                t_s[rows, :] += part
                dk, dv = dk + a, dv + b
            add_up(first, dk, dv)
            return carry

        lax.fori_loop(1, tiles, more, 0)
        dq = jnp.zeros((BLOCK, width), F32)
        for h in range(heads):
            dq = closing(h, t_s[h * BLOCK : (h + 1) * BLOCK, :], dq)
        dq_ref[...] = dq.astype(BF16)

    @pl.when(step == pl.num_programs(0) - 1)
    def _():
        for k in range(dk_ref.shape[0]):
            dk_ref[k] = dk_s[k + 1].astype(BF16)
            dv_ref[k] = dv_s[k + 1].astype(BF16)
        sums = [jnp.sum(ref[h], axis=0, keepdims=True) for ref in (dpre_ref, dpost_ref) for h in range(heads)]
        row = lax.broadcasted_iota(jnp.int32, (width, BLOCK), 0)
        col = lax.broadcasted_iota(jnp.int32, (width, BLOCK), 1)
        member = (row // (width // heads) == col).astype(F32)
        mixes = jnp.dot(
            jnp.concatenate(sums), member, preferred_element_type=F32, precision=lax.Precision.HIGHEST
        )
        lines = 2 * heads * BLOCK // width
        small_ref[...] = jnp.zeros(small_ref.shape, F32)
        small_ref[:lines, :] = jnp.concatenate(
            [mixes[k * lines : (k + 1) * lines] for k in range(width // BLOCK)], axis=1
        )


def attend_back(query, grad, u, lse, k_all, v_all, segs, pre, post):
    heads, width = pre.shape
    rows, stack = query.shape[0], heads * BLOCK
    blocks = rows // BLOCK
    groups = BACKWARD_GROUPS
    lines = 2 * heads * BLOCK // width + 2
    lines += -lines % 8
    by_block = pl.BlockSpec((BLOCK, width), lambda i: (i, 0))
    return pl.pallas_call(
        functools.partial(backward_kernel, heads, groups),
        grid=(blocks,),
        in_specs=[
            by_block,
            by_block,
            pl.BlockSpec((1, heads, BLOCK, width), lambda i: (i, 0, 0, 0)),
            pl.BlockSpec((1, stack, BLOCK), lambda i: (i, 0, 0)),
            ANY, ANY, SCALARS, whole((2 * blocks, 1, BLOCK)), whole(pre.shape), whole(post.shape),
        ],
        out_specs=[
            by_block,
            whole((2 * blocks, BLOCK, width)),
            whole((2 * blocks, BLOCK, width)),
            whole((lines, width)),
        ],
        scratch_shapes=[
            pltpu.VMEM((heads, 8, width), F32),
            pltpu.VMEM((heads, 8, width), F32),
            pltpu.VMEM((2 * blocks + 1, BLOCK, width), BF16),
            pltpu.VMEM((2 * blocks + 1, BLOCK, width), BF16),
            pltpu.VMEM((2 * blocks + 1, 1, BLOCK), jnp.int32),
            pltpu.VMEM((2 * blocks + 1, BLOCK, width), F32),
            pltpu.VMEM((2 * blocks + 1, BLOCK, width), F32),
            pltpu.VMEM((stack, width), BF16),
            pltpu.VMEM((stack, width), BF16),
            pltpu.VMEM((stack, BLOCK), F32),
            pltpu.VMEM((stack, width), F32),
            pltpu.SemaphoreType.DMA((2, blocks)),
        ],
        out_shape=[
            jax.ShapeDtypeStruct((rows, width), BF16),
            jax.ShapeDtypeStruct((2 * blocks, BLOCK, width), BF16),
            jax.ShapeDtypeStruct((2 * blocks, BLOCK, width), BF16),
            jax.ShapeDtypeStruct((lines, width), F32),
        ],
        compiler_params=pltpu.CompilerParams(vmem_limit_bytes=62 << 20),
        cost_estimate=cost(10 * rows * 1024 * stack // BLOCK * width, 4 * rows * stack // BLOCK * width),
        name="attend_back",
    )(query, grad, u, lse, k_all, v_all, segs, segs[:, None, :], pre, post)


MESH = pl.DeviceIdType.MESH


def device(place):
    d, t = place
    return d // 2, d % 2, t


def flip(index, bit):
    return index + bit - 2 * bit * ((index // bit) % 2)


def greet(nd, nt, d, t):
    barrier = pltpu.get_barrier_semaphore()
    core = d % 2
    partners = [(d, lax.rem(t + s, nt)) for s in range(1, nt)]
    partners += [(flip(d, 1), lax.rem(t + s, nt)) for s in range(nt)]
    partners += [(flips(d, mask), t) for mask in range(2, nd, 2)]
    for partner in partners:
        pl.semaphore_signal(barrier, inc=1, device_id=device(partner), device_id_type=MESH)
    pl.semaphore_wait(barrier, len(partners))


def remote(src, dst, send_sem, recv_sem, to):
    return pltpu.make_async_remote_copy(
        src_ref=src, dst_ref=dst, send_sem=send_sem, recv_sem=recv_sem, device_id=device(to), device_id_type=MESH
    )


def start_kernel(
    nd, nt, share, halves, *refs,
):
    tokens, grads, segments, pre_mix, post_mix = refs[:5]
    later = refs[5:7] if halves else refs[5:6]
    refs = refs[5 + len(later) - 4 :]
    if halves:
        weights, norms = refs[4:8], refs[8]
        x_out, q_out, k_out, v_out, seg_out, pre_out, post_out, mail_out, later_out, w_out, o_out, gain_out, near_out = refs[9:22]
        wg_s, w_send, w_recv, n_send, n_recv, n_self = refs[22:28]
    else:
        w_out, gain_out = refs[4:6]
        x_out, q_out, k_out, v_out, seg_out, pre_out, post_out, mail_out, later_out = refs[6:15]
    (g_send, g_recv, g_self, l_send, l_recv, x_s, kv_s, x_send, x_recv, x_self, kv_send, kv_recv, kv_self, seg_send, seg_recv, seg_self) = refs[-16:]
    d, t = 2 * lax.axis_index("plane") + lax.axis_index("core"), lax.axis_index("tensor")
    core = d % 2
    width = x_out.shape[1]
    micro = tokens.shape[0]
    per = tokens.shape[1]
    greet(nd, nt, d, t)

    n_copies = []
    if halves:
        for k, weight in enumerate(later):
            there = near_out.at[d // 2, pl.ds(k * weight.shape[0], weight.shape[0])]
            n_copies.append(pltpu.make_async_copy(weight, there, n_self.at[k]))
            for mask in range(2, nd, 2):
                sems = n_send.at[k, mask // 2], n_recv.at[k, mask // 2]
                n_copies.append(remote(weight, there, *sems, (flips(d, mask), t)))
        for copy in n_copies:
            copy.start()

    if halves:
        line = lax.broadcasted_iota(jnp.int32, (8, width), 0)
        lane = lax.broadcasted_iota(jnp.int32, (8, width), 1)
        gains = jnp.zeros((8, width), F32)
        for n in range(2):
            for k in range(share):
                here = (line == n) & (lane == (d * nt + t) * share + k)
                gains = jnp.where(here, norms[n, k], gains)
        own = [weight[...].astype(F32) for weight in weights] + [gains]
        rest = wg_s.shape[2] - 4 * share - 8
        own = own + ([jnp.zeros((rest, width), F32)] if rest else [])
        wg_s[d, t] = jnp.concatenate(own).astype(BF16)
        z_copies = []
        for s in range(1, nt):
            slab = wg_s.at[d, t]
            copy = remote(slab, slab, w_send.at[0, 0, s], w_recv.at[0, 0, s], (d, lax.rem(t + s, nt)))
            copy.start()
            z_copies.append(copy)

    heads = pre_mix.shape[0]
    lane = lax.broadcasted_iota(jnp.int32, (heads, width), 1) // (width // heads)
    member = (lane == lax.broadcasted_iota(jnp.int32, (heads, width), 0)).astype(BF16)
    pre_out[...] = (left_t(pre_mix[...], member) * (width // heads) ** (-0.5)).astype(BF16)
    post_out[...] = matmul(post_mix[...], member)

    g_copies = []
    for m in range(micro):
        there = mail_out.at[2 * m + core]
        g_copies.append(pltpu.make_async_copy(grads.at[m, :, core], there, g_self.at[m]))
        g_copies.append(remote(grads.at[m, :, 1 - core], there, g_send.at[m], g_recv.at[m], (flip(d, 1), t)))
    for copy in g_copies:
        copy.start()

    sends = []
    for m in range(micro):
        for c in range(2):
            to = (d - core + c, 2 * m + core)
            here = (to[0] == d) & (to[1] == t)
            src, dst = tokens.at[m, :, c], x_s.at[pl.ds(per * t, per)]
            far = remote(src, dst, x_send.at[2 * m + c], x_recv.at[t], to)
            near = pltpu.make_async_copy(src, dst, x_self)
            pl.when(jnp.logical_not(here))(far.start)
            pl.when(here)(near.start)
            sends.append((here, far, near))

    holder = t % 2 == core
    seg_here = pltpu.make_async_copy(segments.at[t // 2], seg_out, seg_self)
    seg_there = remote(segments.at[t // 2], seg_out, seg_send, seg_recv, (flip(d, 1), t))

    @pl.when(holder)
    def _():
        seg_here.start()
        seg_there.start()

    l_copies = []
    for s in range(1, nt):
        for k, weight in enumerate(later):
            there = later_out.at[s - 1]
            if len(later) > 1:
                there = later_out.at[s - 1, pl.ds(k * weight.shape[0], weight.shape[0])]
            l_copies.append(remote(weight, there, l_send.at[s, k], l_recv.at[s, k], (d, lax.rem(t + s, nt))))
    for copy in l_copies:
        copy.start()

    if halves:
        bits = [1 << k for k in range(1, nd.bit_length() - 1)]
        routes = [bits + [1], bits[::-1] + [1]]
        have = [[0] for _ in halves]
        for copy in z_copies:
            copy.wait()
        for stage in range(len(bits) + 1):
            copies = []
            for h, (lo, hi) in enumerate(halves):
                bit = routes[h][stage]
                for k, mask in enumerate(have[h]):
                    slab = d
                    for b in [1 << j for j in range(nd.bit_length() - 1)]:
                        if mask & b:
                            slab = flip(slab, b)
                    ref = wg_s.at[slab, :, pl.ds(lo, hi - lo)]
                    copies.append(
                        remote(ref, ref, w_send.at[1 + h, stage, k], w_recv.at[1 + h, stage, k], (flip(d, bit), t))
                    )
                have[h] = have[h] + [mask | bit for mask in have[h]]
            for copy in copies:
                copy.start()
            for copy in copies:
                copy.wait()

        gains = jnp.zeros((8, width), F32)
        for pair in range(nd * nt // 2):
            slabs = [wg_s[(2 * pair + e) // nt, (2 * pair + e) % nt].astype(F32) for e in range(2)]
            for k in range(3):
                both = jnp.concatenate([slab[k * share : (k + 1) * share] for slab in slabs])
                w_out[2 * pair * share : 2 * (pair + 1) * share, k * width : (k + 1) * width] = both.astype(BF16)
            both = jnp.concatenate([slab[3 * share : 4 * share] for slab in slabs])
            o_out[2 * pair * share : 2 * (pair + 1) * share, :] = both.astype(BF16)
            gains = gains + (slabs[0] + slabs[1])[4 * share : 4 * share + 8]
        gain_out[...] = gains

    kv_copies = []
    gain = gain_out[:1]
    for s in range(nt):
        source = lax.rem(t + s, nt)
        here = (source == t) & holder
        arrival = remote(
            x_s.at[pl.ds(per * source, per)], x_s.at[pl.ds(per * source, per)], x_send.at[0], x_recv.at[source], (flip(d, 1), t)
        )
        local = pltpu.make_async_copy(tokens.at[0, :, 0], x_s.at[pl.ds(per * source, per)], x_self)
        pl.when(jnp.logical_not(here))(arrival.wait_recv)
        pl.when(here)(local.wait)
        x = x_s[pl.ds(per * source, per)].reshape(per * BLOCK, width)
        rows = pl.ds(pl.multiple_of(source * per * BLOCK, per * BLOCK), per * BLOCK)
        x_out[rows, :] = x
        x = x.astype(F32)
        h = (x * rms_scale(x) * gain).astype(BF16)
        q_out[rows, :] = matmul(h, w_out[:, :width]).astype(BF16)
        for k, out in enumerate((k_out, v_out)):
            value = matmul(h, w_out[:, (k + 1) * width : (k + 2) * width]).astype(BF16)
            kv_s[k, s] = value.reshape(per, BLOCK, width)
            dst = out.at[pl.ds(per * source, per), core]
            near = pltpu.make_async_copy(kv_s.at[k, s], dst, kv_self.at[k, s])
            far = remote(kv_s.at[k, s], dst, kv_send.at[k, s], kv_recv.at[k, s], (flip(d, 1), t))
            near.start()
            far.start()
            kv_copies += [near, far]
    for copy in kv_copies + l_copies + n_copies + g_copies:
        copy.wait()
    for here, far, near in sends:
        pl.when(jnp.logical_not(here))(far.wait_send)

    @pl.when(holder)
    def _():
        seg_here.wait()
        seg_there.wait_send()

    @pl.when(jnp.logical_not(holder))
    def _():
        seg_there.wait_recv()


def start(tokens, grads, segments, pre_mix, post_mix, weights, norms, up, down):
    micro, _, rows, width = tokens.shape
    nd, nt = 2 * lax.axis_size("plane"), lax.axis_size("tensor")
    count = rows * nt // 2
    blocks = count // BLOCK
    per = blocks // nt
    share = weights[0].shape[0]
    length = 4 * share + 8 + -(4 * share + 8) % 16
    dma = pltpu.SemaphoreType.DMA
    vmem = pl.BlockSpec(memory_space=pltpu.VMEM)
    shaped = jax.ShapeDtypeStruct
    most = max(nd // 2, nt)
    inside = 2 * share % 16 == 0 and length >= 32
    middle = length // 32 * 16
    if inside:
        halves, given = [(0, middle), (middle, length)], [*weights, jnp.stack(norms).astype(F32)]
        given_specs = [vmem] * 4 + [SCALARS]
        gathered_specs = [vmem, vmem, vmem, vmem]
        gathered = [shaped((width, 3 * width), BF16), shaped((width, width), BF16), shaped((8, width), F32)]
        gathered.append(shaped((nd // 2, 2 * up.shape[0], up.shape[1]), BF16))
        later = [up, down]
        scratch = [
            pltpu.VMEM((nd, nt, length, width), BF16),
            dma((3, nd.bit_length(), most)), dma((3, nd.bit_length(), most)),
            dma((2, nd // 2)), dma((2, nd // 2)), dma((2,)),
        ]
    else:
        place = (lax.axis_index("plane") * 2 * nt + lax.axis_index("core") * nt + lax.axis_index("tensor")) * share
        gains = lax.dynamic_update_slice(jnp.zeros((8, width), BF16), jnp.stack(norms), (0, place))
        slabs = lax.all_gather(jnp.concatenate([*weights, gains]), AXES, axis=0, tiled=False)
        w_qkv = slabs[:, : 3 * share].reshape(nd * nt, 3, share, width).transpose(0, 2, 1, 3)
        w_qkv = w_qkv.reshape(width, 3 * width)
        w_out = slabs[:, 3 * share : 4 * share].reshape(width, width)
        gains = jnp.sum(slabs[:, 4 * share : 4 * share + 8].astype(F32), axis=0)
        halves, given, given_specs, gathered_specs, gathered, scratch = [], [w_qkv, gains], [vmem, vmem], [], [], []
        later = [jnp.concatenate([up, down])]
    results = pl.pallas_call(
        functools.partial(start_kernel, nd, nt, share, halves),
        in_specs=[ANY, ANY, ANY, vmem, vmem] + [ANY] * len(later) + given_specs,
        out_specs=[vmem, vmem, ANY, ANY, ANY, vmem, vmem, vmem, ANY] + gathered_specs,
        out_shape=[
            shaped((count, width), BF16),
            shaped((count, width), BF16),
            shaped((blocks, 2, BLOCK, width), BF16),
            shaped((blocks, 2, BLOCK, width), BF16),
            shaped((2 * blocks, BLOCK), jnp.int32),
            shaped((pre_mix.shape[0], width), BF16),
            shaped((pre_mix.shape[0], width), F32),
            shaped((nt, per, BLOCK, width), BF16),
            shaped((nt - 1, 2 * up.shape[0], up.shape[1]), BF16),
            *gathered,
        ],
        scratch_shapes=scratch + [
            dma((micro,)), dma((micro,)), dma((micro,)),
            dma((nt, 2)), dma((nt, 2)),
            pltpu.VMEM((blocks, BLOCK, width), BF16),
            pltpu.VMEM((2, nt, per, BLOCK, width), BF16),
            dma((nt,)), dma((nt,)), dma,
            dma((2, nt)), dma((2, nt)), dma((2, nt)),
            dma, dma, dma,
        ],
        compiler_params=pltpu.CompilerParams(
            collective_id=0, has_side_effects=True, vmem_limit_bytes=62 << 20
        ),
        name="start",
    )(
        tokens.reshape(micro, rows // TILE, 2, BLOCK, width),
        grads.reshape(micro, rows // TILE, 2, BLOCK, width),
        segments.reshape(micro, 2 * blocks, BLOCK),
        pre_mix,
        post_mix,
        *later,
        *given,
    )
    if inside:
        rest = [results[8]] + [send(results[8], by_bit(mask)) for mask in range(2, nd, 2)]
        return (*results[:8], results[12], rest, *results[9:12])
    near = lax.all_gather(later[0], ("plane", "core"), axis=0, tiled=False).reshape(nd // 2, 2, *later[0].shape)
    rest = lax.all_gather(results[8], ("plane", "core"), axis=0, tiled=False).reshape(nd // 2, 2, *results[8].shape)
    return (*results[:8], near, [rest], w_qkv, w_out, gains)


def gelu_parts(v):
    t = 1.0 / (1.0 + 0.23164189 * jnp.abs(v))
    bell = jnp.exp(-0.5 * v * v)
    series = t * (0.127414796 + t * (-0.142248368 + t * (0.7107068705 + t * (-0.7265760135 + t * 0.5307027145))))
    tail = series * bell
    return jnp.where(v < 0.0, tail, 1.0 - tail), 0.3989422804 * bell


def middle_kernel(rb, nd, nt, share, inside, *refs):
    x_ref, att_ref, w_out, gain_ref, near_all, dy_all = refs[:6]
    pieces = nd // 2 if inside else 1
    rest_all, refs = refs[6 : 6 + pieces], refs[pieces - 1 :]
    mail_ref, after_ref, datt_ref, dwo_ref, dgain_ref, part_ref, last_ref = refs[7:14]
    dy_ref, h_s, ht_s, dyt_s, o_s, dh_s, hid_s, dhid_s, w_s, dy_sem, w_self = refs[14:25]
    if inside:
        g_s, core_s, plane_s, c_send, c_recv, p_send, p_recv, w_send, w_recv = refs[25:]
    step = pl.program_id(0)
    d, t = 2 * lax.axis_index("plane") + lax.axis_index("core"), lax.axis_index("tensor")
    count, width = x_ref.shape
    parts = range(0, count, rb)
    bits = [1 << k for k in range(1, nd.bit_length() - 1)]
    routes = [bits, bits[::-1]]

    def weight_copies(k):
        if not inside:
            return [pltpu.make_async_copy(rest_all[0].at[:, :, k - 1] if k else near_all, w_s.at[k], w_self.at[k, 0])]
        pairs = [(near_all, w_s.at[k, :, d % 2])]
        if k:
            pairs = [(rest_all[j].at[k - 1], w_s.at[k, flips(d, 2 * j) // 2, d % 2]) for j in range(pieces)]
        copies = []
        for j, (rows, there) in enumerate(pairs):
            copies.append(pltpu.make_async_copy(rows, there, w_self.at[k, j]))
            copies.append(remote(rows, there, w_send.at[k, j], w_recv.at[k, j], (flip(d, 1), t)))
        return copies

    @pl.when(step == 0)
    def _():
        if inside:
            greet(nd, nt, d, t)
        for k in range(nt):
            for copy in weight_copies(k):
                copy.start()
        dy_copy = pltpu.make_async_copy(dy_all, dy_ref, dy_sem)
        dy_copy.start()
        for r in parts:
            rows = slice(r, r + rb)
            after = x_ref[rows, :].astype(F32) + matmul(att_ref[rows, :], w_out[...])
            after_ref[rows, :] = after
            o_s[rows, :] = after
            h = (after * rms_scale(after) * gain_ref[1:2]).astype(BF16)
            h_s[rows, :] = h
            ht_s[:, rows] = h.T
            dh_s[rows, :] = jnp.zeros((rb, width), F32)
        dy_copy.wait()
        for r in parts:
            rows = slice(r, r + rb)
            dyt_s[:, rows] = dy_ref[rows, :].T

    for k in range(nt):

        @pl.when(step == k)
        def _(k=k):
            for copy in weight_copies(k):
                copy.wait()

    def core_copies(slot):
        return [
            remote(
                g_s.at[slot, flips(flip(d, 1), mask)], core_s.at[slot, j],
                c_send.at[slot, j], c_recv.at[slot, j], (flip(d, 1), t),
            )
            for j, mask in enumerate(masks_of(bits))
        ]

    def plane_copies(slot, stage):
        copies = []
        for h in range(2):
            bit, rows = routes[h][stage], pl.ds(h * share, share)
            for j, mask in enumerate(masks_of(routes[h][stage + 1 :])):
                copies.append(
                    remote(
                        g_s.at[slot, flips(flip(d, bit), mask), rows], plane_s.at[slot, stage, j, rows],
                        p_send.at[slot, stage, h, j], p_recv.at[slot, stage, h, j], (flip(d, bit), t),
                    )
                )
        return copies

    def core_done(k):
        slot = lax.rem(k, 2)
        for copy in core_copies(slot):
            copy.wait()
        for j, mask in enumerate(masks_of(bits)):
            mine = flips(d, mask)
            total = (g_s[slot, mine].astype(F32) + core_s[slot, j].astype(F32)).astype(BF16)
            if isinstance(k, int):
                last_ref[j] = total
            else:
                g_s[slot, mine] = total
        for copy in [] if isinstance(k, int) else plane_copies(slot, 0):
            copy.start()

    def plane_done(k, stage):
        slot = lax.rem(k, 2)
        for copy in plane_copies(slot, stage):
            copy.wait()
        for h in range(2):
            rows = slice(h * share, (h + 1) * share)
            for j, mask in enumerate(masks_of(routes[h][stage + 1 :])):
                mine = flips(d, mask)
                total = g_s[slot, mine, rows].astype(F32) + plane_s[slot, stage, j, rows].astype(F32)
                g_s[slot, mine, rows] = total.astype(BF16)
        if stage + 1 < len(bits):
            for copy in plane_copies(slot, stage + 1):
                copy.start()
        else:
            mail_ref[lax.rem(t + nt - k, nt), : 2 * share] = g_s[slot, d]

    def when(condition, stage, *args):
        if inside:
            pl.when(condition)(functools.partial(stage, *args))

    @pl.when(step < nt)
    def _():
        up, down = (w_s[step, :, :, k * share : (k + 1) * share].reshape(width, -1) for k in range(2))
        for point, r in enumerate(parts):
            rows = slice(r, r + rb)
            v = matmul(h_s[rows, :], up)
            cumulative, density = gelu_parts(v)
            hid_s[rows, :] = (v * cumulative).astype(BF16)
            d_hidden = matmul(dy_ref[rows, :], down) * (cumulative + v * density)
            dhid_s[rows, :] = d_hidden.astype(BF16)
            if point == 1:
                when(step >= 1, core_done, step - 1)
        when(step >= 2, plane_done, step - 2, len(bits) - 1)
        slot = lax.rem(step, 2)
        for r in range(0, width, 2 * share):
            rows = slice(r, r + 2 * share)
            for k, (left, right) in enumerate(((ht_s, dhid_s), (dyt_s, hid_s))):
                both = matmul(left[rows, :], right[...]).astype(BF16)
                for e in range(2):
                    grad = both[e * share : (e + 1) * share]
                    if inside:
                        g_s[slot, r // share + e, k * share : (k + 1) * share] = grad
                    else:
                        part_ref[r // share + e, 0, k] = grad
                        last_ref[...] = jnp.zeros(last_ref.shape, BF16)
        if inside:
            for copy in core_copies(slot):
                copy.start()
        for r in parts:
            rows = slice(r, r + rb)
            o_s[rows, :] += right_t(hid_s[rows, :], down)
            dh_s[rows, :] += right_t(dhid_s[rows, :], up)
        for stage in range(len(bits) - 1):
            when(step >= 1, plane_done, step - 1, stage)

    @pl.when(step == nt)
    def _():
        gain = gain_ref[1:2]
        total = jnp.zeros((8, width), F32)
        mail_ref[:, mail_ref.shape[1] - count // nt :] = o_s[...].astype(BF16).reshape(nt, count // nt, width)
        for point, r in enumerate(parts):
            rows = slice(r, r + rb)
            after = after_ref[rows, :]
            scale = rms_scale(after)
            normed = after * scale
            dh = dh_s[rows, :]
            total = total + jnp.sum((dh * normed).reshape(rb // 8, 8, width), axis=0)
            d_after = dy_ref[rows, :].astype(F32) + rms_back(dh, normed, scale, gain)
            after_ref[rows, :] = d_after
            branch = d_after.astype(BF16)
            hid_s[rows, :] = branch
            datt_ref[rows, :] = right_t(branch, w_out[...]).astype(BF16)
            if inside and point == 0:
                core_done(nt - 1)
        if inside:
            plane_done(step - 2, len(bits) - 1)
        dgain_ref[...] = total
        dwo_ref[...] = left_t(att_ref[...], hid_s[...]).astype(BF16)
        if inside:
            part_ref[...] = jnp.zeros(part_ref.shape, BF16)
            mail_ref[lax.rem(t + 1, nt), : 2 * share] = jnp.zeros((2 * share, width), BF16)


def feed_forward(x, attended, dy, w_out, gain, near, rest, nd):
    count, width = x.shape
    nt, units = rest[0].shape[-3] + 1, rest[0].shape[-1]
    share = rest[0].shape[-2] // 2
    inside = share % 16 == 0 and nd >= 8
    rb = 256
    rows = whole((count, width))
    mail = (nt, count // nt + (2 * share if inside else 0), width)
    dma = pltpu.SemaphoreType.DMA
    scratch = [
        pltpu.VMEM((count, width), BF16),
        pltpu.VMEM((count, width), BF16),
        pltpu.VMEM((width, count), BF16),
        pltpu.VMEM((width, count), BF16),
        pltpu.VMEM((count, width), F32),
        pltpu.VMEM((count, width), F32),
        pltpu.VMEM((count, units), BF16),
        pltpu.VMEM((count, units), BF16),
        pltpu.VMEM((nt, nd // 2, 2, 2 * share, units), BF16),
        dma, dma((nt, nd // 2)),
    ]
    if inside:
        stages = nd.bit_length() - 2
        grads, grads_spec = jax.ShapeDtypeStruct((8, units), BF16), whole((8, units))
        scratch += [
            pltpu.VMEM((2, nd, 2 * share, units), BF16),
            pltpu.VMEM((2, nd // 2, 2 * share, units), BF16),
            pltpu.VMEM((2, stages, nd // 4, 2 * share, units), BF16),
            dma((2, nd // 2)), dma((2, nd // 2)),
            dma((2, stages, 2, nd // 4)), dma((2, stages, 2, nd // 4)),
            dma((nt, nd // 2)), dma((nt, nd // 2)),
        ]
        params = dict(collective_id=2, has_side_effects=True)
    else:
        grads = jax.ShapeDtypeStruct((nd, nt, 2, share, units), BF16)
        grads_spec = pl.BlockSpec((nd, 1, 2, share, units), lambda s: (0, jnp.minimum(s, nt - 1), 0, 0, 0))
        params = {}
    return pl.pallas_call(
        functools.partial(middle_kernel, rb, nd, nt, share, inside),
        grid=(nt + 1,),
        in_specs=[
            rows, rows, whole((width, width)), whole((8, width)), ANY, ANY,
        ] + [ANY] * len(rest),
        out_specs=[whole(mail), rows, rows, whole((width, width)), whole((8, width)), grads_spec, whole((nd // 2, 2 * share, units))],
        out_shape=[
            jax.ShapeDtypeStruct(mail, BF16),
            jax.ShapeDtypeStruct((count, width), F32),
            jax.ShapeDtypeStruct((count, width), BF16),
            jax.ShapeDtypeStruct((width, width), BF16),
            jax.ShapeDtypeStruct((8, width), F32),
            grads,
            jax.ShapeDtypeStruct((nd // 2, 2 * share, units), BF16),
        ],
        scratch_shapes=scratch,
        compiler_params=pltpu.CompilerParams(vmem_limit_bytes=62 << 20, **params),
        cost_estimate=cost(12 * count * width * nt * units, 4 * nd * nt * share * units),
        name="feed_forward",
    )(x, attended, w_out, gain, near, dy, *rest)


def masks_of(bits):
    masks = [0]
    for bit in bits:
        masks = masks + [mask | bit for mask in masks]
    return masks


def flips(index, mask):
    bit = 1
    while bit <= mask:
        if mask & bit:
            index = flip(index, bit)
        bit *= 2
    return index


def finish_kernel(
    nd, nt, share, inside, x_all, dq_all, dk_all, dv_all, after_all, w_all, gain_ref, dwo_all, small_ref,
    ffn_ref, back, *refs,
):
    last_refs, refs = refs[: nd // 2], refs[nd // 2 :]
    tok_out, out_out, dw_out, small_out, last_out = refs[:5]
    own_s, other_s, grads_s, ht_s, tok_s, own_sems, kv_send, kv_recv, tok_send, tok_recv, tok_self = refs[5:16]
    b_send, b_recv, b_self, x_ref, dq_ref, after_ref, w_ref, dwo_ref, in_sems, last4_s, last_sems, last_s, l_send, l_recv = refs[16:30]
    if inside:
        slab_s, core_s, plane_s, mine_s, z_s, sm_s, sm_in, g_send, g_recv, s_send, s_recv = refs[30:]
    d, t = 2 * lax.axis_index("plane") + lax.axis_index("core"), lax.axis_index("tensor")
    core = d % 2
    count, width = x_all.shape
    per = tok_out.shape[1]
    rows_in = per * BLOCK
    holder = t % 2 == core
    bits = [1 << k for k in range(1, nd.bit_length() - 1)]
    loads = [
        pltpu.make_async_copy(far, near, in_sems.at[k])
        for k, (far, near) in enumerate(
            ((dq_all, dq_ref), (w_all, w_ref), (x_all, x_ref), (after_all, after_ref), (dwo_all, dwo_ref))
        )
    ]
    own = [pltpu.make_async_copy(a.at[:, core], own_s.at[k], own_sems.at[k]) for k, a in enumerate((dk_all, dv_all))]
    loads += [pltpu.make_async_copy(far, last4_s.at[k], last_sems.at[k]) for k, far in enumerate(last_refs)]
    for copy in own + loads:
        copy.start()
    greet(nd, nt, d, t)

    order = [lax.rem(t + s, nt) for s in list(range(1, nt)) + [0]]
    exchanged = []
    for s, source in enumerate(order):
        pair = []
        for k, a in enumerate((dk_all, dv_all)):
            pair.append(
                remote(
                    a.at[pl.ds(per * source, per), 1 - core], other_s.at[k, pl.ds(per * source, per)],
                    kv_send.at[k, s], kv_recv.at[k, s], (flip(d, 1), t),
                )
            )
        exchanged.append(pair)
    for copy in exchanged[0] + exchanged[1]:
        copy.start()
    b_copies = []
    skip = back.shape[1] - rows_in
    for m in range(out_out.shape[0]):
        for k in range(per):
            there, lines = out_out.at[m, k, core], pl.ds(skip + k * BLOCK, BLOCK)
            b_copies.append(pltpu.make_async_copy(back.at[2 * m + core, lines], there, b_self.at[m, k]))
            b_copies.append(
                remote(back.at[2 * m + 1 - core, lines], there, b_send.at[m, k], b_recv.at[m, k], (flip(d, 1), t))
            )
    gain = gain_ref[:1]

    def norms(rows):
        x = x_ref[rows, :].astype(F32)
        scale = rms_scale(x)
        return x * scale, scale

    routes = [[1] + bits, [1] + bits[::-1]]
    rows_of_slab = width // nd

    def fill(bundle, which, left, right):
        for k in range(nd):
            lines = slice(k * rows_of_slab, (k + 1) * rows_of_slab)
            if k % 2 == 0:
                both = matmul(left[lines.start : lines.stop + rows_of_slab, :], right)
                slab_s[bundle, which, k : k + 2] = both.astype(BF16).reshape(2, rows_of_slab, width)

    def stage_copies(bundle, stage):
        copies, adds = [], []
        for h in range(2):
            bit = routes[h][stage]
            for k, mask in enumerate(masks_of(routes[h][stage + 1 :])):
                buffer = core_s.at[bundle] if stage == 0 else plane_s.at[bundle, stage - 1]
                copies.append(
                    remote(
                        slab_s.at[bundle, h, flips(flip(d, bit), mask)], buffer.at[h, k],
                        g_send.at[bundle, h, stage, k], g_recv.at[bundle, h, stage, k], (flip(d, bit), t),
                    )
                )
                adds.append((h, flips(d, mask), buffer, k))
        return copies, adds

    def stage_start(bundle, stage):
        for copy in stage_copies(bundle, stage)[0]:
            copy.start()

    def stage_done(bundle, stage):
        copies, adds = stage_copies(bundle, stage)
        for copy in copies:
            copy.wait()
        last = stage == len(bits)
        totals = []
        for h, mine, buffer, k in adds:
            total = slab_s[bundle, h, mine].astype(F32) + buffer[h, k].astype(F32)
            if last:
                totals.append(total.reshape(nt, share, width))
            else:
                slab_s[bundle, h, mine] = total.astype(BF16)
        if last:
            mine_s[bundle] = jnp.concatenate(totals, axis=1).astype(BF16)

    def z_copies(bundle):
        copies = []
        for s in range(1, nt):
            to = lax.rem(t + s, nt)
            copies.append(
                remote(
                    mine_s.at[bundle, to], z_s.at[bundle, s],
                    g_send.at[bundle, 2, 0, s], g_recv.at[bundle, 2, 0, s], (d, to),
                )
            )
        return copies

    def small_copies(stage):
        if stage <= len(bits):
            return [remote(sm_s, sm_in.at[stage], s_send.at[stage], s_recv.at[stage], (flip(d, routes[0][stage]), t))]
        copies = []
        for s in range(1, nt):
            k = len(bits) + s
            copies.append(remote(sm_s, sm_in.at[k], s_send.at[k], s_recv.at[k], (d, lax.rem(t + s, nt))))
        return copies

    sends, gains = [], []
    to_core = d - core + t % 2

    def sum_group(s):
        source = order[s]
        for copy in exchanged[s]:
            copy.wait()
        for copy in exchanged[s + 2] if s + 2 < nt else []:
            copy.start()
        rows = pl.ds(pl.multiple_of(source * rows_in, rows_in), rows_in)
        grads_s[rows, :width] = dq_ref[rows, :]
        for k in range(2):
            total = own_s[k, pl.ds(per * source, per)].astype(F32) + other_s[k, pl.ds(per * source, per)].astype(F32)
            grads_s[rows, (k + 1) * width : (k + 2) * width] = total.reshape(rows_in, width).astype(BF16)

    def token_group(s):
        source = order[s]
        rows = pl.ds(pl.multiple_of(source * rows_in, rows_in), rows_in)
        dh = right_t(grads_s[rows, :], w_ref[...])
        normed, scale = norms(rows)
        gains.append(jnp.sum((dh * normed).reshape(rows_in // 8, 8, width), axis=0))
        tok = after_ref[rows, :] + rms_back(dh, normed, scale, gain)
        tok_s[s] = tok.astype(BF16).reshape(per, BLOCK, width)
        here = (source == t) & holder
        dst = tok_out.at[t // 2, :, core]
        far = remote(tok_s.at[s], dst, tok_send.at[s], tok_recv.at[2 * (t // 2) + core], (to_core, source))
        near = pltpu.make_async_copy(tok_s.at[s], dst, tok_self)
        pl.when(jnp.logical_not(here))(far.start)
        pl.when(here)(near.start)
        sends.append((here, far, near))

    for copy in own + loads:
        copy.wait()
    last_s[...] = sum(last4_s[k].astype(F32) for k in range(last4_s.shape[0])).astype(BF16)
    last = remote(last_s, last_out, l_send, l_recv, (d, lax.rem(t + 1, nt)))
    last.start()
    for r in range(0, count, rows_in):
        lines = slice(r, r + rows_in)
        normed, scale = norms(lines)
        ht_s[:, lines] = (normed * gain).astype(BF16).T
    if inside:
        slab_s[0, 1] = dwo_ref[...].reshape(nd, rows_of_slab, width)
        fill(0, 0, ht_s, dq_ref[...])
        stage_start(0, 0)
    for s in range(nt // 2):
        sum_group(s)
        token_group(s)
    if inside:
        stage_done(0, 0)
        stage_start(0, 1)
    for s in range(nt // 2, nt):
        sum_group(s)
    if inside:
        for which in range(2):
            fill(1, which, ht_s, grads_s[:, (which + 1) * width : (which + 2) * width])
        stage_start(1, 0)
    for s in range(nt // 2, nt):
        token_group(s)

    for copy in b_copies:
        copy.start()
    small = small_ref[...]
    line = lax.broadcasted_iota(jnp.int32, small.shape, 0)
    small = small + jnp.where(line == small.shape[0] - 2, jnp.sum(sum(gains), axis=0, keepdims=True), 0.0)
    small = small + jnp.where(line == small.shape[0] - 1, jnp.sum(ffn_ref[...], axis=0, keepdims=True), 0.0)
    if inside:
        sm_s[...] = small
        tiny = small_copies(0)
        for copy in tiny:
            copy.start()
        for stage in range(len(bits) + 1):
            for copy in tiny:
                copy.wait()
            sm_s[...] += sm_in[stage]
            tiny = small_copies(stage + 1)
            for copy in tiny:
                copy.start()
            stage_done(1, stage)
            if stage < len(bits):
                stage_start(1, stage + 1)
                stage_done(0, stage + 1)
                if stage + 1 < len(bits):
                    stage_start(0, stage + 2)
                else:
                    first_z = z_copies(0)
                    for copy in first_z:
                        copy.start()
        second_z = z_copies(1)
        for copy in second_z:
            copy.start()
        for copy in first_z + second_z + tiny:
            copy.wait()
        for bundle in range(2):
            total = mine_s[bundle, t].astype(F32)
            for s in range(1, nt):
                total = total + z_s[bundle, s].astype(F32)
            dw_out[bundle * 2 * share : (bundle + 1) * 2 * share] = total
        small_out[...] = sm_s[...] + sum(sm_in[len(bits) + s] for s in range(1, nt))
    else:
        small_out[...] = small
        for r in range(0, width, 256):
            lines = slice(r, r + 256)
            dw_out[lines, : 3 * width] = matmul(ht_s[lines, :], grads_s[...]).astype(BF16)
            dw_out[lines, 3 * width :] = dwo_ref[lines, :]

    for copy in b_copies + [last]:
        copy.wait()
    for here, far, near in sends:
        pl.when(jnp.logical_not(here))(far.wait_send)
        pl.when(here)(near.wait)
    for m in range(tok_out.shape[0]):
        for c in range(2):
            here = (2 * m + core == t) & (c == core)
            dst = tok_out.at[m, :, c]
            back = remote(dst, dst, tok_send.at[0], tok_recv.at[2 * m + c], (flip(d, 1), t))
            pl.when(jnp.logical_not(here))(back.wait_recv)


def finish(x, dq, dk_all, dv_all, after, w_qkv, gains, dwo, small, gain_ffn, back, last, share, micro):
    count, width = x.shape
    nd, nt = 2 * lax.axis_size("plane"), lax.axis_size("tensor")
    inside = 2 * share % 16 == 0 and nd >= 8
    blocks = count // BLOCK
    per = blocks // nt
    dma = pltpu.SemaphoreType.DMA
    vmem = pl.BlockSpec(memory_space=pltpu.VMEM)
    shaped = jax.ShapeDtypeStruct
    scratch = [
        pltpu.VMEM((2, blocks, BLOCK, width), BF16),
        pltpu.VMEM((2, blocks, BLOCK, width), BF16),
        pltpu.VMEM((count, 3 * width), BF16),
        pltpu.VMEM((width, count), BF16),
        pltpu.VMEM((nt, per, BLOCK, width), BF16),
        dma((2,)), dma((2, nt)), dma((2, nt)), dma((nt,)), dma((nt,)), dma,
        dma((micro, per)), dma((micro, per)), dma((micro, per)),
        pltpu.VMEM(x.shape, x.dtype), pltpu.VMEM(dq.shape, dq.dtype), pltpu.VMEM(after.shape, after.dtype),
        pltpu.VMEM(w_qkv.shape, w_qkv.dtype), pltpu.VMEM(dwo.shape, dwo.dtype), dma((5,)),
        pltpu.VMEM((nd // 2,) + last[0].shape, BF16), dma((nd // 2,)), pltpu.VMEM(last[0].shape, BF16), dma, dma,
    ]
    if inside:
        most = max(nd // 2, nt)
        stages = nd.bit_length() - 1
        scratch += [
            pltpu.VMEM((2, 2, nd, nt * share, width), BF16),
            pltpu.VMEM((2, 2, nd // 2, nt * share, width), BF16),
            pltpu.VMEM((2, stages - 1, 2, nd // 4, nt * share, width), BF16),
            pltpu.VMEM((2, nt, 2 * share, width), BF16),
            pltpu.VMEM((2, nt, 2 * share, width), BF16),
            pltpu.VMEM(small.shape, F32),
            pltpu.VMEM((stages + nt,) + small.shape, F32),
            dma((2, 3, stages, most)), dma((2, 3, stages, most)), dma((stages + nt,)), dma((stages + nt,)),
        ]
    return pl.pallas_call(
        functools.partial(finish_kernel, nd, nt, share, inside),
        in_specs=[ANY, ANY, ANY, ANY, ANY, ANY, vmem, ANY, vmem, vmem, ANY] + [ANY] * len(last),
        out_specs=[vmem, vmem, vmem, vmem, vmem],
        out_shape=[
            shaped((micro, per, 2, BLOCK, width), BF16),
            shaped((micro, per, 2, BLOCK, width), BF16),
            shaped((4 * share, width), F32) if inside else shaped((width, 4 * width), BF16),
            shaped(small.shape, F32),
            shaped(last[0].shape, BF16),
        ],
        scratch_shapes=scratch,
        compiler_params=pltpu.CompilerParams(
            collective_id=1, has_side_effects=True, vmem_limit_bytes=62 << 20
        ),
        cost_estimate=cost(24 * count * width * width, 16 * count * width),
        name="finish",
    )(x, dq, dk_all, dv_all, after, w_qkv, gains, dwo, small, gain_ffn, back, *last)


def emit_kernel(heads, share, tok_ref, out_ref, dw_ref, ffn_ref, last_ref, small_ref, tok, out, *rest):
    grads, ups, gains, mixes = rest[:4], rest[4:6], rest[6:8], rest[8:10]
    tok[...] = tok_ref[...].astype(F32)
    out[...] = out_ref[...]

    @pl.when(pl.program_id(0) == 0)
    def _():
        for grad, k in zip(grads, (0, 2, 3, 1)):
            grad[...] = dw_ref[k * share : (k + 1) * share]
        half = last_ref.shape[0] // 2
        for k, up in enumerate(ups):
            lines = slice(k * half, (k + 1) * half)
            total = last_ref[lines].astype(F32)
            for z in range(ffn_ref.shape[0]):
                total = total + ffn_ref[z, lines].astype(F32)
            up[...] = total
        width = small_ref.shape[1]
        place = (
            (lax.axis_index("plane") * 2 + lax.axis_index("core")) * lax.axis_size("tensor") + lax.axis_index("tensor")
        ) * share
        row = lax.broadcasted_iota(jnp.int32, (width, share), 0)
        col = lax.broadcasted_iota(jnp.int32, (width, share), 1)
        exact = dict(preferred_element_type=F32, precision=lax.Precision.HIGHEST)
        own = jnp.dot(small_ref[small_ref.shape[0] - 8 :, :], (row == place + col).astype(F32), **exact)
        for k, gain in enumerate(gains):
            gain[...] = own[6 + k : 7 + k]
        lines = 2 * heads * BLOCK // width
        sums = jnp.concatenate(
            [small_ref[:lines, k * BLOCK : (k + 1) * BLOCK] for k in range(width // BLOCK)]
        )[:, :heads]
        mixes[0][...] = sums[:heads].T * (width // heads) ** (-0.5)
        mixes[1][...] = sums[heads:]


def emit(tok, out, dw, ffn, last, small, heads, share):
    width = small.shape[1]
    micro, per, cores, block, _ = tok.shape
    rows = per * cores * block

    def part(k):
        return pl.BlockSpec((1, rows, width), lambda i: (i, 0, 0))

    shaped = jax.ShapeDtypeStruct
    small_shapes = [(share, width)] * 4 + [(last.shape[0] // 2, width)] * 2 + [(1, share)] * 2 + [(heads, heads)] * 2
    return pl.pallas_call(
        functools.partial(emit_kernel, heads, share),
        grid=(micro,),
        in_specs=[part(0), part(1), whole(dw.shape), whole((ffn.shape[0],) + last.shape), whole(last.shape), whole(small.shape)],
        out_specs=[part(0), part(1)] + [whole(shape) for shape in small_shapes],
        out_shape=[shaped((micro, rows, width), F32), shaped((micro, rows, width), BF16)]
        + [shaped(shape, F32) for shape in small_shapes],
        compiler_params=pltpu.CompilerParams(vmem_limit_bytes=62 << 20),
        name="emit",
    )(tok.reshape(micro, rows, width), out.reshape(micro, rows, width), dw, ffn, last, small)


def per_device(
    tokens, segments, w_query, w_key, w_value, w_out, norm_attn, norm_ffn, pre_mix, post_mix, w_up, w_down, out_grad,
):
    micro, _, rows, width = tokens.shape
    nd, nt = 2 * lax.axis_size("plane"), lax.axis_size("tensor")
    heads = pre_mix.shape[0]
    head_width = width // heads
    length = rows * nt
    count = length // 2
    blocks = count // BLOCK
    share = w_query.shape[0]
    bits = [1 << k for k in range(nd.bit_length() - 1)]
    d, t = 2 * lax.axis_index("plane") + lax.axis_index("core"), lax.axis_index("tensor")
    core = d % 2

    x, query, k_all, v_all, segs, pre, post, mail, near, rest, w_qkv, all_out, gains = start(
        tokens, out_grad, segments, pre_mix, post_mix, [w_query, w_key, w_value, w_out], [norm_attn, norm_ffn], w_up, w_down
    )
    k_all, v_all = (a.reshape(2 * blocks, BLOCK, width) for a in (k_all, v_all))
    dy = lax.all_to_all(mail, "tensor", 0, 0, tiled=True).reshape(count, width)
    attended, u, lse = attend(query, k_all, v_all, segs, pre, post)
    mail, grad_after, grad_attended, grad_w_out, grad_gain_ffn, part_both, last_both = feed_forward(
        x, attended, dy, all_out, gains, near, rest, nd
    )
    back = lax.all_to_all(mail, "tensor", 0, 0, tiled=True)
    last_both = [last_both[0]] + [send(last_both[k], by_bit(2 * k)) for k in range(1, nd // 2)]
    if part_both.ndim > 3:
        part_both = lax.dynamic_slice_in_dim(jnp.concatenate([part_both[:, ::-1]] * 2, axis=1), nt - 1 - t, nt, 1)
        part_both = lax.psum_scatter(part_both, ("plane", "core"), scatter_dimension=0, tiled=False)
        part_both = lax.psum_scatter(part_both, "tensor", scatter_dimension=0, tiled=False)
        part_both = part_both.reshape(1, 2 * w_up.shape[0], w_up.shape[1])
    else:
        part_both = back

    grad_query, grad_key, grad_value, small = attend_back(
        query, grad_attended, u, lse, k_all, v_all, segs, pre, post
    )
    d_tokens, out, owned, small, last_both = finish(
        x, grad_query, grad_key.reshape(blocks, 2, BLOCK, width), grad_value.reshape(blocks, 2, BLOCK, width),
        grad_after, w_qkv, gains, grad_w_out, small, grad_gain_ffn, back, last_both, share, micro,
    )
    if owned.dtype == BF16:
        owned = lax.psum_scatter(owned, AXES, scatter_dimension=0, tiled=True).astype(F32)
        owned = jnp.concatenate([owned[:, k * width : (k + 1) * width] for k in (0, 3, 1, 2)])
        small = lax.psum(small, AXES)
    d_tokens, out, *grads = emit(d_tokens, out, owned, part_both, last_both, small, heads, share)
    d_query, d_key, d_value, d_out, d_up, d_down, d_gain_attn, d_gain_ffn, d_pre, d_post = grads
    return (
        out.reshape(tokens.shape),
        d_tokens.reshape(tokens.shape),
        d_query,
        d_key,
        d_value,
        d_out,
        d_gain_attn.reshape(share),
        d_gain_ffn.reshape(share),
        d_pre,
        d_post,
        d_up,
        d_down,
    )


def solution(mesh):
    devices = mesh.devices
    devices = devices.reshape(devices.shape[0] // 2, 2, devices.shape[1])
    dp = ("plane", "core")
    both = P(AXES, None)
    gain = P(AXES)
    data = P(None, dp, "tensor", None)
    ffn = P(dp, "tensor")
    return jax.shard_map(
        per_device,
        mesh=jax.sharding.Mesh(devices, AXES),
        in_specs=(data, P(None, dp, None), both, both, both, both, gain, gain, P(), P(), ffn, ffn, data),
        out_specs=(data, data, both, both, both, both, gain, gain, P(), P(), ffn, ffn),
        check_vma=False,
    )
```

```python
import functools

import jax
import jax.numpy as jnp
from jax import lax
from jax.experimental import pallas as pl
from jax.experimental.pallas import tpu as pltpu
from jax.sharding import PartitionSpec as P

F32 = jnp.float32
BF16 = jnp.bfloat16
BLOCK = 128
TILE = 2 * BLOCK
FORWARD_GROUPS = 6
BACKWARD_GROUPS = (2, 2, 2)
AXES = ("plane", "core", "tensor")


def matmul(left, right):
    return jnp.dot(left, right, preferred_element_type=F32)


def right_t(left, right):
    return lax.dot_general(left, right, (((1,), (1,)), ((), ())), preferred_element_type=F32)


def left_t(left, right):
    return lax.dot_general(left, right, (((0,), (0,)), ((), ())), preferred_element_type=F32)


def rms_scale(values):
    return lax.rsqrt(jnp.mean(values * values, axis=-1, keepdims=True) + 1e-06)


def rms_back(grad_norm, normed, scale, gain):
    scaled = grad_norm * gain
    return scale * (scaled - normed * jnp.mean(scaled * normed, axis=-1, keepdims=True))


def gelu_exact(values):
    return jax.nn.gelu(values, approximate=False)


def gelu_back(upper, grad):
    unused, pull = jax.vjp(gelu_exact, upper)
    return pull(grad)[0]


def send(x, to):
    nd, nt = 2 * lax.axis_size("plane"), lax.axis_size("tensor")
    pairs = []
    for d in range(nd):
        for t in range(nt):
            d2, t2 = to(d, t)
            pairs.append((d * nt + t, d2 * nt + t2))
    return lax.ppermute(x, AXES, pairs)


def by_shift(shift):
    nt = lax.axis_size("tensor")
    return lambda d, t: (d, (t + shift) % nt)


def by_bit(bit):
    return lambda d, t: (d ^ bit, t)


def gather(piece, bits):
    nt = lax.axis_size("tensor")
    have = {0: jnp.stack([piece] + [send(piece, by_shift(s)) for s in range(1, nt)])}
    for bit in bits:
        have.update({mask | bit: send(block, by_bit(bit)) for mask, block in have.items()})
    return [have[mask] for mask in range(len(have))]


def pick(x, index, axis):
    return lax.dynamic_index_in_dim(x, index, axis, keepdims=False)


def sum_to_owner(x, bits):
    nt, nd = x.shape[:2]
    d, t = 2 * lax.axis_index("plane") + lax.axis_index("core"), lax.axis_index("tensor")
    rest = x.shape[2:]
    names = [1 << k for k in range(nd.bit_length() - 1)][::-1]
    x = x.reshape((nt,) + (2,) * len(names) + rest)
    for bit in bits:
        axis = 1 + names.index(bit)
        names.remove(bit)
        mine = (d // bit) % 2
        got = send(pick(x, 1 - mine, axis), by_bit(bit))
        x = pick(x, mine, axis).astype(F32) + got.astype(F32)
        if names or nt > 1:
            x = x.astype(BF16)
    total = pick(x, t, 0).astype(F32)
    for shift in range(1, nt):
        total = total + send(pick(x, lax.rem(t + shift, nt), 0), by_shift(shift)).astype(F32)
    return total


def arrive(step, sources, scratches, sems, seg_ref, seg_s):
    blocks = sources[0].shape[0]
    copies = []
    for k, (source, scratch) in enumerate(zip(sources, scratches)):
        for part in range(blocks // 2):
            rows = pl.ds(2 * part, 2)
            there = scratch.at[pl.ds(2 * part + 1, 2)]
            copies.append((part, pltpu.make_async_copy(source.at[rows], there, sems.at[k, part])))

    @pl.when(step == 0)
    def _():
        for _, copy in copies:
            copy.start()
        seg_s[0] = jnp.full((1, BLOCK), -1, jnp.int32)
        seg_s[1:] = seg_ref[...]
        for scratch in scratches:
            scratch[0] = jnp.zeros(scratch.shape[1:], BF16)

    for part, copy in copies:
        pl.when(step == part)(copy.wait)


def reach(block, seg_low):
    first = seg_low[block, 0]
    before = 0
    for k in range(seg_low.shape[0]):
        before += (seg_low[k, BLOCK - 1] < first).astype(jnp.int32)
    return (block + 2 - before) // 2


def rows_of(block, seg_s):
    return jnp.broadcast_to(seg_s[block + 1], (BLOCK, BLOCK)).T


def row_mask(row_seg, first, block, seg_s):
    row = lax.broadcasted_iota(jnp.int32, (BLOCK, BLOCK), 0)
    col = lax.broadcasted_iota(jnp.int32, (BLOCK, BLOCK), 1)
    masks = []
    for k in range(2):
        ahead = (first + k - 1 - block) * BLOCK
        allowed = (row_seg == seg_s[first + k]) & (col + ahead <= row)
        masks.append(jnp.where(allowed, 0.0, -1e30).astype(F32))
    return jnp.concatenate(masks, axis=1)


def forward_kernel(
    heads, groups, most, q_ref, k_all, v_all, seg_low, seg_ref, pre_ref, post_ref,
    att_ref, u_ref, lse_ref, k_s, v_s, seg_s, qp_s, m_s, s_s, sems,
):
    step = pl.program_id(0)
    core = lax.axis_index("core")
    block = 2 * step + core
    width = q_ref.shape[1]
    arrive(step, [k_all, v_all], [k_s, v_s], sems, seg_ref, seg_s)
    tiles = reach(block, seg_low)
    row_seg = rows_of(block, seg_s)

    def scores(left, first, mask):
        keys = k_s[pl.ds(first, 2)].reshape(TILE, -1)
        s = right_t(left, keys).reshape(left.shape[0] // BLOCK, BLOCK, TILE)
        return (s + mask[None]).reshape(left.shape[0], TILE)

    def close(g, per, top, total, u, att):
        size = per * BLOCK
        lse_ref[0, g * size : (g + 1) * size, :] = jnp.broadcast_to(top + jnp.log(total), (size, BLOCK))
        for k in range(per):
            h = g * per + k
            part = u[k * BLOCK : (k + 1) * BLOCK]
            u_ref[0, h] = part.astype(BF16)
            att = att + part * post_ref[h : h + 1, :]
        return att

    @pl.when(tiles == 1)
    def _():
        per = heads // groups
        query = q_ref[...]
        mask = row_mask(row_seg, block, block, seg_s)
        att = jnp.zeros((BLOCK, width), F32)
        values = v_s[pl.ds(block, 2)].reshape(TILE, -1)
        for g in range(groups):
            left = jnp.concatenate([query * pre_ref[h : h + 1, :] for h in range(g * per, (g + 1) * per)])
            s = scores(left, block, mask)
            top = jnp.max(s, axis=-1, keepdims=True)
            p = jnp.exp(s - top)
            total = jnp.sum(p, axis=-1, keepdims=True)
            u = matmul((p * (1.0 / total)).astype(BF16), values)
            att = close(g, per, top, total, u, att)
        att_ref[...] = att.astype(BF16)

    @pl.when(tiles > 1)
    def _():
        query = q_ref[...]
        for h in range(heads):
            qp_s[h * BLOCK : (h + 1) * BLOCK, :] = query * pre_ref[h : h + 1, :]
        m_s[...] = jnp.full(m_s.shape, -3e38, F32)
        split = 2
        size = heads // split * BLOCK

        def meet(tile, carry):
            first = block - 2 * tile
            mask = row_mask(row_seg, first, block, seg_s)
            for g in range(split):
                rows = slice(g * size, (g + 1) * size)
                s = scores(qp_s[rows, :], first, mask)
                s_s[tile, rows, :] = s
                m_s[rows, :] = jnp.maximum(m_s[rows, :], jnp.maximum(s[:, :BLOCK], s[:, BLOCK:]))
            return carry

        lax.fori_loop(0, tiles, meet, 0)

    for n in range(2, most + 1):

        @pl.when(tiles == n)
        def _(n=n):
            per = heads // groups
            size = per * BLOCK
            values = v_s[pl.ds(block - 2 * n + 2, 2 * n)].reshape(n * TILE, -1)
            att = jnp.zeros((BLOCK, width), F32)
            for g in range(groups):
                rows = slice(g * size, (g + 1) * size)
                top = jnp.max(m_s[rows, :], axis=-1, keepdims=True)
                parts = [jnp.exp(s_s[tile, rows, :] - top) for tile in range(n)]
                total = jnp.sum(sum(p[:, :BLOCK] + p[:, BLOCK:] for p in parts), axis=-1, keepdims=True)
                p = jnp.concatenate([part.astype(BF16) for part in parts[::-1]], axis=1)
                u = matmul(p, values) * (1.0 / total)
                att = close(g, per, top, total, u, att)
            att_ref[...] = att.astype(BF16)


def whole(shape):
    return pl.BlockSpec(shape, lambda i: (0,) * len(shape), pipeline_mode=pl.Buffered(1))


def cost(flops, moved):
    return pl.CostEstimate(flops=int(flops), bytes_accessed=int(moved), transcendentals=0)


ANY = pl.BlockSpec(memory_space=pl.ANY)
SCALARS = pl.BlockSpec(memory_space=pltpu.SMEM)


def attend(query, k_all, v_all, segs, pre, post):
    heads, width = pre.shape
    rows, stack = query.shape[0], heads * BLOCK
    blocks = rows // BLOCK
    groups = FORWARD_GROUPS
    most = (1024 // BLOCK + 2) // 2
    by_block = pl.BlockSpec((BLOCK, width), lambda i: (i, 0))
    return pl.pallas_call(
        functools.partial(forward_kernel, heads, groups, most),
        grid=(blocks,),
        in_specs=[
            by_block, ANY, ANY, SCALARS, whole((2 * blocks, 1, BLOCK)), whole(pre.shape), whole(post.shape),
        ],
        out_specs=[
            by_block,
            pl.BlockSpec((1, heads, BLOCK, width), lambda i: (i, 0, 0, 0)),
            pl.BlockSpec((1, stack, BLOCK), lambda i: (i, 0, 0)),
        ],
        scratch_shapes=[
            pltpu.VMEM((2 * blocks + 1, BLOCK, width), BF16),
            pltpu.VMEM((2 * blocks + 1, BLOCK, width), BF16),
            pltpu.VMEM((2 * blocks + 1, 1, BLOCK), jnp.int32),
            pltpu.VMEM((stack, width), BF16),
            pltpu.VMEM((stack, BLOCK), F32),
            pltpu.VMEM((most, stack, TILE), F32),
            pltpu.SemaphoreType.DMA((2, blocks)),
        ],
        out_shape=[
            jax.ShapeDtypeStruct((rows, width), BF16),
            jax.ShapeDtypeStruct((blocks, heads, BLOCK, width), BF16),
            jax.ShapeDtypeStruct((blocks, stack, BLOCK), F32),
        ],
        compiler_params=pltpu.CompilerParams(vmem_limit_bytes=62 << 20),
        cost_estimate=cost(4 * rows * 1024 * stack // BLOCK * width, 4 * rows * stack // BLOCK * width),
        name="attend",
    )(query, k_all, v_all, segs, segs[:, None, :], pre, post)


def backward_kernel(
    heads, groups, q_ref, g_ref, u_ref, lse_ref, k_all, v_all, seg_low, seg_ref, pre_ref, post_ref,
    dq_ref, dk_ref, dv_ref, small_ref,
    dpre_ref, dpost_ref, k_s, v_s, seg_s, dk_s, dv_s, qp_s, gp_s, d_s, t_s, sems,
):
    step = pl.program_id(0)
    core = lax.axis_index("core")
    block = 2 * step + core
    width = q_ref.shape[1]
    arrive(step, [k_all, v_all], [k_s, v_s], sems, seg_ref, seg_s)

    @pl.when(step == 0)
    def _():
        dk_s[...] = jnp.zeros(dk_s.shape, F32)
        dv_s[...] = jnp.zeros(dv_s.shape, F32)
        dpre_ref[...] = jnp.zeros(dpre_ref.shape, F32)
        dpost_ref[...] = jnp.zeros(dpost_ref.shape, F32)

    tiles = reach(block, seg_low)
    row_seg = rows_of(block, seg_s)

    def opening(g, per):
        query, grad_low = q_ref[...], g_ref[...]
        grad = grad_low.astype(F32)
        left, right, terms = [], [], []
        for h in range(g * per, (g + 1) * per):
            gain = post_ref[h : h + 1, :]
            left.append(query * pre_ref[h : h + 1, :])
            right.append(grad_low * gain.astype(BF16))
            both = grad * u_ref[0, h].astype(F32)
            terms.append(jnp.sum(both * gain, axis=-1, keepdims=True))
            dpost_ref[h] += jnp.sum(both.reshape(BLOCK // 8, 8, -1), axis=0)
        return jnp.concatenate(left), jnp.concatenate(right), jnp.concatenate(terms)

    def closing(h, part, dq):
        dpre_ref[h] += jnp.sum((q_ref[...].astype(F32) * part).reshape(BLOCK // 8, 8, -1), axis=0)
        return dq + part * pre_ref[h : h + 1, :].astype(F32)

    def tile_part(first, mask, g, left, right, term):
        size = left.shape[0]
        per = size // BLOCK
        keys = k_s[pl.ds(first, 2)].reshape(TILE, -1)
        values = v_s[pl.ds(first, 2)].reshape(TILE, -1)
        s = (right_t(left, keys).reshape(per, BLOCK, TILE) + mask[None]).reshape(size, TILE)
        top = lse_ref[0, g * size : (g + 1) * size, :]
        p = jnp.exp(s - jnp.concatenate([top, top], axis=1))
        dw = right_t(right, values)
        ds = (p * (dw - term)).astype(BF16)
        return matmul(ds, keys), left_t(ds, left), left_t(p.astype(BF16), right)

    def add_up(first, dk, dv):
        dk_s[pl.ds(first, 2)] += dk.reshape(2, BLOCK, -1)
        dv_s[pl.ds(first, 2)] += dv.reshape(2, BLOCK, -1)

    @pl.when(tiles == 1)
    def _():
        mask = row_mask(row_seg, block, block, seg_s)
        dk = dv = jnp.zeros((TILE, width), F32)
        dq = jnp.zeros((BLOCK, width), F32)
        per = heads // groups[0]
        for g in range(groups[0]):
            part, a, b = tile_part(block, mask, g, *opening(g, per))
            dk, dv = dk + a, dv + b
            for k in range(per):
                dq = closing(g * per + k, part[k * BLOCK : (k + 1) * BLOCK], dq)
        add_up(block, dk, dv)
        dq_ref[...] = dq.astype(BF16)

    @pl.when(tiles > 1)
    def _():
        mask = row_mask(row_seg, block, block, seg_s)
        dk = dv = jnp.zeros((TILE, width), F32)
        per = heads // groups[1]
        size = per * BLOCK
        for g in range(groups[1]):
            rows = slice(g * size, (g + 1) * size)
            left, right, term = opening(g, per)
            qp_s[rows, :], gp_s[rows, :] = left, right
            d_s[rows, :] = jnp.broadcast_to(term, (size, BLOCK))
            t_s[rows, :], a, b = tile_part(block, mask, g, left, right, term)
            dk, dv = dk + a, dv + b
        add_up(block, dk, dv)

        def more(tile, carry):
            first = block - 2 * tile
            mask = row_mask(row_seg, first, block, seg_s)
            dk = dv = jnp.zeros((TILE, width), F32)
            size = heads // groups[2] * BLOCK
            for g in range(groups[2]):
                rows = slice(g * size, (g + 1) * size)
                term = jnp.concatenate([d_s[rows, :]] * 2, axis=1)
                part, a, b = tile_part(first, mask, g, qp_s[rows, :], gp_s[rows, :], term)
                t_s[rows, :] += part
                dk, dv = dk + a, dv + b
            add_up(first, dk, dv)
            return carry

        lax.fori_loop(1, tiles, more, 0)
        dq = jnp.zeros((BLOCK, width), F32)
        for h in range(heads):
            dq = closing(h, t_s[h * BLOCK : (h + 1) * BLOCK, :], dq)
        dq_ref[...] = dq.astype(BF16)

    @pl.when(step == pl.num_programs(0) - 1)
    def _():
        for k in range(dk_ref.shape[0]):
            dk_ref[k] = dk_s[k + 1].astype(BF16)
            dv_ref[k] = dv_s[k + 1].astype(BF16)
        sums = [jnp.sum(ref[h], axis=0, keepdims=True) for ref in (dpre_ref, dpost_ref) for h in range(heads)]
        row = lax.broadcasted_iota(jnp.int32, (width, BLOCK), 0)
        col = lax.broadcasted_iota(jnp.int32, (width, BLOCK), 1)
        member = (row // (width // heads) == col).astype(F32)
        mixes = jnp.dot(
            jnp.concatenate(sums), member, preferred_element_type=F32, precision=lax.Precision.HIGHEST
        )
        lines = 2 * heads * BLOCK // width
        small_ref[...] = jnp.zeros(small_ref.shape, F32)
        small_ref[:lines, :] = jnp.concatenate(
            [mixes[k * lines : (k + 1) * lines] for k in range(width // BLOCK)], axis=1
        )


def attend_back(query, grad, u, lse, k_all, v_all, segs, pre, post):
    heads, width = pre.shape
    rows, stack = query.shape[0], heads * BLOCK
    blocks = rows // BLOCK
    groups = BACKWARD_GROUPS
    lines = 2 * heads * BLOCK // width + 2
    lines += -lines % 8
    by_block = pl.BlockSpec((BLOCK, width), lambda i: (i, 0))
    return pl.pallas_call(
        functools.partial(backward_kernel, heads, groups),
        grid=(blocks,),
        in_specs=[
            by_block,
            by_block,
            pl.BlockSpec((1, heads, BLOCK, width), lambda i: (i, 0, 0, 0)),
            pl.BlockSpec((1, stack, BLOCK), lambda i: (i, 0, 0)),
            ANY, ANY, SCALARS, whole((2 * blocks, 1, BLOCK)), whole(pre.shape), whole(post.shape),
        ],
        out_specs=[
            by_block,
            whole((2 * blocks, BLOCK, width)),
            whole((2 * blocks, BLOCK, width)),
            whole((lines, width)),
        ],
        scratch_shapes=[
            pltpu.VMEM((heads, 8, width), F32),
            pltpu.VMEM((heads, 8, width), F32),
            pltpu.VMEM((2 * blocks + 1, BLOCK, width), BF16),
            pltpu.VMEM((2 * blocks + 1, BLOCK, width), BF16),
            pltpu.VMEM((2 * blocks + 1, 1, BLOCK), jnp.int32),
            pltpu.VMEM((2 * blocks + 1, BLOCK, width), F32),
            pltpu.VMEM((2 * blocks + 1, BLOCK, width), F32),
            pltpu.VMEM((stack, width), BF16),
            pltpu.VMEM((stack, width), BF16),
            pltpu.VMEM((stack, BLOCK), F32),
            pltpu.VMEM((stack, width), F32),
            pltpu.SemaphoreType.DMA((2, blocks)),
        ],
        out_shape=[
            jax.ShapeDtypeStruct((rows, width), BF16),
            jax.ShapeDtypeStruct((2 * blocks, BLOCK, width), BF16),
            jax.ShapeDtypeStruct((2 * blocks, BLOCK, width), BF16),
            jax.ShapeDtypeStruct((lines, width), F32),
        ],
        compiler_params=pltpu.CompilerParams(vmem_limit_bytes=62 << 20),
        cost_estimate=cost(10 * rows * 1024 * stack // BLOCK * width, 4 * rows * stack // BLOCK * width),
        name="attend_back",
    )(query, grad, u, lse, k_all, v_all, segs, segs[:, None, :], pre, post)


MESH = pl.DeviceIdType.MESH


def device(place):
    d, t = place
    return d // 2, d % 2, t


def flip(index, bit):
    return index + bit - 2 * bit * ((index // bit) % 2)


def greet(nd, nt, d, t):
    barrier = pltpu.get_barrier_semaphore()
    core = d % 2
    partners = [(d, lax.rem(t + s, nt)) for s in range(1, nt)]
    partners += [(flip(d, 1), lax.rem(t + s, nt)) for s in range(nt)]
    partners += [(flips(d, mask), t) for mask in range(2, nd, 2)]
    for partner in partners:
        pl.semaphore_signal(barrier, inc=1, device_id=device(partner), device_id_type=MESH)
    pl.semaphore_wait(barrier, len(partners))


def remote(src, dst, send_sem, recv_sem, to):
    return pltpu.make_async_remote_copy(
        src_ref=src, dst_ref=dst, send_sem=send_sem, recv_sem=recv_sem, device_id=device(to), device_id_type=MESH
    )


def start_kernel(
    nd, nt, share, halves, *refs,
):
    tokens, grads, segments, pre_mix, post_mix = refs[:5]
    later = refs[5:7] if halves else refs[5:6]
    refs = refs[5 + len(later) - 4 :]
    if halves:
        weights, norms = refs[4:8], refs[8]
        x_out, q_out, k_out, v_out, seg_out, pre_out, post_out, mail_out, later_out, w_out, o_out, gain_out, near_out = refs[9:22]
        wg_s, w_send, w_recv, n_send, n_recv, n_self = refs[22:28]
    else:
        w_out, gain_out = refs[4:6]
        x_out, q_out, k_out, v_out, seg_out, pre_out, post_out, mail_out, later_out = refs[6:15]
    (g_send, g_recv, g_self, l_send, l_recv, x_s, kv_s, x_send, x_recv, x_self, kv_send, kv_recv, kv_self, seg_send, seg_recv, seg_self) = refs[-16:]
    d, t = 2 * lax.axis_index("plane") + lax.axis_index("core"), lax.axis_index("tensor")
    core = d % 2
    width = x_out.shape[1]
    micro = tokens.shape[0]
    per = tokens.shape[1]
    greet(nd, nt, d, t)

    n_copies = []
    if halves:
        for k, weight in enumerate(later):
            there = near_out.at[d // 2, pl.ds(k * weight.shape[0], weight.shape[0])]
            n_copies.append(pltpu.make_async_copy(weight, there, n_self.at[k]))
            for mask in range(2, nd, 2):
                sems = n_send.at[k, mask // 2], n_recv.at[k, mask // 2]
                n_copies.append(remote(weight, there, *sems, (flips(d, mask), t)))
        for copy in n_copies:
            copy.start()

    if halves:
        line = lax.broadcasted_iota(jnp.int32, (8, width), 0)
        lane = lax.broadcasted_iota(jnp.int32, (8, width), 1)
        gains = jnp.zeros((8, width), F32)
        for n in range(2):
            for k in range(share):
                here = (line == n) & (lane == (d * nt + t) * share + k)
                gains = jnp.where(here, norms[n, k], gains)
        own = [weight[...].astype(F32) for weight in weights] + [gains]
        rest = wg_s.shape[2] - 4 * share - 8
        own = own + ([jnp.zeros((rest, width), F32)] if rest else [])
        wg_s[d, t] = jnp.concatenate(own).astype(BF16)
        z_copies = []
        for s in range(1, nt):
            slab = wg_s.at[d, t]
            copy = remote(slab, slab, w_send.at[0, 0, s], w_recv.at[0, 0, s], (d, lax.rem(t + s, nt)))
            copy.start()
            z_copies.append(copy)

    heads = pre_mix.shape[0]
    lane = lax.broadcasted_iota(jnp.int32, (heads, width), 1) // (width // heads)
    member = (lane == lax.broadcasted_iota(jnp.int32, (heads, width), 0)).astype(BF16)
    pre_out[...] = (left_t(pre_mix[...], member) * (width // heads) ** (-0.5)).astype(BF16)
    post_out[...] = matmul(post_mix[...], member)

    g_copies = []
    for m in range(micro):
        there = mail_out.at[2 * m + core]
        g_copies.append(pltpu.make_async_copy(grads.at[m, :, core], there, g_self.at[m]))
        g_copies.append(remote(grads.at[m, :, 1 - core], there, g_send.at[m], g_recv.at[m], (flip(d, 1), t)))
    for copy in g_copies:
        copy.start()

    sends = []
    for m in range(micro):
        for c in range(2):
            to = (d - core + c, 2 * m + core)
            here = (to[0] == d) & (to[1] == t)
            src, dst = tokens.at[m, :, c], x_s.at[pl.ds(per * t, per)]
            far = remote(src, dst, x_send.at[2 * m + c], x_recv.at[t], to)
            near = pltpu.make_async_copy(src, dst, x_self)
            pl.when(jnp.logical_not(here))(far.start)
            pl.when(here)(near.start)
            sends.append((here, far, near))

    holder = t % 2 == core
    seg_here = pltpu.make_async_copy(segments.at[t // 2], seg_out, seg_self)
    seg_there = remote(segments.at[t // 2], seg_out, seg_send, seg_recv, (flip(d, 1), t))

    @pl.when(holder)
    def _():
        seg_here.start()
        seg_there.start()

    l_copies = []
    for s in range(1, nt):
        for k, weight in enumerate(later):
            there = later_out.at[s - 1]
            if len(later) > 1:
                there = later_out.at[s - 1, pl.ds(k * weight.shape[0], weight.shape[0])]
            l_copies.append(remote(weight, there, l_send.at[s, k], l_recv.at[s, k], (d, lax.rem(t + s, nt))))
    for copy in l_copies:
        copy.start()

    if halves:
        bits = [1 << k for k in range(1, nd.bit_length() - 1)]
        routes = [bits + [1], bits[::-1] + [1]]
        have = [[0] for _ in halves]
        for copy in z_copies:
            copy.wait()
        for stage in range(len(bits) + 1):
            copies = []
            for h, (lo, hi) in enumerate(halves):
                bit = routes[h][stage]
                for k, mask in enumerate(have[h]):
                    slab = d
                    for b in [1 << j for j in range(nd.bit_length() - 1)]:
                        if mask & b:
                            slab = flip(slab, b)
                    ref = wg_s.at[slab, :, pl.ds(lo, hi - lo)]
                    copies.append(
                        remote(ref, ref, w_send.at[1 + h, stage, k], w_recv.at[1 + h, stage, k], (flip(d, bit), t))
                    )
                have[h] = have[h] + [mask | bit for mask in have[h]]
            for copy in copies:
                copy.start()
            for copy in copies:
                copy.wait()

        gains = jnp.zeros((8, width), F32)
        for pair in range(nd * nt // 2):
            slabs = [wg_s[(2 * pair + e) // nt, (2 * pair + e) % nt].astype(F32) for e in range(2)]
            for k in range(3):
                both = jnp.concatenate([slab[k * share : (k + 1) * share] for slab in slabs])
                w_out[2 * pair * share : 2 * (pair + 1) * share, k * width : (k + 1) * width] = both.astype(BF16)
            both = jnp.concatenate([slab[3 * share : 4 * share] for slab in slabs])
            o_out[2 * pair * share : 2 * (pair + 1) * share, :] = both.astype(BF16)
            gains = gains + (slabs[0] + slabs[1])[4 * share : 4 * share + 8]
        gain_out[...] = gains

    kv_copies = []
    gain = gain_out[:1]
    for s in range(nt):
        source = lax.rem(t + s, nt)
        here = (source == t) & holder
        arrival = remote(
            x_s.at[pl.ds(per * source, per)], x_s.at[pl.ds(per * source, per)], x_send.at[0], x_recv.at[source], (flip(d, 1), t)
        )
        local = pltpu.make_async_copy(tokens.at[0, :, 0], x_s.at[pl.ds(per * source, per)], x_self)
        pl.when(jnp.logical_not(here))(arrival.wait_recv)
        pl.when(here)(local.wait)
        x = x_s[pl.ds(per * source, per)].reshape(per * BLOCK, width)
        rows = pl.ds(pl.multiple_of(source * per * BLOCK, per * BLOCK), per * BLOCK)
        x_out[rows, :] = x
        x = x.astype(F32)
        h = (x * rms_scale(x) * gain).astype(BF16)
        q_out[rows, :] = matmul(h, w_out[:, :width]).astype(BF16)
        for k, out in enumerate((k_out, v_out)):
            value = matmul(h, w_out[:, (k + 1) * width : (k + 2) * width]).astype(BF16)
            kv_s[k, s] = value.reshape(per, BLOCK, width)
            dst = out.at[pl.ds(per * source, per), core]
            near = pltpu.make_async_copy(kv_s.at[k, s], dst, kv_self.at[k, s])
            far = remote(kv_s.at[k, s], dst, kv_send.at[k, s], kv_recv.at[k, s], (flip(d, 1), t))
            near.start()
            far.start()
            kv_copies += [near, far]
    for copy in kv_copies + l_copies + n_copies + g_copies:
        copy.wait()
    for here, far, near in sends:
        pl.when(jnp.logical_not(here))(far.wait_send)

    @pl.when(holder)
    def _():
        seg_here.wait()
        seg_there.wait_send()

    @pl.when(jnp.logical_not(holder))
    def _():
        seg_there.wait_recv()


def start(tokens, grads, segments, pre_mix, post_mix, weights, norms, up, down):
    micro, _, rows, width = tokens.shape
    nd, nt = 2 * lax.axis_size("plane"), lax.axis_size("tensor")
    count = rows * nt // 2
    blocks = count // BLOCK
    per = blocks // nt
    share = weights[0].shape[0]
    length = 4 * share + 8 + -(4 * share + 8) % 16
    dma = pltpu.SemaphoreType.DMA
    vmem = pl.BlockSpec(memory_space=pltpu.VMEM)
    shaped = jax.ShapeDtypeStruct
    most = max(nd // 2, nt)
    inside = 2 * share % 16 == 0 and length >= 32
    middle = length // 32 * 16
    if inside:
        halves, given = [(0, middle), (middle, length)], [*weights, jnp.stack(norms).astype(F32)]
        given_specs = [vmem] * 4 + [SCALARS]
        gathered_specs = [vmem, vmem, vmem, vmem]
        gathered = [shaped((width, 3 * width), BF16), shaped((width, width), BF16), shaped((8, width), F32)]
        gathered.append(shaped((nd // 2, 2 * up.shape[0], up.shape[1]), BF16))
        later = [up, down]
        scratch = [
            pltpu.VMEM((nd, nt, length, width), BF16),
            dma((3, nd.bit_length(), most)), dma((3, nd.bit_length(), most)),
            dma((2, nd // 2)), dma((2, nd // 2)), dma((2,)),
        ]
    else:
        place = (lax.axis_index("plane") * 2 * nt + lax.axis_index("core") * nt + lax.axis_index("tensor")) * share
        gains = lax.dynamic_update_slice(jnp.zeros((8, width), BF16), jnp.stack(norms), (0, place))
        slabs = lax.all_gather(jnp.concatenate([*weights, gains]), AXES, axis=0, tiled=False)
        w_qkv = slabs[:, : 3 * share].reshape(nd * nt, 3, share, width).transpose(0, 2, 1, 3)
        w_qkv = w_qkv.reshape(width, 3 * width)
        w_out = slabs[:, 3 * share : 4 * share].reshape(width, width)
        gains = jnp.sum(slabs[:, 4 * share : 4 * share + 8].astype(F32), axis=0)
        halves, given, given_specs, gathered_specs, gathered, scratch = [], [w_qkv, gains], [vmem, vmem], [], [], []
        later = [jnp.concatenate([up, down])]
    results = pl.pallas_call(
        functools.partial(start_kernel, nd, nt, share, halves),
        in_specs=[ANY, ANY, ANY, vmem, vmem] + [ANY] * len(later) + given_specs,
        out_specs=[vmem, vmem, ANY, ANY, ANY, vmem, vmem, vmem, ANY] + gathered_specs,
        out_shape=[
            shaped((count, width), BF16),
            shaped((count, width), BF16),
            shaped((blocks, 2, BLOCK, width), BF16),
            shaped((blocks, 2, BLOCK, width), BF16),
            shaped((2 * blocks, BLOCK), jnp.int32),
            shaped((pre_mix.shape[0], width), BF16),
            shaped((pre_mix.shape[0], width), F32),
            shaped((nt, per, BLOCK, width), BF16),
            shaped((nt - 1, 2 * up.shape[0], up.shape[1]), BF16),
            *gathered,
        ],
        scratch_shapes=scratch + [
            dma((micro,)), dma((micro,)), dma((micro,)),
            dma((nt, 2)), dma((nt, 2)),
            pltpu.VMEM((blocks, BLOCK, width), BF16),
            pltpu.VMEM((2, nt, per, BLOCK, width), BF16),
            dma((nt,)), dma((nt,)), dma,
            dma((2, nt)), dma((2, nt)), dma((2, nt)),
            dma, dma, dma,
        ],
        compiler_params=pltpu.CompilerParams(
            collective_id=0, has_side_effects=True, vmem_limit_bytes=62 << 20
        ),
        name="start",
    )(
        tokens.reshape(micro, rows // TILE, 2, BLOCK, width),
        grads.reshape(micro, rows // TILE, 2, BLOCK, width),
        segments.reshape(micro, 2 * blocks, BLOCK),
        pre_mix,
        post_mix,
        *later,
        *given,
    )
    if inside:
        rest = [results[8]] + [send(results[8], by_bit(mask)) for mask in range(2, nd, 2)]
        return (*results[:8], results[12], rest, *results[9:12])
    near = lax.all_gather(later[0], ("plane", "core"), axis=0, tiled=False).reshape(nd // 2, 2, *later[0].shape)
    rest = lax.all_gather(results[8], ("plane", "core"), axis=0, tiled=False).reshape(nd // 2, 2, *results[8].shape)
    return (*results[:8], near, [rest], w_qkv, w_out, gains)


def gelu_parts(v):
    t = 1.0 / (1.0 + 0.23164189 * jnp.abs(v))
    bell = jnp.exp(-0.5 * v * v)
    series = t * (0.127414796 + t * (-0.142248368 + t * (0.7107068705 + t * (-0.7265760135 + t * 0.5307027145))))
    tail = series * bell
    return jnp.where(v < 0.0, tail, 1.0 - tail), 0.3989422804 * bell


def middle_kernel(rb, nd, nt, share, inside, *refs):
    x_ref, att_ref, w_out, gain_ref, near_all, dy_all = refs[:6]
    pieces = nd // 2 if inside else 1
    rest_all, refs = refs[6 : 6 + pieces], refs[pieces - 1 :]
    mail_ref, after_ref, datt_ref, dwo_ref, dgain_ref, part_ref, last_ref = refs[7:14]
    dy_ref, h_s, ht_s, dyt_s, o_s, dh_s, hid_s, dhid_s, w_s, dy_sem, w_self = refs[14:25]
    if inside:
        g_s, core_s, plane_s, c_send, c_recv, p_send, p_recv, w_send, w_recv = refs[25:]
    step = pl.program_id(0)
    d, t = 2 * lax.axis_index("plane") + lax.axis_index("core"), lax.axis_index("tensor")
    count, width = x_ref.shape
    parts = range(0, count, rb)
    bits = [1 << k for k in range(1, nd.bit_length() - 1)]
    routes = [bits, bits[::-1]]

    def weight_copies(k):
        if not inside:
            return [pltpu.make_async_copy(rest_all[0].at[:, :, k - 1] if k else near_all, w_s.at[k], w_self.at[k, 0])]
        pairs = [(near_all, w_s.at[k, :, d % 2])]
        if k:
            pairs = [(rest_all[j].at[k - 1], w_s.at[k, flips(d, 2 * j) // 2, d % 2]) for j in range(pieces)]
        copies = []
        for j, (rows, there) in enumerate(pairs):
            copies.append(pltpu.make_async_copy(rows, there, w_self.at[k, j]))
            copies.append(remote(rows, there, w_send.at[k, j], w_recv.at[k, j], (flip(d, 1), t)))
        return copies

    @pl.when(step == 0)
    def _():
        if inside:
            greet(nd, nt, d, t)
        for k in range(nt):
            for copy in weight_copies(k):
                copy.start()
        dy_copy = pltpu.make_async_copy(dy_all, dy_ref, dy_sem)
        dy_copy.start()
        for r in parts:
            rows = slice(r, r + rb)
            after = x_ref[rows, :].astype(F32) + matmul(att_ref[rows, :], w_out[...])
            after_ref[rows, :] = after
            o_s[rows, :] = after
            h = (after * rms_scale(after) * gain_ref[1:2]).astype(BF16)
            h_s[rows, :] = h
            ht_s[:, rows] = h.T
            dh_s[rows, :] = jnp.zeros((rb, width), F32)
        dy_copy.wait()
        for r in parts:
            rows = slice(r, r + rb)
            dyt_s[:, rows] = dy_ref[rows, :].T

    for k in range(nt):

        @pl.when(step == k)
        def _(k=k):
            for copy in weight_copies(k):
                copy.wait()

    def core_copies(slot):
        return [
            remote(
                g_s.at[slot, flips(flip(d, 1), mask)], core_s.at[slot, j],
                c_send.at[slot, j], c_recv.at[slot, j], (flip(d, 1), t),
            )
            for j, mask in enumerate(masks_of(bits))
        ]

    def plane_copies(slot, stage):
        copies = []
        for h in range(2):
            bit, rows = routes[h][stage], pl.ds(h * share, share)
            for j, mask in enumerate(masks_of(routes[h][stage + 1 :])):
                copies.append(
                    remote(
                        g_s.at[slot, flips(flip(d, bit), mask), rows], plane_s.at[slot, stage, j, rows],
                        p_send.at[slot, stage, h, j], p_recv.at[slot, stage, h, j], (flip(d, bit), t),
                    )
                )
        return copies

    def core_done(k):
        slot = lax.rem(k, 2)
        for copy in core_copies(slot):
            copy.wait()
        for j, mask in enumerate(masks_of(bits)):
            mine = flips(d, mask)
            total = (g_s[slot, mine].astype(F32) + core_s[slot, j].astype(F32)).astype(BF16)
            if isinstance(k, int):
                last_ref[j] = total
            else:
                g_s[slot, mine] = total
        for copy in [] if isinstance(k, int) else plane_copies(slot, 0):
            copy.start()

    def plane_done(k, stage):
        slot = lax.rem(k, 2)
        for copy in plane_copies(slot, stage):
            copy.wait()
        for h in range(2):
            rows = slice(h * share, (h + 1) * share)
            for j, mask in enumerate(masks_of(routes[h][stage + 1 :])):
                mine = flips(d, mask)
                total = g_s[slot, mine, rows].astype(F32) + plane_s[slot, stage, j, rows].astype(F32)
                g_s[slot, mine, rows] = total.astype(BF16)
        if stage + 1 < len(bits):
            for copy in plane_copies(slot, stage + 1):
                copy.start()
        else:
            mail_ref[lax.rem(t + nt - k, nt), : 2 * share] = g_s[slot, d]

    def when(condition, stage, *args):
        if inside:
            pl.when(condition)(functools.partial(stage, *args))

    @pl.when(step < nt)
    def _():
        up, down = (w_s[step, :, :, k * share : (k + 1) * share].reshape(width, -1) for k in range(2))
        for point, r in enumerate(parts):
            rows = slice(r, r + rb)
            v = matmul(h_s[rows, :], up)
            cumulative, density = gelu_parts(v)
            hid_s[rows, :] = (v * cumulative).astype(BF16)
            d_hidden = matmul(dy_ref[rows, :], down) * (cumulative + v * density)
            dhid_s[rows, :] = d_hidden.astype(BF16)
            if point == 1:
                when(step >= 1, core_done, step - 1)
        when(step >= 2, plane_done, step - 2, len(bits) - 1)
        slot = lax.rem(step, 2)
        for r in range(0, width, 2 * share):
            rows = slice(r, r + 2 * share)
            for k, (left, right) in enumerate(((ht_s, dhid_s), (dyt_s, hid_s))):
                both = matmul(left[rows, :], right[...]).astype(BF16)
                for e in range(2):
                    grad = both[e * share : (e + 1) * share]
                    if inside:
                        g_s[slot, r // share + e, k * share : (k + 1) * share] = grad
                    else:
                        part_ref[r // share + e, 0, k] = grad
                        last_ref[...] = jnp.zeros(last_ref.shape, BF16)
        if inside:
            for copy in core_copies(slot):
                copy.start()
        for r in parts:
            rows = slice(r, r + rb)
            o_s[rows, :] += right_t(hid_s[rows, :], down)
            dh_s[rows, :] += right_t(dhid_s[rows, :], up)
        for stage in range(len(bits) - 1):
            when(step >= 1, plane_done, step - 1, stage)

    @pl.when(step == nt)
    def _():
        gain = gain_ref[1:2]
        total = jnp.zeros((8, width), F32)
        mail_ref[:, mail_ref.shape[1] - count // nt :] = o_s[...].astype(BF16).reshape(nt, count // nt, width)
        for point, r in enumerate(parts):
            rows = slice(r, r + rb)
            after = after_ref[rows, :]
            scale = rms_scale(after)
            normed = after * scale
            dh = dh_s[rows, :]
            total = total + jnp.sum((dh * normed).reshape(rb // 8, 8, width), axis=0)
            d_after = dy_ref[rows, :].astype(F32) + rms_back(dh, normed, scale, gain)
            after_ref[rows, :] = d_after
            branch = d_after.astype(BF16)
            hid_s[rows, :] = branch
            datt_ref[rows, :] = right_t(branch, w_out[...]).astype(BF16)
            if inside and point == 0:
                core_done(nt - 1)
        if inside:
            plane_done(step - 2, len(bits) - 1)
        dgain_ref[...] = total
        dwo_ref[...] = left_t(att_ref[...], hid_s[...]).astype(BF16)
        if inside:
            part_ref[...] = jnp.zeros(part_ref.shape, BF16)
            mail_ref[lax.rem(t + 1, nt), : 2 * share] = jnp.zeros((2 * share, width), BF16)


def feed_forward(x, attended, dy, w_out, gain, near, rest, nd):
    count, width = x.shape
    nt, units = rest[0].shape[-3] + 1, rest[0].shape[-1]
    share = rest[0].shape[-2] // 2
    inside = share % 16 == 0 and nd >= 8
    rb = 256
    rows = whole((count, width))
    mail = (nt, count // nt + (2 * share if inside else 0), width)
    dma = pltpu.SemaphoreType.DMA
    scratch = [
        pltpu.VMEM((count, width), BF16),
        pltpu.VMEM((count, width), BF16),
        pltpu.VMEM((width, count), BF16),
        pltpu.VMEM((width, count), BF16),
        pltpu.VMEM((count, width), F32),
        pltpu.VMEM((count, width), F32),
        pltpu.VMEM((count, units), BF16),
        pltpu.VMEM((count, units), BF16),
        pltpu.VMEM((nt, nd // 2, 2, 2 * share, units), BF16),
        dma, dma((nt, nd // 2)),
    ]
    if inside:
        stages = nd.bit_length() - 2
        grads, grads_spec = jax.ShapeDtypeStruct((8, units), BF16), whole((8, units))
        scratch += [
            pltpu.VMEM((2, nd, 2 * share, units), BF16),
            pltpu.VMEM((2, nd // 2, 2 * share, units), BF16),
            pltpu.VMEM((2, stages, nd // 4, 2 * share, units), BF16),
            dma((2, nd // 2)), dma((2, nd // 2)),
            dma((2, stages, 2, nd // 4)), dma((2, stages, 2, nd // 4)),
            dma((nt, nd // 2)), dma((nt, nd // 2)),
        ]
        params = dict(collective_id=2, has_side_effects=True)
    else:
        grads = jax.ShapeDtypeStruct((nd, nt, 2, share, units), BF16)
        grads_spec = pl.BlockSpec((nd, 1, 2, share, units), lambda s: (0, jnp.minimum(s, nt - 1), 0, 0, 0))
        params = {}
    return pl.pallas_call(
        functools.partial(middle_kernel, rb, nd, nt, share, inside),
        grid=(nt + 1,),
        in_specs=[
            rows, rows, whole((width, width)), whole((8, width)), ANY, ANY,
        ] + [ANY] * len(rest),
        out_specs=[whole(mail), rows, rows, whole((width, width)), whole((8, width)), grads_spec, whole((nd // 2, 2 * share, units))],
        out_shape=[
            jax.ShapeDtypeStruct(mail, BF16),
            jax.ShapeDtypeStruct((count, width), F32),
            jax.ShapeDtypeStruct((count, width), BF16),
            jax.ShapeDtypeStruct((width, width), BF16),
            jax.ShapeDtypeStruct((8, width), F32),
            grads,
            jax.ShapeDtypeStruct((nd // 2, 2 * share, units), BF16),
        ],
        scratch_shapes=scratch,
        compiler_params=pltpu.CompilerParams(vmem_limit_bytes=62 << 20, **params),
        cost_estimate=cost(12 * count * width * nt * units, 4 * nd * nt * share * units),
        name="feed_forward",
    )(x, attended, w_out, gain, near, dy, *rest)


def masks_of(bits):
    masks = [0]
    for bit in bits:
        masks = masks + [mask | bit for mask in masks]
    return masks


def flips(index, mask):
    bit = 1
    while bit <= mask:
        if mask & bit:
            index = flip(index, bit)
        bit *= 2
    return index


def finish_kernel(
    nd, nt, share, inside, x_all, dq_all, dk_all, dv_all, after_all, w_all, gain_ref, dwo_all, small_ref,
    ffn_ref, back, *refs,
):
    last_refs, refs = refs[: nd // 2], refs[nd // 2 :]
    tok_out, out_out, dw_out, small_out, last_out = refs[:5]
    own_s, other_s, grads_s, ht_s, tok_s, own_sems, kv_send, kv_recv, tok_send, tok_recv, tok_self = refs[5:16]
    b_send, b_recv, b_self, x_ref, dq_ref, after_ref, w_ref, dwo_ref, in_sems, last4_s, last_sems, last_s, l_send, l_recv = refs[16:30]
    if inside:
        slab_s, core_s, plane_s, mine_s, z_s, sm_s, sm_in, g_send, g_recv, s_send, s_recv = refs[30:]
    d, t = 2 * lax.axis_index("plane") + lax.axis_index("core"), lax.axis_index("tensor")
    core = d % 2
    count, width = x_all.shape
    per = tok_out.shape[1]
    rows_in = per * BLOCK
    holder = t % 2 == core
    bits = [1 << k for k in range(1, nd.bit_length() - 1)]
    loads = [
        pltpu.make_async_copy(far, near, in_sems.at[k])
        for k, (far, near) in enumerate(
            ((dq_all, dq_ref), (w_all, w_ref), (x_all, x_ref), (after_all, after_ref), (dwo_all, dwo_ref))
        )
    ]
    own = [pltpu.make_async_copy(a.at[:, core], own_s.at[k], own_sems.at[k]) for k, a in enumerate((dk_all, dv_all))]
    loads += [pltpu.make_async_copy(far, last4_s.at[k], last_sems.at[k]) for k, far in enumerate(last_refs)]
    for copy in own + loads:
        copy.start()
    greet(nd, nt, d, t)

    order = [flips(t, mask) for mask in (2, 3, 1, 0)] if nt == 4 else [lax.rem(t + s, nt) for s in range(nt)]
    exchanged = []
    for s, source in enumerate(order):
        pair = []
        for k, a in enumerate((dk_all, dv_all)):
            pair.append(
                remote(
                    a.at[pl.ds(per * source, per), 1 - core], other_s.at[k, pl.ds(per * source, per)],
                    kv_send.at[k, s], kv_recv.at[k, s], (flip(d, 1), t),
                )
            )
        exchanged.append(pair)
    for copy in exchanged[0] + exchanged[1]:
        copy.start()
    b_copies = []
    skip = back.shape[1] - rows_in
    for m in range(out_out.shape[0]):
        for k in range(per):
            there, lines = out_out.at[m, k, core], pl.ds(skip + k * BLOCK, BLOCK)
            b_copies.append(pltpu.make_async_copy(back.at[2 * m + core, lines], there, b_self.at[m, k]))
            b_copies.append(
                remote(back.at[2 * m + 1 - core, lines], there, b_send.at[m, k], b_recv.at[m, k], (flip(d, 1), t))
            )
    gain = gain_ref[:1]

    def norms(rows):
        x = x_ref[rows, :].astype(F32)
        scale = rms_scale(x)
        return x * scale, scale

    routes = [[1] + bits, [1] + bits[::-1]]
    rows_of_slab = width // nd

    def fill(bundle, which, left, right):
        for k in range(nd):
            lines = slice(k * rows_of_slab, (k + 1) * rows_of_slab)
            if k % 2 == 0:
                both = matmul(left[lines.start : lines.stop + rows_of_slab, :], right)
                slab_s[bundle, which, k : k + 2] = both.astype(BF16).reshape(2, rows_of_slab, width)

    def stage_copies(bundle, stage):
        copies, adds = [], []
        for h in range(2):
            bit = routes[h][stage]
            for k, mask in enumerate(masks_of(routes[h][stage + 1 :])):
                buffer = core_s.at[bundle] if stage == 0 else plane_s.at[bundle, stage - 1]
                copies.append(
                    remote(
                        slab_s.at[bundle, h, flips(flip(d, bit), mask)], buffer.at[h, k],
                        g_send.at[bundle, h, stage, k], g_recv.at[bundle, h, stage, k], (flip(d, bit), t),
                    )
                )
                adds.append((h, flips(d, mask), buffer, k))
        return copies, adds

    def stage_start(bundle, stage):
        for copy in stage_copies(bundle, stage)[0]:
            copy.start()

    def stage_done(bundle, stage):
        copies, adds = stage_copies(bundle, stage)
        for copy in copies:
            copy.wait()
        last = stage == len(bits)
        totals = []
        for h, mine, buffer, k in adds:
            total = slab_s[bundle, h, mine].astype(F32) + buffer[h, k].astype(F32)
            if last:
                totals.append(total.reshape(nt, share, width))
            else:
                slab_s[bundle, h, mine] = total.astype(BF16)
        if last:
            mine_s[bundle] = jnp.concatenate(totals, axis=1).astype(BF16)

    def z_copies(bundle):
        copies = []
        for s in range(1, nt):
            to = lax.rem(t + s, nt)
            copies.append(
                remote(
                    mine_s.at[bundle, to], z_s.at[bundle, s],
                    g_send.at[bundle, 2, 0, s], g_recv.at[bundle, 2, 0, s], (d, to),
                )
            )
        return copies

    def small_copies(stage):
        if stage <= len(bits):
            return [remote(sm_s, sm_in.at[stage], s_send.at[stage], s_recv.at[stage], (flip(d, routes[0][stage]), t))]
        copies = []
        for s in range(1, nt):
            k = len(bits) + s
            copies.append(remote(sm_s, sm_in.at[k], s_send.at[k], s_recv.at[k], (d, lax.rem(t + s, nt))))
        return copies

    sends, gains = [], []
    to_core = d - core + t % 2

    def sum_group(s):
        source = order[s]
        for copy in exchanged[s]:
            copy.wait()
        for copy in exchanged[s + 2] if s + 2 < nt else []:
            copy.start()
        rows = pl.ds(pl.multiple_of(source * rows_in, rows_in), rows_in)
        grads_s[rows, :width] = dq_ref[rows, :]
        for k in range(2):
            total = own_s[k, pl.ds(per * source, per)].astype(F32) + other_s[k, pl.ds(per * source, per)].astype(F32)
            grads_s[rows, (k + 1) * width : (k + 2) * width] = total.reshape(rows_in, width).astype(BF16)

    def token_group(s):
        source = order[s]
        rows = pl.ds(pl.multiple_of(source * rows_in, rows_in), rows_in)
        dh = right_t(grads_s[rows, :], w_ref[...])
        normed, scale = norms(rows)
        gains.append(jnp.sum((dh * normed).reshape(rows_in // 8, 8, width), axis=0))
        tok = after_ref[rows, :] + rms_back(dh, normed, scale, gain)
        tok_s[s] = tok.astype(BF16).reshape(per, BLOCK, width)
        here = (source == t) & holder
        dst = tok_out.at[t // 2, :, core]
        far = remote(tok_s.at[s], dst, tok_send.at[s], tok_recv.at[2 * (t // 2) + core], (to_core, source))
        near = pltpu.make_async_copy(tok_s.at[s], dst, tok_self)
        pl.when(jnp.logical_not(here))(far.start)
        pl.when(here)(near.start)
        sends.append((here, far, near))

    for copy in own + loads:
        copy.wait()
    last_s[...] = sum(last4_s[k].astype(F32) for k in range(last4_s.shape[0])).astype(BF16)
    last = remote(last_s, last_out, l_send, l_recv, (d, lax.rem(t + 1, nt)))
    last.start()
    for r in range(0, count, rows_in):
        lines = slice(r, r + rows_in)
        normed, scale = norms(lines)
        ht_s[:, lines] = (normed * gain).astype(BF16).T
    if inside:
        slab_s[0, 1] = dwo_ref[...].reshape(nd, rows_of_slab, width)
        fill(0, 0, ht_s, dq_ref[...])
        stage_start(0, 0)
    for s in range(nt // 2):
        sum_group(s)
        token_group(s)
    if inside:
        stage_done(0, 0)
        stage_start(0, 1)
    for s in range(nt // 2, nt):
        sum_group(s)
    if inside:
        for which in range(2):
            fill(1, which, ht_s, grads_s[:, (which + 1) * width : (which + 2) * width])
        stage_start(1, 0)
    for s in range(nt // 2, nt):
        token_group(s)

    for copy in b_copies:
        copy.start()
    small = small_ref[...]
    line = lax.broadcasted_iota(jnp.int32, small.shape, 0)
    small = small + jnp.where(line == small.shape[0] - 2, jnp.sum(sum(gains), axis=0, keepdims=True), 0.0)
    small = small + jnp.where(line == small.shape[0] - 1, jnp.sum(ffn_ref[...], axis=0, keepdims=True), 0.0)
    if inside:
        sm_s[...] = small
        tiny = small_copies(0)
        for copy in tiny:
            copy.start()
        for stage in range(len(bits) + 1):
            for copy in tiny:
                copy.wait()
            sm_s[...] += sm_in[stage]
            tiny = small_copies(stage + 1)
            for copy in tiny:
                copy.start()
            stage_done(1, stage)
            if stage < len(bits):
                stage_start(1, stage + 1)
                stage_done(0, stage + 1)
                if stage + 1 < len(bits):
                    stage_start(0, stage + 2)
                else:
                    first_z = z_copies(0)
                    for copy in first_z:
                        copy.start()
        second_z = z_copies(1)
        for copy in second_z:
            copy.start()
        for copy in first_z + second_z + tiny:
            copy.wait()
        for bundle in range(2):
            total = mine_s[bundle, t].astype(F32)
            for s in range(1, nt):
                total = total + z_s[bundle, s].astype(F32)
            dw_out[bundle * 2 * share : (bundle + 1) * 2 * share] = total
        small_out[...] = sm_s[...] + sum(sm_in[len(bits) + s] for s in range(1, nt))
    else:
        small_out[...] = small
        for r in range(0, width, 256):
            lines = slice(r, r + 256)
            dw_out[lines, : 3 * width] = matmul(ht_s[lines, :], grads_s[...]).astype(BF16)
            dw_out[lines, 3 * width :] = dwo_ref[lines, :]

    for copy in b_copies + [last]:
        copy.wait()
    for here, far, near in sends:
        pl.when(jnp.logical_not(here))(far.wait_send)
        pl.when(here)(near.wait)
    for m in range(tok_out.shape[0]):
        for c in range(2):
            here = (2 * m + core == t) & (c == core)
            dst = tok_out.at[m, :, c]
            back = remote(dst, dst, tok_send.at[0], tok_recv.at[2 * m + c], (flip(d, 1), t))
            pl.when(jnp.logical_not(here))(back.wait_recv)


def finish(x, dq, dk_all, dv_all, after, w_qkv, gains, dwo, small, gain_ffn, back, last, share, micro):
    count, width = x.shape
    nd, nt = 2 * lax.axis_size("plane"), lax.axis_size("tensor")
    inside = 2 * share % 16 == 0 and nd >= 8
    blocks = count // BLOCK
    per = blocks // nt
    dma = pltpu.SemaphoreType.DMA
    vmem = pl.BlockSpec(memory_space=pltpu.VMEM)
    shaped = jax.ShapeDtypeStruct
    scratch = [
        pltpu.VMEM((2, blocks, BLOCK, width), BF16),
        pltpu.VMEM((2, blocks, BLOCK, width), BF16),
        pltpu.VMEM((count, 3 * width), BF16),
        pltpu.VMEM((width, count), BF16),
        pltpu.VMEM((nt, per, BLOCK, width), BF16),
        dma((2,)), dma((2, nt)), dma((2, nt)), dma((nt,)), dma((nt,)), dma,
        dma((micro, per)), dma((micro, per)), dma((micro, per)),
        pltpu.VMEM(x.shape, x.dtype), pltpu.VMEM(dq.shape, dq.dtype), pltpu.VMEM(after.shape, after.dtype),
        pltpu.VMEM(w_qkv.shape, w_qkv.dtype), pltpu.VMEM(dwo.shape, dwo.dtype), dma((5,)),
        pltpu.VMEM((nd // 2,) + last[0].shape, BF16), dma((nd // 2,)), pltpu.VMEM(last[0].shape, BF16), dma, dma,
    ]
    if inside:
        most = max(nd // 2, nt)
        stages = nd.bit_length() - 1
        scratch += [
            pltpu.VMEM((2, 2, nd, nt * share, width), BF16),
            pltpu.VMEM((2, 2, nd // 2, nt * share, width), BF16),
            pltpu.VMEM((2, stages - 1, 2, nd // 4, nt * share, width), BF16),
            pltpu.VMEM((2, nt, 2 * share, width), BF16),
            pltpu.VMEM((2, nt, 2 * share, width), BF16),
            pltpu.VMEM(small.shape, F32),
            pltpu.VMEM((stages + nt,) + small.shape, F32),
            dma((2, 3, stages, most)), dma((2, 3, stages, most)), dma((stages + nt,)), dma((stages + nt,)),
        ]
    return pl.pallas_call(
        functools.partial(finish_kernel, nd, nt, share, inside),
        in_specs=[ANY, ANY, ANY, ANY, ANY, ANY, vmem, ANY, vmem, vmem, ANY] + [ANY] * len(last),
        out_specs=[vmem, vmem, vmem, vmem, vmem],
        out_shape=[
            shaped((micro, per, 2, BLOCK, width), BF16),
            shaped((micro, per, 2, BLOCK, width), BF16),
            shaped((4 * share, width), F32) if inside else shaped((width, 4 * width), BF16),
            shaped(small.shape, F32),
            shaped(last[0].shape, BF16),
        ],
        scratch_shapes=scratch,
        compiler_params=pltpu.CompilerParams(
            collective_id=1, has_side_effects=True, vmem_limit_bytes=62 << 20
        ),
        cost_estimate=cost(24 * count * width * width, 16 * count * width),
        name="finish",
    )(x, dq, dk_all, dv_all, after, w_qkv, gains, dwo, small, gain_ffn, back, *last)


def emit_kernel(heads, share, tok_ref, out_ref, dw_ref, ffn_ref, last_ref, small_ref, tok, out, *rest):
    grads, ups, gains, mixes = rest[:4], rest[4:6], rest[6:8], rest[8:10]
    tok[...] = tok_ref[...].astype(F32)
    out[...] = out_ref[...]

    @pl.when(pl.program_id(0) == 0)
    def _():
        for grad, k in zip(grads, (0, 2, 3, 1)):
            grad[...] = dw_ref[k * share : (k + 1) * share]
        half = last_ref.shape[0] // 2
        for k, up in enumerate(ups):
            lines = slice(k * half, (k + 1) * half)
            total = last_ref[lines].astype(F32)
            for z in range(ffn_ref.shape[0]):
                total = total + ffn_ref[z, lines].astype(F32)
            up[...] = total
        width = small_ref.shape[1]
        place = (
            (lax.axis_index("plane") * 2 + lax.axis_index("core")) * lax.axis_size("tensor") + lax.axis_index("tensor")
        ) * share
        row = lax.broadcasted_iota(jnp.int32, (width, share), 0)
        col = lax.broadcasted_iota(jnp.int32, (width, share), 1)
        exact = dict(preferred_element_type=F32, precision=lax.Precision.HIGHEST)
        own = jnp.dot(small_ref[small_ref.shape[0] - 8 :, :], (row == place + col).astype(F32), **exact)
        for k, gain in enumerate(gains):
            gain[...] = own[6 + k : 7 + k]
        lines = 2 * heads * BLOCK // width
        sums = jnp.concatenate(
            [small_ref[:lines, k * BLOCK : (k + 1) * BLOCK] for k in range(width // BLOCK)]
        )[:, :heads]
        mixes[0][...] = sums[:heads].T * (width // heads) ** (-0.5)
        mixes[1][...] = sums[heads:]


def emit(tok, out, dw, ffn, last, small, heads, share):
    width = small.shape[1]
    micro, per, cores, block, _ = tok.shape
    rows = per * cores * block

    def part(k):
        return pl.BlockSpec((1, rows, width), lambda i: (i, 0, 0))

    shaped = jax.ShapeDtypeStruct
    small_shapes = [(share, width)] * 4 + [(last.shape[0] // 2, width)] * 2 + [(1, share)] * 2 + [(heads, heads)] * 2
    return pl.pallas_call(
        functools.partial(emit_kernel, heads, share),
        grid=(micro,),
        in_specs=[part(0), part(1), whole(dw.shape), whole((ffn.shape[0],) + last.shape), whole(last.shape), whole(small.shape)],
        out_specs=[part(0), part(1)] + [whole(shape) for shape in small_shapes],
        out_shape=[shaped((micro, rows, width), F32), shaped((micro, rows, width), BF16)]
        + [shaped(shape, F32) for shape in small_shapes],
        compiler_params=pltpu.CompilerParams(vmem_limit_bytes=62 << 20),
        name="emit",
    )(tok.reshape(micro, rows, width), out.reshape(micro, rows, width), dw, ffn, last, small)


def per_device(
    tokens, segments, w_query, w_key, w_value, w_out, norm_attn, norm_ffn, pre_mix, post_mix, w_up, w_down, out_grad,
):
    micro, _, rows, width = tokens.shape
    nd, nt = 2 * lax.axis_size("plane"), lax.axis_size("tensor")
    heads = pre_mix.shape[0]
    head_width = width // heads
    length = rows * nt
    count = length // 2
    blocks = count // BLOCK
    share = w_query.shape[0]
    bits = [1 << k for k in range(nd.bit_length() - 1)]
    d, t = 2 * lax.axis_index("plane") + lax.axis_index("core"), lax.axis_index("tensor")
    core = d % 2

    x, query, k_all, v_all, segs, pre, post, mail, near, rest, w_qkv, all_out, gains = start(
        tokens, out_grad, segments, pre_mix, post_mix, [w_query, w_key, w_value, w_out], [norm_attn, norm_ffn], w_up, w_down
    )
    k_all, v_all = (a.reshape(2 * blocks, BLOCK, width) for a in (k_all, v_all))
    dy = lax.all_to_all(mail, "tensor", 0, 0, tiled=True).reshape(count, width)
    attended, u, lse = attend(query, k_all, v_all, segs, pre, post)
    mail, grad_after, grad_attended, grad_w_out, grad_gain_ffn, part_both, last_both = feed_forward(
        x, attended, dy, all_out, gains, near, rest, nd
    )
    back = lax.all_to_all(mail, "tensor", 0, 0, tiled=True)
    last_both = [last_both[0]] + [send(last_both[k], by_bit(2 * k)) for k in range(1, nd // 2)]
    if part_both.ndim > 3:
        part_both = lax.dynamic_slice_in_dim(jnp.concatenate([part_both[:, ::-1]] * 2, axis=1), nt - 1 - t, nt, 1)
        part_both = lax.psum_scatter(part_both, ("plane", "core"), scatter_dimension=0, tiled=False)
        part_both = lax.psum_scatter(part_both, "tensor", scatter_dimension=0, tiled=False)
        part_both = part_both.reshape(1, 2 * w_up.shape[0], w_up.shape[1])
    else:
        part_both = back

    grad_query, grad_key, grad_value, small = attend_back(
        query, grad_attended, u, lse, k_all, v_all, segs, pre, post
    )
    d_tokens, out, owned, small, last_both = finish(
        x, grad_query, grad_key.reshape(blocks, 2, BLOCK, width), grad_value.reshape(blocks, 2, BLOCK, width),
        grad_after, w_qkv, gains, grad_w_out, small, grad_gain_ffn, back, last_both, share, micro,
    )
    if owned.dtype == BF16:
        owned = lax.psum_scatter(owned, AXES, scatter_dimension=0, tiled=True).astype(F32)
        owned = jnp.concatenate([owned[:, k * width : (k + 1) * width] for k in (0, 3, 1, 2)])
        small = lax.psum(small, AXES)
    d_tokens, out, *grads = emit(d_tokens, out, owned, part_both, last_both, small, heads, share)
    d_query, d_key, d_value, d_out, d_up, d_down, d_gain_attn, d_gain_ffn, d_pre, d_post = grads
    return (
        out.reshape(tokens.shape),
        d_tokens.reshape(tokens.shape),
        d_query,
        d_key,
        d_value,
        d_out,
        d_gain_attn.reshape(share),
        d_gain_ffn.reshape(share),
        d_pre,
        d_post,
        d_up,
        d_down,
    )


def solution(mesh):
    devices = mesh.devices
    devices = devices.reshape(devices.shape[0] // 2, 2, devices.shape[1])
    dp = ("plane", "core")
    both = P(AXES, None)
    gain = P(AXES)
    data = P(None, dp, "tensor", None)
    ffn = P(dp, "tensor")
    return jax.shard_map(
        per_device,
        mesh=jax.sharding.Mesh(devices, AXES),
        in_specs=(data, P(None, dp, None), both, both, both, both, gain, gain, P(), P(), ffn, ffn, data),
        out_specs=(data, data, both, both, both, both, gain, gain, P(), P(), ffn, ffn),
        check_vma=False,
    )
```
